32 devices in a mesh: table: 8 (over z, core), row: 4 (over y, x).
Axes of the slice: x: 2, y: 2, z: 4, core: 2. Of those that a mesh axis runs over, the one named last changes fastest.
Arguments:
- dense_feat: bfloat16 [8192, 128], P(('table', 'row')), may hold values from -6 to 6
- pooled: bfloat16 [8192, 2048], P(('table', 'row')), may hold values from -6 to 6
- labels: int32 [8192], P(('table', 'row')), may hold values 0 or 1
- cross_down: bfloat16 [2176, 256], replicated, may hold values from -0.125 to 0.125
- cross_up: bfloat16 [256, 2176], replicated, may hold values from -0.375 to 0.375
- cross_bias: float32 [2176], replicated, may hold values from -3 to 3
- w_hidden1: bfloat16 [2176, 1024], replicated, may hold values from -0.125 to 0.125
- bias1: float32 [1024], replicated, may hold values from -3 to 3
- w_hidden2: bfloat16 [1024, 1024], replicated, may hold values from -0.1875 to 0.1875
- bias2: float32 [1024], replicated, may hold values from -3 to 3
- w_logit: float32 [1024], replicated, may hold values from -0.6 to 0.6
- lookup_slots: int32 [16, 8192, 4], P('table'), may hold values from 0 to 2047, as said below
Outputs:
- row_grads: float32 [16, 2048, 128], P('table', 'row')
- grad_cross_down: float32 [2176, 256], P('row')
- grad_cross_up: float32 [256, 2176], P('row')
- grad_cross_bias: float32 [2176], P('row')
- grad_hidden1: float32 [2176, 1024], P('row')
- grad_bias1: float32 [1024], P('row')
- grad_hidden2: float32 [1024, 1024], P('row')
- grad_bias2: float32 [1024], P('row')
- grad_logit: float32 [1024], P('row')
The draws below stay inside these ranges and needn't reach their ends.
Inputs may be any that keep to these rules, and one draw needn't show every extreme that they name: `lookup_slots`: row shard r of a table owns the slots r * 512 to (r + 1) * 512 - 1; a lookup's slot is the deduplicated row that it reads.
All inputs are finite; a program needn't handle non-finite values. No bound on the sum of `labels` on one device may be relied on, other than what follows from the above.
Results may differ from the reference program's by a relative error of at most 0.015.
Values may be sent and summed in bfloat16 or wider, within the bound.
No kernel may reach another device: no remote copies, remote signals or barrier semaphores. Data moves between devices by JAX's collectives and lax.ppermute only.
A program may use at most 128 MiB of HBM per device.

```python
import jax
import jax.numpy as jnp
from jax import lax

EMB = 128
TABLES = 16
RANK = 256
HID = 1024
HOT = 4
BATCH = 8192
FEAT = 2176
U_SHARD = 512
SLOTS = 2048
N_ROW = 4


def draw_lookup_slots(key, part):
    key = jax.random.fold_in(key, 7)
    keys = jax.random.split(key, 4)
    shape = (TABLES, BATCH, HOT)
    first = jax.random.randint(keys[0], shape, 0, N_ROW)
    second = jax.random.randint(keys[1], shape, 0, N_ROW)
    shard = jnp.maximum(first, second)
    upper = jax.random.randint(keys[2], shape, 0, U_SHARD)
    lower = jax.random.randint(keys[3], shape, 0, U_SHARD)
    within = U_SHARD - 1 - jnp.minimum(upper, lower)
    slots = shard * U_SHARD + within
    slots = slots.at[:, 0, 0].set(SLOTS - 1)
    slots = slots.at[:, 0, 1].set(0)
    return slots.astype(jnp.int32)


def touch_ends(drawn, own_key, low, high):
    longest = drawn.shape.index(max(drawn.shape))
    spots = []
    for shift in (0, 1):
        where = [jax.random.randint(jax.random.fold_in(own_key, axis), (), 0, length) for axis, length in enumerate(drawn.shape)]
        where[longest] = (where[longest] + shift) % drawn.shape[longest]
        spots.append(tuple(where))
    return drawn.at[spots[0]].set(low).at[spots[1]].set(high)


def level_of(key, shape, cuts, least, largest):
    def one(axis_at, shards_of):
        draws = jax.random.uniform(jax.random.fold_in(jax.random.fold_in(key, 6), axis_at), (shards_of,), jnp.float32, least / len(cuts), largest / len(cuts))
        return jnp.repeat(jnp.exp(draws), shape[axis_at] // shards_of).reshape((-1,) + (1,) * (len(shape) - axis_at - 1))

    level = one(*cuts[0])
    for cut in cuts[1:]:
        level = level * one(*cut)
    return level


def gaussian(key, dims, width, bound, shards=(), kind=jnp.bfloat16):
    entries = width * jax.random.normal(key, dims, jnp.float32)
    if shards:
        entries = entries * level_of(key, dims, shards, -0.22, 0.18)
    return jnp.clip(entries, -bound, bound).astype(kind)


def setup_inputs(seed: int = 0) -> dict:
    streams_of = jax.random.split(jax.random.key(seed), 13)
    dense_feat = gaussian(streams_of[0], (BATCH, EMB), 1.0, 6.0, ((0, 32),))
    pooled = gaussian(streams_of[1], (BATCH, TABLES * EMB), 1.0, 6.0, ((0, 32),))
    labels = touch_ends((jax.random.randint(streams_of[2], (BATCH,), 0, 4) < 1).astype(jnp.int32), jax.random.fold_in(streams_of[2], 1), 0, 1)
    cross_down = gaussian(streams_of[3], (FEAT, RANK), FEAT ** -0.5, 0.125)
    cross_up = gaussian(streams_of[4], (RANK, FEAT), RANK ** -0.5, 0.375)
    cross_bias = gaussian(streams_of[5], (FEAT,), 0.5, 3.0, (), jnp.float32)
    w_hidden1 = gaussian(streams_of[6], (FEAT, HID), FEAT ** -0.5, 0.125)
    bias1 = gaussian(streams_of[7], (HID,), 0.5, 3.0, (), jnp.float32)
    w_hidden2 = gaussian(streams_of[8], (HID, HID), HID ** -0.5, 0.1875)
    bias2 = gaussian(streams_of[9], (HID,), 0.5, 3.0, (), jnp.float32)
    w_logit = gaussian(streams_of[10], (HID,), 0.1, 0.6, (), jnp.float32)
    lookup_slots = draw_lookup_slots(jax.random.fold_in(streams_of[12], 71), 0)
    return {"dense_feat": dense_feat, "pooled": pooled, "labels": labels, "cross_down": cross_down, "cross_up": cross_up, "cross_bias": cross_bias, "w_hidden1": w_hidden1, "bias1": bias1, "w_hidden2": w_hidden2, "bias2": bias2, "w_logit": w_logit, "lookup_slots": lookup_slots}


loss_scale = 16.0


def swish_slope(value):
    sig = jax.nn.sigmoid(value)
    return sig * (1.0 + value * (1.0 - sig))


def dense_backward(dense_feat, pooled, labels, cross_down, cross_up, cross_bias, w_hidden1, bias1, w_hidden2, bias2, w_logit):
    stacked = jnp.concatenate([dense_feat, pooled], axis=1)
    stacked_wide = stacked.astype(jnp.float32)
    reduced = jnp.dot(stacked, cross_down, preferred_element_type=jnp.float32).astype(jnp.bfloat16)
    widened = jnp.dot(reduced, cross_up, preferred_element_type=jnp.float32) + cross_bias
    crossed = (stacked_wide * widened + stacked_wide).astype(jnp.bfloat16)
    pre_first = jnp.dot(crossed, w_hidden1, preferred_element_type=jnp.float32) + bias1
    act_first = jax.nn.silu(pre_first).astype(jnp.bfloat16)
    pre_second = jnp.dot(act_first, w_hidden2, preferred_element_type=jnp.float32) + bias2
    act_second = jax.nn.silu(pre_second).astype(jnp.bfloat16)
    act_wide = act_second.astype(jnp.float32)
    logits = jnp.sum(act_wide * w_logit, axis=1)
    delta_logit = loss_scale * (jax.nn.sigmoid(logits) - labels.astype(jnp.float32))
    delta_second = (delta_logit[:, None] * w_logit[None, :] * swish_slope(pre_second)).astype(jnp.bfloat16)
    grad_logit = jnp.sum(act_wide * delta_logit[:, None], axis=0)
    grad_hidden2 = jnp.dot(act_first.T, delta_second, preferred_element_type=jnp.float32)
    grad_bias2 = jnp.sum(delta_second.astype(jnp.float32), axis=0)
    back_first = jnp.dot(delta_second, w_hidden2.T, preferred_element_type=jnp.float32)
    delta_first = (back_first * swish_slope(pre_first)).astype(jnp.bfloat16)
    grad_hidden1 = jnp.dot(crossed.T, delta_first, preferred_element_type=jnp.float32)
    grad_bias1 = jnp.sum(delta_first.astype(jnp.float32), axis=0)
    delta_crossed = jnp.dot(delta_first, w_hidden1.T, preferred_element_type=jnp.float32)
    delta_widened = (delta_crossed * stacked_wide).astype(jnp.bfloat16)
    grad_cross_up = jnp.dot(reduced.T, delta_widened, preferred_element_type=jnp.float32)
    grad_cross_bias = jnp.sum(delta_widened.astype(jnp.float32), axis=0)
    delta_reduced = jnp.dot(delta_widened, cross_up.T, preferred_element_type=jnp.float32).astype(jnp.bfloat16)
    grad_cross_down = jnp.dot(stacked.T, delta_reduced, preferred_element_type=jnp.float32)
    delta_stacked = delta_crossed * (widened + 1.0) + jnp.dot(delta_reduced, cross_down.T, preferred_element_type=jnp.float32)
    grads = (grad_cross_down, grad_cross_up, grad_cross_bias, grad_hidden1, grad_bias1, grad_hidden2, grad_bias2, grad_logit)
    return grads, delta_stacked


def reference(dense_feat, pooled, labels, cross_down, cross_up, cross_bias, w_hidden1, bias1, w_hidden2, bias2, w_logit, lookup_slots):
    grads, delta_stacked = dense_backward(dense_feat, pooled, labels, cross_down, cross_up, cross_bias, w_hidden1, bias1, w_hidden2, bias2, w_logit)
    rounded = delta_stacked[:, EMB:].astype(jnp.bfloat16)
    rounded = lax.optimization_barrier(rounded)
    pooled_grad = rounded.astype(jnp.float32).reshape(BATCH, TABLES, EMB)
    by_table = jnp.transpose(pooled_grad, (1, 0, 2))
    values = jnp.broadcast_to(by_table[:, :, None, :], (TABLES, BATCH, HOT, EMB)).reshape(TABLES * BATCH * HOT, EMB)
    offsets = (jnp.arange(TABLES, dtype=jnp.int32) * jnp.int32(SLOTS)).astype(jnp.int32)
    flat_ids = (lookup_slots.astype(jnp.int32) + offsets[:, None, None]).astype(jnp.int32).reshape(TABLES * BATCH * HOT)
    summed = jax.ops.segment_sum(values, flat_ids, num_segments=TABLES * SLOTS)
    row_grads = summed.reshape(TABLES, SLOTS, EMB)
    return (row_grads, grads[0], grads[1], grads[2], grads[3], grads[4], grads[5], grads[6], grads[7])
```

```python
import functools

import jax
import jax.numpy as jnp
from jax import lax
from jax.experimental import pallas as pl
from jax.experimental.pallas import tpu as pltpu
from jax.sharding import PartitionSpec as P

loss_scale = 16.0
LANES = 128
VMEM_BYTES = 52 * 1024 * 1024
bf16 = jnp.bfloat16
f32 = jnp.float32


def round_up(value, unit):
    return -(-value // unit) * unit


def matmul(left, right):
    return jnp.dot(left, right, preferred_element_type=f32)


def matmul_rt(left, right):
    return lax.dot_general(left, right, (((1,), (1,)), ((), ())), preferred_element_type=f32)


def put_blocks(ref, offset, value, shards):
    rows = value.shape[0] // shards
    step = round_up(rows, 16)
    for shard in range(shards):
        for block in range(value.shape[1] // LANES):
            start = offset + block * step
            ref[shard, start : start + rows, :] = value[
                shard * rows : (shard + 1) * rows, block * LANES : (block + 1) * LANES
            ].astype(ref.dtype)


def put_rows(ref, offset, value):
    for block in range(value.shape[1] // LANES):
        ref[offset + block : offset + block + 1, :] = value[:, block * LANES : (block + 1) * LANES]


def front_kernel(
    shards,
    pos,
    dense_feat,
    pooled,
    labels,
    cross_down,
    cross_up,
    cross_bias,
    w_hidden1,
    bias1,
    w_hidden2,
    bias2,
    w_logit,
    send2,
    keep2,
    send1,
    keep1,
    delta_first_out,
    reduced_out,
    small,
    halves,
):
    core = pos[0]
    stacked = jnp.concatenate([dense_feat[...], pooled[...]], axis=1)
    reduced = matmul(stacked, cross_down[...]).astype(bf16)
    reduced_out[...] = reduced
    widened = matmul(reduced, cross_up[...]) + cross_bias[...]
    wide = stacked.astype(f32)
    crossed = (wide * widened + wide).astype(bf16)
    pre_first = matmul(crossed, w_hidden1[...]) + bias1[...]
    sig_first = jax.nn.sigmoid(pre_first)
    act_first = (pre_first * sig_first).astype(bf16)
    slope_first = sig_first * (1.0 + pre_first * (1.0 - sig_first))
    pre_second = matmul(act_first, w_hidden2[...]) + bias2[...]
    sig_second = jax.nn.sigmoid(pre_second)
    act_second = (pre_second * sig_second).astype(bf16).astype(f32)
    slope_second = sig_second * (1.0 + pre_second * (1.0 - sig_second))
    logits = jnp.sum(act_second * w_logit[...], axis=1, keepdims=True)
    count = labels.shape[1]
    same = lax.broadcasted_iota(jnp.int32, (count, count), 0) == lax.broadcasted_iota(
        jnp.int32, (count, count), 1
    )
    label_col = jnp.sum(jnp.where(same, labels[...].astype(f32), 0.0), axis=1, keepdims=True)
    delta_logit = loss_scale * (jax.nn.sigmoid(logits) - label_col)
    delta_second = (delta_logit * w_logit[...] * slope_second).astype(bf16)
    put_rows(small, 16, jnp.sum(act_second * delta_logit, axis=0, keepdims=True))
    put_rows(small, 8, jnp.sum(delta_second.astype(f32), axis=0, keepdims=True))
    half = halves.shape[2]
    halves[0] = delta_second[:, :half]
    halves[1] = delta_second[:, half:]
    act_t = act_first.T
    put_blocks(send2, 0, matmul(act_t, halves[1 - core]), shards)
    put_blocks(keep2, 0, matmul(act_t, halves[core]), shards)
    delta_first = (matmul_rt(delta_second, w_hidden2[...]) * slope_first).astype(bf16)
    delta_first_out[...] = delta_first
    put_rows(small, 0, jnp.sum(delta_first.astype(f32), axis=0, keepdims=True))
    halves[0] = delta_first[:, :half]
    halves[1] = delta_first[:, half:]
    crossed_t = crossed.T
    put_blocks(send1, 0, matmul(crossed_t, halves[1 - core]), shards)
    put_blocks(keep1, 0, matmul(crossed_t, halves[core]), shards)


def back_kernel(
    shards,
    groups,
    pos,
    dense_feat,
    pooled,
    cross_down,
    cross_up,
    cross_bias,
    w_hidden1,
    delta_first,
    reduced,
    small_in,
    send3,
    keep3,
    *rest,
):
    outs = rest[:groups]
    wide_delta, half_delta, by_group, small = rest[groups:]
    core = pos[0]
    table_pos = pos[2]
    width = dense_feat.shape[1]
    rank = cross_down.shape[1]
    feat = cross_up.shape[1]
    stacked = jnp.concatenate([dense_feat[...], pooled[...]], axis=1)
    wide = stacked.astype(f32)
    delta_crossed = matmul_rt(delta_first[...], w_hidden1[...])
    delta_widened = (delta_crossed * wide).astype(bf16)
    delta_reduced = matmul_rt(delta_widened, cross_up[...]).astype(bf16)
    widened = matmul(reduced[...], cross_up[...]) + cross_bias[...]
    delta_stacked = delta_crossed * (widened + 1.0) + matmul_rt(delta_reduced, cross_down[...])
    per_group = by_group.shape[1]
    for table in range(groups * per_group):
        by_group[table // per_group, table % per_group] = delta_stacked[
            :, width * (table + 1) : width * (table + 2)
        ].astype(bf16)
    for which in range(groups):
        outs[which][...] = by_group[table_pos ^ which]
    span = 9 * LANES
    wide_delta[...] = delta_widened
    half_delta[0] = delta_reduced[:, : rank // 2]
    half_delta[1] = delta_reduced[:, rank // 2 :]
    put_rows(small, 24, jnp.sum(delta_widened.astype(f32), axis=0, keepdims=True))
    small[0:24, :] = small_in[...]
    reduced_t = reduced[...].T
    stacked_t = stacked.T
    down_rows = (rank // 2 // LANES) * round_up(feat // shards, 16)
    up_rows = 9 * round_up(rank // shards, 16)
    for ref, who in ((send3, 1 - core), (keep3, core)):
        put_blocks(ref, 0, matmul(stacked_t, half_delta[who]), shards)
        start = pl.multiple_of(who * (feat - span), LANES)
        put_blocks(ref, down_rows, matmul(reduced_t, wide_delta[:, pl.ds(start, span)]), shards)
        for shard in range(shards):
            ref[shard, down_rows + up_rows : down_rows + up_rows + 48, :] = small[...].astype(bf16)
            if ref.shape[1] > down_rows + up_rows + 48:
                ref[shard, down_rows + up_rows + 48 :, :] = jnp.zeros(
                    (ref.shape[1] - down_rows - up_rows - 48, LANES), bf16
                )


def count_kernel(n_row, block, hot, n_src, pos, slots, *rest):
    values, out = rest[:n_src], rest[n_src]
    table = pl.program_id(0)
    base = pl.program_id(1) * block
    samples = values[0].shape[1]
    row_pos, table_pos = pos[1], pos[2]
    names = base + lax.broadcasted_iota(jnp.int32, (block, samples), 0)
    total = jnp.zeros((block, values[0].shape[2]), f32)
    for which in range(n_src):
        start = pl.multiple_of(((table_pos ^ which) * n_row + row_pos) * samples, LANES)
        counts = jnp.zeros((block, samples), f32)
        for look in range(hot):
            line = slots[table, look : look + 1, pl.ds(start, samples)]
            counts = counts + jnp.where(line == names, 1.0, 0.0)
        total = total + matmul(counts.astype(bf16), values[which][table])
    out[0] = total.astype(out.dtype)


def unpack_kernel(shards, pos, *refs):
    own, other = refs[0:3], refs[3:6]
    g_down, g_up, g_first, g_second, g_small = refs[6:11]
    held = refs[11:14]
    core = pos[0]
    z_pos = pos[2] // 2
    for mine, theirs, ref in zip(own, other, held):
        n_z, rows = mine.shape[0], mine.shape[1]
        for which in range(n_z):
            start = pl.multiple_of((z_pos ^ which) * rows, 16)
            ref[core, pl.ds(start, rows), :] = mine[which]
            ref[1 - core, pl.ds(start, rows), :] = theirs[which]
    second, first, third = held
    for out, ref, offset, spans in (
        (g_second, second, 0, None),
        (g_first, first, 0, None),
        (g_down, third, 0, None),
        (g_up, third, -1, 9),
    ):
        rows = out.shape[0]
        step = round_up(rows, 16)
        blocks = out.shape[1] // LANES
        if offset < 0:
            offset = round_up(g_down.shape[0], 16) * (g_down.shape[1] // 2 // LANES)
        for block in range(blocks):
            if spans is None:
                half, place = divmod(block, blocks // 2)
            else:
                half = 0 if block < spans else 1
                place = block - half * (blocks - spans)
            start = offset + place * step
            out[:, block * LANES : (block + 1) * LANES] = ref[
                half, start : start + rows, :
            ].astype(f32)
    start = round_up(g_down.shape[0], 16) * (g_down.shape[1] // 2 // LANES)
    start = start + 9 * round_up(g_up.shape[0], 16)
    g_small[...] = third[0, start : start + 48, :].astype(f32)


def whole(memory=pltpu.VMEM):
    return pl.BlockSpec(memory_space=memory)


def call(body, outs, scratch, n_in, name):
    return pl.pallas_call(
        body,
        out_shape=outs,
        in_specs=[whole(pltpu.SMEM)] + [whole()] * (n_in - 1),
        out_specs=[whole()] * len(outs),
        scratch_shapes=scratch,
        compiler_params=pltpu.CompilerParams(vmem_limit_bytes=VMEM_BYTES),
        name=name,
    )


def pick(value, index, axis):
    return lax.dynamic_index_in_dim(value, index, axis, keepdims=False)


def local(
    dense_feat,
    pooled,
    labels,
    cross_down,
    cross_up,
    cross_bias,
    w_hidden1,
    bias1,
    w_hidden2,
    bias2,
    w_logit,
    lookup_slots,
):
    n_table = lax.axis_size("table")
    n_row = lax.axis_size("row")
    n_z = n_table // 2
    bits = n_row.bit_length() - 1
    table_pos = lax.axis_index("table")
    row_pos = lax.axis_index("row")
    core = table_pos % 2
    z_pos = table_pos // 2
    pos = jnp.stack([core, row_pos, table_pos]).astype(jnp.int32)
    batch, width = dense_feat.shape
    feat, rank = cross_down.shape
    hid = w_hidden1.shape[1]
    tab_grp, _, hot = lookup_slots.shape
    u_shard = batch * n_table * hot // 16

    core_perm = [(at, at ^ 1) for at in range(n_table)]

    def z_perm(which):
        return [(at, at ^ (2 * which)) for at in range(n_table)]

    def row_perm(bit):
        return [(at, at ^ (1 << bit)) for at in range(n_row)]

    def packed(rows):
        return jax.ShapeDtypeStruct((n_row, rows, LANES), bf16)

    rows2 = (hid // 2 // LANES) * round_up(hid // n_row, 16)
    rows1 = (hid // 2 // LANES) * round_up(feat // n_row, 16)
    rows3 = (rank // 2 // LANES) * round_up(feat // n_row, 16) + 9 * round_up(rank // n_row, 16) + 48
    rows1, rows2, rows3 = (round_up(rows, 16 * n_z) for rows in (rows1, rows2, rows3))

    cbias = cross_bias.reshape(1, feat)
    send2, keep2, send1, keep1, delta_first, reduced, small = call(
        functools.partial(front_kernel, n_row),
        [
            packed(rows2),
            packed(rows2),
            packed(rows1),
            packed(rows1),
            jax.ShapeDtypeStruct((batch, hid), bf16),
            jax.ShapeDtypeStruct((batch, rank), bf16),
            jax.ShapeDtypeStruct((24, LANES), f32),
        ],
        [pltpu.VMEM((2, batch, hid // 2), bf16)],
        12,
        "front",
    )(
        pos,
        dense_feat,
        pooled,
        labels.reshape(1, batch),
        cross_down,
        cross_up,
        cbias,
        w_hidden1,
        bias1.reshape(1, hid),
        w_hidden2,
        bias2.reshape(1, hid),
        w_logit.reshape(1, hid),
    )
    got2 = lax.ppermute(send2, "table", core_perm)
    got1 = lax.ppermute(send1, "table", core_perm)

    outs = call(
        functools.partial(back_kernel, n_row, n_table),
        [packed(rows3), packed(rows3)]
        + [jax.ShapeDtypeStruct((tab_grp, batch, width), bf16)] * n_table,
        [
            pltpu.VMEM((batch, feat), bf16),
            pltpu.VMEM((2, batch, rank // 2), bf16),
            pltpu.VMEM((n_table, tab_grp, batch, width), bf16),
            pltpu.VMEM((48, LANES), f32),
        ],
        10,
        "back",
    )(pos, dense_feat, pooled, cross_down, cross_up, cbias, w_hidden1, delta_first, reduced, small)
    send3, keep3 = outs[:2]
    got3 = lax.ppermute(send3, "table", core_perm)
    values = [outs[2]]
    for which in range(1, n_table):
        perm = [(at, at ^ which) for at in range(n_table)]
        values.append(lax.ppermute(outs[2 + which], "table", perm))

    def halve(total, order):
        left = list(range(bits - 1, -1, -1))
        total = total.reshape((2,) * bits + total.shape[1:])
        for bit in order:
            axis = left.index(bit)
            left.remove(bit)
            mine = (row_pos >> bit) & 1
            sent = pick(total, 1 - mine, axis).astype(bf16)
            got = lax.ppermute(sent, "row", row_perm(bit))
            total = pick(total, mine, axis) + got.astype(f32)
        return total

    up_order = tuple(range(bits))
    down_order = up_order[::-1]

    def sum_z(total):
        parts = total.astype(bf16).reshape(n_z, total.shape[0] // n_z, LANES)
        result = pick(parts, z_pos, 0).astype(f32)
        for which in range(1, n_z):
            got = lax.ppermute(pick(parts, z_pos ^ which, 0), "table", z_perm(which))
            result = result + got.astype(f32)
        result = result.astype(bf16)
        pieces = [result]
        for which in range(1, n_z):
            pieces.append(lax.ppermute(result, "table", z_perm(which)))
        mine = jnp.stack(pieces)
        return mine, lax.ppermute(mine, "table", core_perm)

    streams = []
    for keep, got, order in (
        (keep2, got2, down_order),
        (keep1, got1, up_order),
        (keep3, got3, down_order),
    ):
        streams.append(sum_z(halve(keep.astype(f32) + got.astype(f32), order)))

    slots = jnp.transpose(lookup_slots, (0, 2, 1))
    n_slots = n_row * u_shard
    block = min(512, u_shard)
    sums = pl.pallas_call(
        functools.partial(count_kernel, n_row, block, hot, n_table),
        out_shape=jax.ShapeDtypeStruct((tab_grp, n_slots, width), bf16),
        grid=(tab_grp, n_slots // block),
        in_specs=[whole(pltpu.SMEM)] + [whole()] * (1 + n_table),
        out_specs=pl.BlockSpec((1, block, width), lambda table, at: (table, at, 0)),
        compiler_params=pltpu.CompilerParams(vmem_limit_bytes=VMEM_BYTES),
        name="counts",
    )(pos, slots, *values)
    row_grads = jnp.stack(
        [
            halve(
                sums[table].reshape(n_row, u_shard, width).astype(f32),
                down_order if table % 2 else up_order,
            )
            for table in range(tab_grp)
        ]
    )

    g_down, g_up, g_first, g_second, g_small = call(
        functools.partial(unpack_kernel, n_row),
        [
            jax.ShapeDtypeStruct((feat // n_row, rank), f32),
            jax.ShapeDtypeStruct((rank // n_row, feat), f32),
            jax.ShapeDtypeStruct((feat // n_row, hid), f32),
            jax.ShapeDtypeStruct((hid // n_row, hid), f32),
            jax.ShapeDtypeStruct((48, LANES), f32),
        ],
        [pltpu.VMEM((2, rows, LANES), bf16) for rows in (rows2, rows1, rows3)],
        7,
        "unpack",
    )(pos, *[mine for mine, _ in streams], *[theirs for _, theirs in streams])

    flat = g_small.reshape(-1)

    def part(start, length):
        share = length // n_row
        return lax.dynamic_slice(flat, (start * LANES + row_pos * share,), (share,))

    return (
        row_grads,
        g_down,
        g_up,
        part(24, feat),
        g_first,
        part(0, hid),
        g_second,
        part(8, hid),
        part(16, hid),
    )


def solution(mesh):
    in_specs = (
        P(("table", "row"), None),
        P(("table", "row"), None),
        P(("table", "row")),
        P(),
        P(),
        P(),
        P(),
        P(),
        P(),
        P(),
        P(),
        P("table", None, None),
    )
    out_specs = (
        P("table", "row", None),
        P("row", None),
        P("row", None),
        P("row"),
        P("row", None),
        P("row"),
        P("row", None),
        P("row"),
        P("row"),
    )
    return jax.shard_map(local, mesh=mesh, in_specs=in_specs, out_specs=out_specs, check_vma=False)
```

```python
import functools

import jax
import jax.numpy as jnp
from jax import lax
from jax.experimental import pallas as pl
from jax.experimental.pallas import tpu as pltpu
from jax.sharding import PartitionSpec as P

loss_scale = 16.0
LANES = 128
VMEM_BYTES = 52 * 1024 * 1024
bf16 = jnp.bfloat16
f32 = jnp.float32


def round_up(value, unit):
    return -(-value // unit) * unit


def matmul(left, right):
    return jnp.dot(left, right, preferred_element_type=f32)


def matmul_rt(left, right):
    return lax.dot_general(left, right, (((1,), (1,)), ((), ())), preferred_element_type=f32)


def reverse_bits(value, bits):
    out = 0
    for bit in range(bits):
        out = out | (((value >> bit) & 1) << (bits - 1 - bit))
    return out


def places_of(z_pos, n_z):
    bits = n_z.bit_length() - 1
    return [reverse_bits(z_pos ^ quarter, bits) for quarter in range(n_z)]


def put_blocks(ref, row_pos, places, offset, value):
    shards, rows_q = ref.shape[0], ref.shape[2]
    rows = value.shape[0] // shards
    step = round_up(rows, 16)
    blocks = value.shape[1] // LANES
    for shard in range(shards):
        slot = shard ^ row_pos
        for block in range(blocks):
            done = 0
            while done < rows:
                quarter, at = divmod(offset + block * step + done, rows_q)
                length = min(rows - done, rows_q - at)
                ref[slot, places[quarter], at : at + length, :] = value[
                    shard * rows + done : shard * rows + done + length,
                    block * LANES : (block + 1) * LANES,
                ].astype(ref.dtype)
                done += length
    return offset + blocks * step


def put_rows(ref, offset, value):
    for block in range(value.shape[1] // LANES):
        ref[offset + block : offset + block + 1, :] = value[:, block * LANES : (block + 1) * LANES]


def front_kernel(
    pos,
    dense_feat,
    pooled,
    labels,
    cross_down,
    cross_up,
    cross_bias,
    w_hidden1,
    bias1,
    w_hidden2,
    bias2,
    w_logit,
    send,
    keep,
    delta_first_out,
    crossed_out,
    reduced_out,
    small,
    halves,
    quarters,
):
    row_pos = pos[1]
    places = places_of(pos[2] // 2, send.shape[1])
    core = pos[0]
    stacked = jnp.concatenate([dense_feat[...], pooled[...]], axis=1)
    reduced = matmul(stacked, cross_down[...]).astype(bf16)
    reduced_out[...] = reduced
    widened = matmul(reduced, cross_up[...]) + cross_bias[...]
    wide = stacked.astype(f32)
    crossed = (wide * widened + wide).astype(bf16)
    pre_first = matmul(crossed, w_hidden1[...]) + bias1[...]
    sig_first = jax.nn.sigmoid(pre_first)
    act_first = (pre_first * sig_first).astype(bf16)
    slope_first = sig_first * (1.0 + pre_first * (1.0 - sig_first))
    pre_second = matmul(act_first, w_hidden2[...]) + bias2[...]
    sig_second = jax.nn.sigmoid(pre_second)
    act_second = (pre_second * sig_second).astype(bf16).astype(f32)
    slope_second = sig_second * (1.0 + pre_second * (1.0 - sig_second))
    logits = jnp.sum(act_second * w_logit[...], axis=1, keepdims=True)
    count = labels.shape[1]
    same = lax.broadcasted_iota(jnp.int32, (count, count), 0) == lax.broadcasted_iota(
        jnp.int32, (count, count), 1
    )
    label_col = jnp.sum(jnp.where(same, labels[...].astype(f32), 0.0), axis=1, keepdims=True)
    delta_logit = loss_scale * (jax.nn.sigmoid(logits) - label_col)
    delta_second = (delta_logit * w_logit[...] * slope_second).astype(bf16)
    put_rows(small, 16, jnp.sum(act_second * delta_logit, axis=0, keepdims=True))
    put_rows(small, 8, jnp.sum(delta_second.astype(f32), axis=0, keepdims=True))
    half = halves.shape[2]
    halves[0] = delta_second[:, :half]
    halves[1] = delta_second[:, half:]
    act_t = act_first.T
    offset = put_blocks(send, row_pos, places, 0, matmul(act_t, halves[1 - core]))
    put_blocks(keep, row_pos, places, 0, matmul(act_t, halves[core]))
    delta_first = (matmul_rt(delta_second, w_hidden2[...]) * slope_first).astype(bf16)
    delta_first_out[...] = delta_first
    crossed_out[...] = crossed
    put_rows(small, 0, jnp.sum(delta_first.astype(f32), axis=0, keepdims=True))
    quarter = quarters.shape[2]
    quarters[0] = delta_first[:, :quarter]
    quarters[1] = delta_first[:, half : half + quarter]
    crossed_t = crossed.T
    put_blocks(send, row_pos, places, offset, matmul(crossed_t, quarters[1 - core]))
    put_blocks(keep, row_pos, places, offset, matmul(crossed_t, quarters[core]))


def back_kernel(
    n_z,
    pos,
    dense_feat,
    pooled,
    cross_down,
    cross_up,
    cross_bias,
    w_hidden1,
    delta_first,
    crossed,
    reduced,
    small_in,
    send,
    keep,
    *rest,
):
    outs = rest[:n_z]
    wide_delta, half_delta, quarters, by_group, small = rest[n_z:]
    core, row_pos, z_pos = pos[0], pos[1], pos[2] // 2
    places = places_of(z_pos, send.shape[1])
    width = dense_feat.shape[1]
    rank = cross_down.shape[1]
    feat = cross_up.shape[1]
    stacked = jnp.concatenate([dense_feat[...], pooled[...]], axis=1)
    wide = stacked.astype(f32)
    delta_crossed = matmul_rt(delta_first[...], w_hidden1[...])
    delta_widened = (delta_crossed * wide).astype(bf16)
    delta_reduced = matmul_rt(delta_widened, cross_up[...]).astype(bf16)
    widened = matmul(reduced[...], cross_up[...]) + cross_bias[...]
    delta_stacked = delta_crossed * (widened + 1.0) + matmul_rt(delta_reduced, cross_down[...])
    per_group = by_group.shape[2]
    for table in range(2 * n_z * per_group):
        group = table // per_group
        by_group[group // 2, group % 2, table % per_group] = delta_stacked[
            :, width * (table + 1) : width * (table + 2)
        ].astype(bf16)
    for which in range(n_z):
        outs[which][0] = by_group[z_pos ^ which, core]
        outs[which][1] = by_group[z_pos ^ which, 1 - core]
    span = 9 * LANES
    wide_delta[...] = delta_widened
    half_delta[0] = delta_reduced[:, : rank // 2]
    half_delta[1] = delta_reduced[:, rank // 2 :]
    hid = delta_first.shape[1]
    quarter = quarters.shape[2]
    quarters[0] = delta_first[:, quarter : hid // 2]
    quarters[1] = delta_first[:, hid // 2 + quarter :]
    put_rows(small, 24, jnp.sum(delta_widened.astype(f32), axis=0, keepdims=True))
    small[0:24, :] = small_in[...]
    small[41:48, :] = jnp.zeros((7, LANES), f32)
    reduced_t = reduced[...].T
    stacked_t = stacked.T
    crossed_t = crossed[...].T
    sums = small[...]
    for ref, who in ((send, 1 - core), (keep, core)):
        offset = put_blocks(ref, row_pos, places, 0, matmul(crossed_t, quarters[who]))
        offset = put_blocks(ref, row_pos, places, offset, matmul(stacked_t, half_delta[who]))
        start = pl.multiple_of(who * (feat - span), LANES)
        offset = put_blocks(
            ref, row_pos, places, offset, matmul(reduced_t, wide_delta[:, pl.ds(start, span)])
        )
        n_row = ref.shape[0]
        end = put_blocks(ref, row_pos, places, offset, jnp.concatenate([sums] * n_row, axis=0))
        tail = ref.shape[1] * ref.shape[2] - end
        if tail:
            put_blocks(ref, row_pos, places, end, jnp.zeros((n_row * tail, LANES), f32))


def count_kernel(n_row, table, hot, n_z, pos, slots, *rest):
    direct, crossed, out = rest[:n_z], rest[n_z : 2 * n_z], rest[2 * n_z]
    block = out.shape[1]
    samples = direct[0].shape[2]
    core, row_pos, z_pos = pos[0], pos[1], pos[2] // 2
    base = (pl.program_id(0) ^ row_pos) * block
    names = lax.broadcasted_iota(jnp.int16, (block, samples), 0)
    total = jnp.zeros((block, out.shape[2]), f32)
    one = jnp.ones((block, samples), bf16)
    zero = jnp.zeros((block, samples), bf16)
    for which in range(n_z):
        for held, who in ((direct[which][0, table], core), (crossed[which][table], 1 - core)):
            source = 2 * (z_pos ^ which) + who
            start = pl.multiple_of((source * n_row + row_pos) * samples, LANES)
            lines = slots[table, :, pl.ds(start, samples)] - base
            lines = jnp.where((lines >= 0) & (lines < block), lines, block).astype(jnp.int16)
            counts = zero
            for look in range(hot):
                line = jnp.broadcast_to(lines[look : look + 1, :], (block, samples))
                counts = counts + jnp.where(line == names, one, zero)
            total = total + matmul(counts, held)
    out[0] = total.astype(out.dtype)


def unpack_kernel(pos, *refs):
    parts = refs[0:8]
    g_down, g_up, g_first, g_second, g_small = refs[8:13]
    held = refs[13:15]
    core = pos[0]
    z_pos = pos[2] // 2
    for stream in range(2):
        lower, upper, lower_other, upper_other = parts[4 * stream : 4 * stream + 4]
        ref = held[stream]
        rows = lower.shape[1]
        n_z = 2 * lower.shape[0]
        z_bits = n_z.bit_length() - 1
        for who, pieces in ((core, (lower, upper)), (1 - core, (lower_other, upper_other))):
            for place in range(n_z):
                start = pl.multiple_of((reverse_bits(place, z_bits) ^ z_pos) * rows, 16)
                ref[who, pl.ds(start, rows), :] = pieces[place // (n_z // 2)][place % (n_z // 2)]
    front, back = held

    def take(ref, out, half, offset, columns):
        rows = out.shape[0]
        step = round_up(rows, 16)
        for column in columns:
            out[:, column * LANES : (column + 1) * LANES] = ref[
                half, offset : offset + rows, :
            ].astype(f32)
            offset += step
        return offset

    for half in range(2):
        blocks = g_second.shape[1] // LANES // 2
        offset = take(front, g_second, half, 0, range(half * blocks, (half + 1) * blocks))
        blocks = g_first.shape[1] // LANES // 4
        take(front, g_first, half, offset, range(2 * half * blocks, (2 * half + 1) * blocks))
        offset = take(
            back, g_first, half, 0, range((2 * half + 1) * blocks, (2 * half + 2) * blocks)
        )
        blocks = g_down.shape[1] // LANES // 2
        offset = take(back, g_down, half, offset, range(half * blocks, (half + 1) * blocks))
        blocks = g_up.shape[1] // LANES
        offset = take(back, g_up, half, offset, range(half * (blocks - 9), half * (blocks - 9) + 9))
    g_small[...] = back[0, offset : offset + 48, :].astype(f32)


def whole(memory=pltpu.VMEM):
    return pl.BlockSpec(memory_space=memory)


def cost(micros):
    return pl.CostEstimate(flops=int(micros * 1.0e9), transcendentals=0, bytes_accessed=int(micros * 3.0e6))


def call(body, outs, scratch, n_in, name, micros):
    return pl.pallas_call(
        body,
        out_shape=outs,
        in_specs=[whole(pltpu.SMEM)] + [whole()] * (n_in - 1),
        out_specs=[whole()] * len(outs),
        scratch_shapes=scratch,
        compiler_params=pltpu.CompilerParams(vmem_limit_bytes=VMEM_BYTES),
        cost_estimate=cost(micros),
        name=name,
    )


def add_terms(terms):
    total = terms[0].astype(f32)
    for term in terms[1:]:
        total = total + term.astype(f32)
    return total


def local(
    dense_feat,
    pooled,
    labels,
    cross_down,
    cross_up,
    cross_bias,
    w_hidden1,
    bias1,
    w_hidden2,
    bias2,
    w_logit,
    lookup_slots,
):
    n_table = lax.axis_size("table")
    n_row = lax.axis_size("row")
    n_z = n_table // 2
    row_bits = n_row.bit_length() - 1
    z_bits = n_z.bit_length() - 1
    table_pos = lax.axis_index("table")
    row_pos = lax.axis_index("row")
    pos = jnp.stack([table_pos % 2, row_pos, table_pos]).astype(jnp.int32)
    batch, width = dense_feat.shape
    feat, rank = cross_down.shape
    hid = w_hidden1.shape[1]
    tab_grp, _, hot = lookup_slots.shape
    u_shard = batch * n_table * hot // 16

    def swap_cores(value):
        return lax.ppermute(value, "table", [(at, at ^ 1) for at in range(n_table)])

    def swap_z(value, which):
        return lax.ppermute(value, "table", [(at, at ^ (2 * which)) for at in range(n_table)])

    def swap_row(value, bit):
        return lax.ppermute(value, "row", [(at, at ^ (1 << bit)) for at in range(n_row)])

    rows_front = (hid // 2 // LANES) * round_up(hid // n_row, 16)
    rows_front += (hid // 4 // LANES) * round_up(feat // n_row, 16)
    rows_back = (hid // 4 // LANES) * round_up(feat // n_row, 16)
    rows_back += (rank // 2 // LANES) * round_up(feat // n_row, 16)
    rows_back += 9 * round_up(rank // n_row, 16) + 48
    rows_front, rows_back = (round_up(rows, 16 * n_z) for rows in (rows_front, rows_back))

    def packed(rows):
        return jax.ShapeDtypeStruct((n_row, n_z, rows // n_z, LANES), bf16)

    cbias = cross_bias.reshape(1, feat)
    send_front, keep_front, delta_first, crossed, reduced, small = call(
        front_kernel,
        [
            packed(rows_front),
            packed(rows_front),
            jax.ShapeDtypeStruct((batch, hid), bf16),
            jax.ShapeDtypeStruct((batch, feat), bf16),
            jax.ShapeDtypeStruct((batch, rank), bf16),
            jax.ShapeDtypeStruct((24, LANES), f32),
        ],
        [pltpu.VMEM((2, batch, hid // 2), bf16), pltpu.VMEM((2, batch, hid // 4), bf16)],
        12,
        "front",
        10,
    )(
        pos,
        dense_feat,
        pooled,
        labels.reshape(1, batch),
        cross_down,
        cross_up,
        cbias,
        w_hidden1,
        bias1.reshape(1, hid),
        w_hidden2,
        bias2.reshape(1, hid),
        w_logit.reshape(1, hid),
    )
    got_front = swap_cores(send_front)

    outs = call(
        functools.partial(back_kernel, n_z),
        [packed(rows_back), packed(rows_back)]
        + [jax.ShapeDtypeStruct((2, tab_grp, batch, width), bf16)] * n_z,
        [
            pltpu.VMEM((batch, feat), bf16),
            pltpu.VMEM((2, batch, rank // 2), bf16),
            pltpu.VMEM((2, batch, hid // 4), bf16),
            pltpu.VMEM((n_z, 2, tab_grp, batch, width), bf16),
            pltpu.VMEM((48, LANES), f32),
        ],
        11,
        "back",
        10,
    )(pos, dense_feat, pooled, cross_down, cross_up, cbias, w_hidden1, delta_first, crossed, reduced, small)
    send_back, keep_back = outs[:2]
    got_back = swap_cores(send_back)
    pooled_out = outs[2:]

    def halve_row(terms, order):
        left = list(range(row_bits - 1, -1, -1))
        terms = [term.reshape((2,) * row_bits + term.shape[1:]) for term in terms]
        for bit in order:
            axis = left.index(bit)
            left.remove(bit)
            sent = add_terms([lax.index_in_dim(term, 1, axis, keepdims=False) for term in terms])
            got = swap_row(sent.astype(bf16), bit)
            terms = [lax.index_in_dim(term, 0, axis, keepdims=False) for term in terms] + [got]
        return terms

    low_first = tuple(range(row_bits))
    high_first = low_first[::-1]

    def sum_dense(terms):
        lower = halve_row([term[:, : n_z // 2] for term in terms], low_first)
        upper = halve_row([term[:, n_z // 2 :] for term in terms], high_first)
        got = swap_z(add_terms(upper).astype(bf16), 1)
        terms = lower + [got]
        for stage in range(1, z_bits):
            middle = n_z >> (stage + 1)
            got = swap_z(add_terms([term[middle:] for term in terms]).astype(bf16), 1 << stage)
            terms = [term[:middle] for term in terms] + [got]
        own = add_terms(terms).astype(bf16)
        for stage in range(z_bits - 1, 0, -1):
            own = jnp.concatenate([own, swap_z(own, 1 << stage)], axis=0)
        far = swap_z(own, 1)
        return [own, far, swap_cores(own), swap_cores(far)]

    streams = sum_dense([keep_front, got_front]) + sum_dense([keep_back, got_back])

    values = [pooled_out[0]] + [swap_z(pooled_out[which], which) for which in range(1, n_z)]
    values += [swap_cores(value[1]) for value in values]
    slots = jnp.transpose(lookup_slots, (0, 2, 1))
    shares = []
    for table in range(tab_grp):
        sums = pl.pallas_call(
            functools.partial(count_kernel, n_row, table, hot, n_z),
            out_shape=jax.ShapeDtypeStruct((n_row, u_shard, width), bf16),
            grid=(n_row,),
            in_specs=[whole(pltpu.SMEM)] + [whole()] * (1 + 2 * n_z),
            out_specs=pl.BlockSpec((1, u_shard, width), lambda at: (at, 0, 0)),
            compiler_params=pltpu.CompilerParams(vmem_limit_bytes=VMEM_BYTES),
            cost_estimate=cost(7),
            name="counts",
        )(pos, slots, *values)
        shares.append(add_terms(halve_row([sums], high_first if table % 2 else low_first)))
    row_grads = jnp.stack(shares)

    g_down, g_up, g_first, g_second, g_small = call(
        unpack_kernel,
        [
            jax.ShapeDtypeStruct((feat // n_row, rank), f32),
            jax.ShapeDtypeStruct((rank // n_row, feat), f32),
            jax.ShapeDtypeStruct((feat // n_row, hid), f32),
            jax.ShapeDtypeStruct((hid // n_row, hid), f32),
            jax.ShapeDtypeStruct((48, LANES), f32),
        ],
        [pltpu.VMEM((2, rows, LANES), bf16) for rows in (rows_front, rows_back)],
        9,
        "unpack",
        4,
    )(pos, *streams)

    flat = g_small.reshape(-1)

    def part(start, length):
        share = length // n_row
        return lax.dynamic_slice(flat, (start * LANES + row_pos * share,), (share,))

    return (
        row_grads,
        g_down,
        g_up,
        part(24, feat),
        g_first,
        part(0, hid),
        g_second,
        part(8, hid),
        part(16, hid),
    )


def solution(mesh):
    in_specs = (
        P(("table", "row"), None),
        P(("table", "row"), None),
        P(("table", "row")),
        P(),
        P(),
        P(),
        P(),
        P(),
        P(),
        P(),
        P(),
        P("table", None, None),
    )
    out_specs = (
        P("table", "row", None),
        P("row", None),
        P("row", None),
        P("row"),
        P("row", None),
        P("row"),
        P("row", None),
        P("row"),
        P("row"),
    )
    return jax.shard_map(local, mesh=mesh, in_specs=in_specs, out_specs=out_specs, check_vma=False)
```

```python
import functools

import jax
import jax.numpy as jnp
from jax import lax
from jax.experimental import pallas as pl
from jax.experimental.pallas import tpu as pltpu
from jax.sharding import PartitionSpec as P

loss_scale = 16.0
LANES = 128
SPAN = 9 * LANES
VMEM_BYTES = 52 * 1024 * 1024
bf16 = jnp.bfloat16
f32 = jnp.float32


def round_up(value, unit):
    return -(-value // unit) * unit


def matmul(left, right):
    return jnp.dot(left, right, preferred_element_type=f32)


def matmul_rt(left, right):
    return lax.dot_general(left, right, (((1,), (1,)), ((), ())), preferred_element_type=f32)


def reverse_bits(value, bits):
    out = 0
    for bit in range(bits):
        out = out | (((value >> bit) & 1) << (bits - 1 - bit))
    return out


def places_of(z_pos, n_z):
    bits = n_z.bit_length() - 1
    return [reverse_bits(z_pos ^ quarter, bits) for quarter in range(n_z)]


def put_blocks(ref, row_pos, places, offset, value):
    shards, rows_q = ref.shape[0], ref.shape[2]
    rows = value.shape[0] // shards
    step = round_up(rows, 16)
    blocks = value.shape[1] // LANES
    for shard in range(shards):
        slot = shard ^ row_pos
        for block in range(blocks):
            done = 0
            while done < rows:
                quarter, at = divmod(offset + block * step + done, rows_q)
                length = min(rows - done, rows_q - at)
                ref[slot, places[quarter], at : at + length, :] = value[
                    shard * rows + done : shard * rows + done + length,
                    block * LANES : (block + 1) * LANES,
                ].astype(ref.dtype)
                done += length
    return offset + blocks * step


def put_rows(ref, offset, value):
    for block in range(value.shape[1] // LANES):
        ref[offset + block : offset + block + 1, :] = value[:, block * LANES : (block + 1) * LANES]


def split_parts(pack, low, high):
    half = low.shape[1]
    low[...] = pack[:, :half]
    high[...] = pack[:, half:]


class Loads:
    def __init__(self, sources, targets, sems):
        self.copies = [
            pltpu.make_async_copy(source, target, sems.at[at])
            for at, (source, target) in enumerate(zip(sources, targets))
        ]
        self.targets = targets
        self.ready = set()
        for copy in self.copies:
            copy.start()

    def __call__(self, at):
        if at not in self.ready:
            self.copies[at].wait()
            self.ready.add(at)
        return self.targets[at][...]


def as_row(value):
    return value.reshape(1, value.shape[-1])


def front_kernel(pos, *refs):
    sources, outs, targets = refs[:11], refs[11:18], refs[18:29]
    halves, quarters, pack, sems = refs[29:]
    send_low, send_high, act_t_out, second_out, crossed_t_out, first_out, small = outs
    load = Loads(sources, targets, sems)
    core, row_pos = pos[0], pos[1]
    places = places_of(pos[2] // 2, pack.shape[1])
    stacked = jnp.concatenate([load(0), load(1)], axis=1)
    reduced = matmul(stacked, load(2)).astype(bf16)
    widened = matmul(reduced, load(3)) + as_row(load(4))
    wide = stacked.astype(f32)
    crossed = (wide * widened + wide).astype(bf16)
    pre_first = matmul(crossed, load(5)) + as_row(load(6))
    sig_first = jax.nn.sigmoid(pre_first)
    act_first = (pre_first * sig_first).astype(bf16)
    slope_first = sig_first * (1.0 + pre_first * (1.0 - sig_first))
    w_hidden2 = load(7)
    pre_second = matmul(act_first, w_hidden2) + as_row(load(8))
    sig_second = jax.nn.sigmoid(pre_second)
    act_second = (pre_second * sig_second).astype(bf16).astype(f32)
    slope_second = sig_second * (1.0 + pre_second * (1.0 - sig_second))
    w_logit = as_row(load(9))
    logits = jnp.sum(act_second * w_logit, axis=1, keepdims=True)
    labels = as_row(load(10))
    count = labels.shape[1]
    same = lax.broadcasted_iota(jnp.int32, (count, count), 0) == lax.broadcasted_iota(
        jnp.int32, (count, count), 1
    )
    label_col = jnp.sum(jnp.where(same, labels.astype(f32), 0.0), axis=1, keepdims=True)
    delta_logit = loss_scale * (jax.nn.sigmoid(logits) - label_col)
    delta_second = (delta_logit * w_logit * slope_second).astype(bf16)
    second_out[...] = delta_second
    put_rows(small, 16, jnp.sum(act_second * delta_logit, axis=0, keepdims=True))
    put_rows(small, 8, jnp.sum(delta_second.astype(f32), axis=0, keepdims=True))
    half = halves.shape[2]
    halves[0] = delta_second[:, :half]
    halves[1] = delta_second[:, half:]
    act_t = act_first.T
    act_t_out[...] = act_t
    offset = put_blocks(pack, row_pos, places, 0, matmul(act_t, halves[1 - core]))
    delta_first = (matmul_rt(delta_second, w_hidden2) * slope_first).astype(bf16)
    first_out[...] = delta_first
    put_rows(small, 0, jnp.sum(delta_first.astype(f32), axis=0, keepdims=True))
    quarter = quarters.shape[2]
    quarters[0] = delta_first[:, :quarter]
    quarters[1] = delta_first[:, half : half + quarter]
    crossed_t = crossed.T
    crossed_t_out[...] = crossed_t
    put_blocks(pack, row_pos, places, offset, matmul(crossed_t, quarters[1 - core]))
    split_parts(pack, send_low, send_high)


def middle_kernel(n_z, pos, *refs):
    sources, direct = refs[:6], refs[6:10]
    keep_low, keep_high, widened_out, reduced_out = refs[10:14]
    pooled_outs = refs[14 : 14 + n_z]
    rest = refs[14 + n_z :]
    targets = rest[:6]
    halves, quarters, pack, by_group, sems = rest[6:]
    act_t, delta_second, crossed_t, delta_first = direct
    load = Loads(sources, targets, sems)
    core, row_pos, z_pos = pos[0], pos[1], pos[2] // 2
    places = places_of(z_pos, pack.shape[1])
    half, quarter = halves.shape[2], quarters.shape[2]
    halves[0] = delta_second[:, :half]
    halves[1] = delta_second[:, half:]
    offset = put_blocks(pack, row_pos, places, 0, matmul(act_t[...], halves[core]))
    quarters[0] = delta_first[:, :quarter]
    quarters[1] = delta_first[:, half : half + quarter]
    put_blocks(pack, row_pos, places, offset, matmul(crossed_t[...], quarters[core]))
    split_parts(pack, keep_low, keep_high)
    delta_crossed = matmul_rt(delta_first[...], load(0))
    stacked = jnp.concatenate([load(1), load(2)], axis=1)
    delta_widened = (delta_crossed * stacked.astype(f32)).astype(bf16)
    widened_out[...] = delta_widened
    cross_up, cross_down = load(3), load(4)
    delta_reduced = matmul_rt(delta_widened, cross_up).astype(bf16)
    reduced_out[...] = delta_reduced
    reduced = matmul(stacked, cross_down).astype(bf16)
    widened = matmul(reduced, cross_up) + as_row(load(5))
    delta_stacked = delta_crossed * (widened + 1.0) + matmul_rt(delta_reduced, cross_down)
    width = targets[1].shape[1]
    per_group = by_group.shape[2]
    for table in range(2 * n_z * per_group):
        group = table // per_group
        by_group[group // 2, group % 2, table % per_group] = delta_stacked[
            :, width * (table + 1) : width * (table + 2)
        ].astype(bf16)
    for which in range(n_z):
        pooled_outs[which][0] = by_group[z_pos ^ which, core]
        pooled_outs[which][1] = by_group[z_pos ^ which, 1 - core]


def back_kernel(pos, *refs):
    dense_feat, pooled, cross_down, crossed_t, delta_first, delta_widened, delta_reduced = refs[:7]
    small_in = refs[7]
    send_low, send_high, keep_low, keep_high = refs[10:14]
    half_delta, quarters, pack, small = refs[14:]
    core, row_pos = pos[0], pos[1]
    n_row = pack.shape[0]
    places = places_of(pos[2] // 2, pack.shape[1])
    rank = delta_reduced.shape[1]
    feat = delta_widened.shape[1]
    hid = delta_first.shape[1]
    quarter = quarters.shape[2]
    half_delta[0] = delta_reduced[:, : rank // 2]
    half_delta[1] = delta_reduced[:, rank // 2 :]
    quarters[0] = delta_first[:, quarter : hid // 2]
    quarters[1] = delta_first[:, hid // 2 + quarter :]
    put_rows(small, 24, jnp.sum(delta_widened[...].astype(f32), axis=0, keepdims=True))
    small[0:24, :] = small_in[...]
    small[41:48, :] = jnp.zeros((7, LANES), f32)
    sums = jnp.concatenate([small[...]] * n_row, axis=0)
    stacked = jnp.concatenate([dense_feat[...], pooled[...]], axis=1)
    reduced_t = matmul(stacked, cross_down[...]).astype(bf16).T
    stacked_t = stacked.T
    for low, high, who in ((send_low, send_high, 1 - core), (keep_low, keep_high, core)):
        offset = put_blocks(pack, row_pos, places, 0, matmul(crossed_t[...], quarters[who]))
        offset = put_blocks(pack, row_pos, places, offset, matmul(stacked_t, half_delta[who]))
        start = pl.multiple_of(who * (feat - SPAN), LANES)
        offset = put_blocks(
            pack, row_pos, places, offset, matmul(reduced_t, delta_widened[:, pl.ds(start, SPAN)])
        )
        offset = put_blocks(pack, row_pos, places, offset, sums)
        tail = pack.shape[1] * pack.shape[2] - offset
        if tail:
            put_blocks(pack, row_pos, places, offset, jnp.zeros((n_row * tail, LANES), f32))
        split_parts(pack, low, high)


def select_kernel(n_z, *refs):
    out = refs[-1]
    for which in range(n_z):
        out[which] = refs[which][1]


def count_kernel(n_row, table, hot, n_z, pos, slots, *rest):
    direct, crossed, out = rest[:n_z], rest[n_z], rest[-1]
    block = out.shape[1]
    samples = crossed.shape[2]
    core, row_pos, z_pos = pos[0], pos[1], pos[2] // 2
    base = (pl.program_id(0) ^ row_pos) * block
    names = lax.broadcasted_iota(jnp.int16, (block, samples), 0)
    total = jnp.zeros((block, out.shape[2]), f32)
    one = jnp.ones((block, samples), bf16)
    zero = jnp.zeros((block, samples), bf16)
    for which in range(n_z):
        for held, who in ((direct[which][0, table], core), (crossed[which, table], 1 - core)):
            source = 2 * (z_pos ^ which) + who
            start = pl.multiple_of((source * n_row + row_pos) * samples, LANES)
            lines = slots[table, :, pl.ds(start, samples)] - base
            lines = jnp.where((lines >= 0) & (lines < block), lines, block).astype(jnp.int16)
            counts = zero
            for look in range(hot):
                line = jnp.broadcast_to(lines[look : look + 1, :], (block, samples))
                counts = counts + jnp.where(line == names, one, zero)
            total = total + matmul(counts, held)
    out[0] = total.astype(out.dtype)


def unpack_kernel(pos, *refs):
    parts = refs[0:8]
    g_down, g_up, g_first, g_second, g_small = refs[8:13]
    held = refs[13:15]
    core = pos[0]
    z_pos = pos[2] // 2
    for stream in range(2):
        lower, upper, lower_other, upper_other = parts[4 * stream : 4 * stream + 4]
        ref = held[stream]
        rows = lower.shape[1]
        n_z = 2 * lower.shape[0]
        z_bits = n_z.bit_length() - 1
        for who, pieces in ((core, (lower, upper)), (1 - core, (lower_other, upper_other))):
            for place in range(n_z):
                start = pl.multiple_of((reverse_bits(place, z_bits) ^ z_pos) * rows, 16)
                ref[who, pl.ds(start, rows), :] = pieces[place // (n_z // 2)][place % (n_z // 2)]
    front, back = held

    def take(ref, out, half, offset, columns):
        rows = out.shape[0]
        step = round_up(rows, 16)
        for column in columns:
            out[:, column * LANES : (column + 1) * LANES] = ref[
                half, offset : offset + rows, :
            ].astype(f32)
            offset += step
        return offset

    for half in range(2):
        blocks = g_second.shape[1] // LANES // 2
        offset = take(front, g_second, half, 0, range(half * blocks, (half + 1) * blocks))
        blocks = g_first.shape[1] // LANES // 4
        take(front, g_first, half, offset, range(2 * half * blocks, (2 * half + 1) * blocks))
        offset = take(
            back, g_first, half, 0, range((2 * half + 1) * blocks, (2 * half + 2) * blocks)
        )
        blocks = g_down.shape[1] // LANES // 2
        offset = take(back, g_down, half, offset, range(half * blocks, (half + 1) * blocks))
        blocks = g_up.shape[1] // LANES
        offset = take(back, g_up, half, offset, range(half * (blocks - 9), half * (blocks - 9) + 9))
    g_small[...] = back[0, offset : offset + 48, :].astype(f32)


def whole(memory=pltpu.VMEM):
    return pl.BlockSpec(memory_space=memory)


def cost(micros):
    return pl.CostEstimate(
        flops=int(micros * 1.0e9), transcendentals=0, bytes_accessed=int(micros * 3.0e6)
    )


def call(body, outs, scratch, in_specs, name, micros):
    return pl.pallas_call(
        body,
        out_shape=outs,
        in_specs=in_specs,
        out_specs=[whole()] * len(outs),
        scratch_shapes=scratch,
        compiler_params=pltpu.CompilerParams(vmem_limit_bytes=VMEM_BYTES),
        cost_estimate=cost(micros),
        name=name,
    )


def held_like(values):
    return [pltpu.VMEM(value.shape, value.dtype) for value in values]


def add_terms(terms):
    total = terms[0].astype(f32)
    for term in terms[1:]:
        total = total + term.astype(f32)
    return total


def local(
    dense_feat,
    pooled,
    labels,
    cross_down,
    cross_up,
    cross_bias,
    w_hidden1,
    bias1,
    w_hidden2,
    bias2,
    w_logit,
    lookup_slots,
):
    n_table = lax.axis_size("table")
    n_row = lax.axis_size("row")
    n_z = n_table // 2
    row_bits = n_row.bit_length() - 1
    z_bits = n_z.bit_length() - 1
    table_pos = lax.axis_index("table")
    row_pos = lax.axis_index("row")
    pos = jnp.stack([table_pos % 2, row_pos, table_pos]).astype(jnp.int32)
    batch, width = dense_feat.shape
    feat, rank = cross_down.shape
    hid = w_hidden1.shape[1]
    tab_grp, _, hot = lookup_slots.shape
    u_shard = batch * n_table * hot // 16

    def swap_cores(value):
        return lax.ppermute(value, "table", [(at, at ^ 1) for at in range(n_table)])

    def swap_z(value, which):
        return lax.ppermute(value, "table", [(at, at ^ (2 * which)) for at in range(n_table)])

    def swap_row(value, bit):
        return lax.ppermute(value, "row", [(at, at ^ (1 << bit)) for at in range(n_row)])

    rows_front = (hid // 2 // LANES) * round_up(hid // n_row, 16)
    rows_front += (hid // 4 // LANES) * round_up(feat // n_row, 16)
    rows_back = (hid // 4 // LANES) * round_up(feat // n_row, 16)
    rows_back += (rank // 2 // LANES) * round_up(feat // n_row, 16)
    rows_back += 9 * round_up(rank // n_row, 16) + 48
    rows_front, rows_back = (round_up(rows, 16 * n_z) for rows in (rows_front, rows_back))

    def half_pack(rows):
        return jax.ShapeDtypeStruct((n_row, n_z // 2, rows // n_z, LANES), bf16)

    def pack_scratch(rows):
        return pltpu.VMEM((n_row, n_z, rows // n_z, LANES), bf16)

    def wide(*shape):
        return jax.ShapeDtypeStruct(shape, bf16)

    smem, hbm, vmem, anywhere = whole(pltpu.SMEM), whole(pltpu.HBM), whole(), whole(pl.ANY)

    sources = (
        dense_feat,
        pooled,
        cross_down,
        cross_up,
        cross_bias,
        w_hidden1,
        bias1,
        w_hidden2,
        bias2,
        w_logit,
        labels,
    )
    send_low, send_high, act_t, delta_second, crossed_t, delta_first, small = call(
        front_kernel,
        [
            half_pack(rows_front),
            half_pack(rows_front),
            wide(hid, batch),
            wide(batch, hid),
            wide(feat, batch),
            wide(batch, hid),
            jax.ShapeDtypeStruct((24, LANES), f32),
        ],
        held_like(sources)
        + [
            pltpu.VMEM((2, batch, hid // 2), bf16),
            pltpu.VMEM((2, batch, hid // 4), bf16),
            pack_scratch(rows_front),
            pltpu.SemaphoreType.DMA((len(sources),)),
        ],
        [smem] + [hbm] * len(sources),
        "front",
        10,
    )(pos, *sources)
    got_low, got_high = swap_cores(send_low), swap_cores(send_high)

    sources = (w_hidden1, dense_feat, pooled, cross_up, cross_down, cross_bias)
    outs = call(
        functools.partial(middle_kernel, n_z),
        [half_pack(rows_front), half_pack(rows_front), wide(batch, feat), wide(batch, rank)]
        + [wide(2, tab_grp, batch, width)] * n_z,
        held_like(sources)
        + [
            pltpu.VMEM((2, batch, hid // 2), bf16),
            pltpu.VMEM((2, batch, hid // 4), bf16),
            pack_scratch(rows_front),
            pltpu.VMEM((n_z, 2, tab_grp, batch, width), bf16),
            pltpu.SemaphoreType.DMA((len(sources),)),
        ],
        [smem] + [hbm] * len(sources) + [vmem] * 4,
        "middle",
        8,
    )(pos, *sources, act_t, delta_second, crossed_t, delta_first)
    keep_low, keep_high, delta_widened, delta_reduced = outs[:4]
    pooled_out = outs[4:]

    low_first = tuple(range(row_bits))
    high_first = low_first[::-1]

    class Halving:
        def __init__(self, terms, order):
            self.terms = [term.reshape((2,) * row_bits + term.shape[1:]) for term in terms]
            self.order, self.left = order, list(range(row_bits - 1, -1, -1))
            self.sent = []

        def step(self, at):
            bit = self.order[at]
            axis = self.left.index(bit)
            self.left.remove(bit)
            far = [lax.index_in_dim(term, 1, axis, keepdims=False) for term in self.terms]
            sent = add_terms(far).astype(bf16)
            self.sent.append(sent)
            got = swap_row(sent, bit)
            near = [lax.index_in_dim(term, 0, axis, keepdims=False) for term in self.terms]
            self.terms = near + [got]
            return sent

    def sum_z(lower, upper):
        sents = [add_terms(upper).astype(bf16)]
        terms = lower + [swap_z(sents[0], 1)]
        for stage in range(1, z_bits):
            middle = n_z >> (stage + 1)
            sents.append(add_terms([term[middle:] for term in terms]).astype(bf16))
            terms = [term[:middle] for term in terms] + [swap_z(sents[-1], 1 << stage)]
        own = add_terms(terms).astype(bf16)
        for stage in range(z_bits - 1, 0, -1):
            own = jnp.concatenate([own, swap_z(own, 1 << stage)], axis=0)
        far = swap_z(own, 1)
        return sents, [own, far, swap_cores(own), swap_cores(far)]

    low1, high1 = Halving([keep_low, got_low], low_first), Halving([keep_high, got_high], high_first)
    ties = [low1.step(0), high1.step(0)]

    values = [pooled_out[0]] + [swap_z(pooled_out[which], which) for which in range(1, n_z)]

    send_low2, send_high2, keep_low2, keep_high2 = call(
        back_kernel,
        [half_pack(rows_back)] * 4,
        [
            pltpu.VMEM((2, batch, rank // 2), bf16),
            pltpu.VMEM((2, batch, hid // 4), bf16),
            pack_scratch(rows_back),
            pltpu.VMEM((48, LANES), f32),
        ],
        [smem] + [vmem] * 8 + [anywhere] * 2,
        "back",
        6,
    )(
        pos,
        dense_feat,
        pooled,
        cross_down,
        crossed_t,
        delta_first,
        delta_widened,
        delta_reduced,
        small,
        *ties,
    )
    got_low2, got_high2 = swap_cores(send_low2), swap_cores(send_high2)
    low2 = Halving([keep_low2, got_low2], low_first)
    high2 = Halving([keep_high2, got_high2], high_first)
    ties = [low2.step(0), high2.step(0)]
    for at in range(1, row_bits):
        ties += [low1.step(at), high1.step(at)]

    far_values = call(
        functools.partial(select_kernel, n_z),
        [wide(n_z, tab_grp, batch, width)],
        [],
        [vmem] * n_z + [anywhere] * len(ties),
        "select",
        1,
    )(*values, *ties)[0]
    values.append(swap_cores(far_values))

    for at in range(1, row_bits):
        low2.step(at), high2.step(at)
    sents1, stream1 = sum_z(low1.terms, high1.terms)
    sents2, stream2 = sum_z(low2.terms, high2.terms)

    slots = jnp.transpose(lookup_slots, (0, 2, 1))
    shares = []
    for table in range(tab_grp):
        sums = pl.pallas_call(
            functools.partial(count_kernel, n_row, table, hot, n_z),
            out_shape=wide(n_row, u_shard, width),
            grid=(n_row,),
            in_specs=[smem] + [vmem] * (2 + n_z) + [anywhere],
            out_specs=pl.BlockSpec((1, u_shard, width), lambda at: (at, 0, 0)),
            compiler_params=pltpu.CompilerParams(vmem_limit_bytes=VMEM_BYTES),
            cost_estimate=cost(6),
            name="counts",
        )(pos, slots, *values, sents1[min(table, len(sents1) - 1)])
        share = Halving([sums], high_first if table % 2 else low_first)
        for at in range(row_bits):
            share.step(at)
        shares.append(add_terms(share.terms))
    row_grads = jnp.stack(shares)

    g_down, g_up, g_first, g_second, g_small = call(
        unpack_kernel,
        [
            jax.ShapeDtypeStruct((feat // n_row, rank), f32),
            jax.ShapeDtypeStruct((rank // n_row, feat), f32),
            jax.ShapeDtypeStruct((feat // n_row, hid), f32),
            jax.ShapeDtypeStruct((hid // n_row, hid), f32),
            jax.ShapeDtypeStruct((48, LANES), f32),
        ],
        [pltpu.VMEM((2, rows, LANES), bf16) for rows in (rows_front, rows_back)],
        [smem] + [vmem] * 8,
        "unpack",
        4,
    )(pos, *stream1, *stream2)

    flat = g_small.reshape(-1)

    def part(start, length):
        share = length // n_row
        return lax.dynamic_slice(flat, (start * LANES + row_pos * share,), (share,))

    return (
        row_grads,
        g_down,
        g_up,
        part(24, feat),
        g_first,
        part(0, hid),
        g_second,
        part(8, hid),
        part(16, hid),
    )


def solution(mesh):
    in_specs = (
        P(("table", "row"), None),
        P(("table", "row"), None),
        P(("table", "row")),
        P(),
        P(),
        P(),
        P(),
        P(),
        P(),
        P(),
        P(),
        P("table", None, None),
    )
    out_specs = (
        P("table", "row", None),
        P("row", None),
        P("row", None),
        P("row"),
        P("row", None),
        P("row"),
        P("row", None),
        P("row"),
        P("row"),
    )
    return jax.shard_map(local, mesh=mesh, in_specs=in_specs, out_specs=out_specs, check_vma=False)
```

```python
import functools

import jax
import jax.numpy as jnp
from jax import lax
from jax.experimental import pallas as pl
from jax.experimental.pallas import tpu as pltpu
from jax.sharding import PartitionSpec as P

loss_scale = 16.0
LANES = 128
SPAN = 9 * LANES
MIB = 1024 * 1024
bf16 = jnp.bfloat16
f32 = jnp.float32


def round_up(value, unit):
    return -(-value // unit) * unit


def matmul(left, right):
    return jnp.dot(left, right, preferred_element_type=f32)


def matmul_rt(left, right):
    return lax.dot_general(left, right, (((1,), (1,)), ((), ())), preferred_element_type=f32)


def reverse_bits(value, bits):
    out = 0
    for bit in range(bits):
        out = out | (((value >> bit) & 1) << (bits - 1 - bit))
    return out


def places_of(z_pos, n_z):
    bits = n_z.bit_length() - 1
    return [reverse_bits(z_pos ^ quarter, bits) for quarter in range(n_z)]


def put_blocks(ref, row_pos, places, offset, value):
    shards, rows_q = ref.shape[0], ref.shape[2]
    rows = value.shape[0] // shards
    step = round_up(rows, 16)
    blocks = value.shape[1] // LANES
    for shard in range(shards):
        slot = shard ^ row_pos
        for block in range(blocks):
            done = 0
            while done < rows:
                quarter, at = divmod(offset + block * step + done, rows_q)
                length = min(rows - done, rows_q - at)
                ref[slot, places[quarter], at : at + length, :] = value[
                    shard * rows + done : shard * rows + done + length,
                    block * LANES : (block + 1) * LANES,
                ].astype(ref.dtype)
                done += length
    return offset + blocks * step


def put_rows(ref, offset, value):
    for block in range(value.shape[1] // LANES):
        ref[offset + block : offset + block + 1, :] = value[:, block * LANES : (block + 1) * LANES]


def split_parts(pack, low, high):
    half = low.shape[1]
    low[...] = pack[:, :half]
    high[...] = pack[:, half:]


class Loads:
    def __init__(self, sources, targets, sems):
        self.copies = [
            pltpu.make_async_copy(source, target, sems.at[at])
            for at, (source, target) in enumerate(zip(sources, targets))
        ]
        self.targets = targets
        self.ready = set()
        for copy in self.copies:
            copy.start()

    def __call__(self, at):
        if at not in self.ready:
            self.copies[at].wait()
            self.ready.add(at)
        return self.targets[at][...]


def as_row(value):
    return value.reshape(1, value.shape[-1])


def front_kernel(pos, *refs):
    sources, outs, targets = refs[:11], refs[11:18], refs[18:29]
    halves, thirds, pack, sems = refs[29:]
    send_low, send_high, keep_low, keep_high, crossed_t_out, first_out, small = outs
    load = Loads(sources, targets, sems)
    core, row_pos = pos[0], pos[1]
    places = places_of(pos[2] // 2, pack.shape[1])
    stacked = jnp.concatenate([load(0), load(1)], axis=1)
    reduced = matmul(stacked, load(2)).astype(bf16)
    widened = matmul(reduced, load(3)) + as_row(load(4))
    wide = stacked.astype(f32)
    crossed = (wide * widened + wide).astype(bf16)
    pre_first = matmul(crossed, load(5)) + as_row(load(6))
    sig_first = jax.nn.sigmoid(pre_first)
    act_first = (pre_first * sig_first).astype(bf16)
    slope_first = sig_first * (1.0 + pre_first * (1.0 - sig_first))
    w_hidden2 = load(7)
    pre_second = matmul(act_first, w_hidden2) + as_row(load(8))
    sig_second = jax.nn.sigmoid(pre_second)
    act_second = (pre_second * sig_second).astype(bf16).astype(f32)
    slope_second = sig_second * (1.0 + pre_second * (1.0 - sig_second))
    w_logit = as_row(load(9))
    logits = jnp.sum(act_second * w_logit, axis=1, keepdims=True)
    labels = as_row(load(10))
    count = labels.shape[1]
    same = lax.broadcasted_iota(jnp.int32, (count, count), 0) == lax.broadcasted_iota(
        jnp.int32, (count, count), 1
    )
    label_col = jnp.sum(jnp.where(same, labels.astype(f32), 0.0), axis=1, keepdims=True)
    delta_logit = loss_scale * (jax.nn.sigmoid(logits) - label_col)
    delta_second = (delta_logit * w_logit * slope_second).astype(bf16)
    put_rows(small, 16, jnp.sum(act_second * delta_logit, axis=0, keepdims=True))
    put_rows(small, 8, jnp.sum(delta_second.astype(f32), axis=0, keepdims=True))
    half = halves.shape[2]
    halves[0] = delta_second[:, :half]
    halves[1] = delta_second[:, half:]
    delta_first = (matmul_rt(delta_second, w_hidden2) * slope_first).astype(bf16)
    first_out[...] = delta_first
    put_rows(small, 0, jnp.sum(delta_first.astype(f32), axis=0, keepdims=True))
    part = thirds.shape[2]
    thirds[0] = delta_first[:, :part]
    thirds[1] = delta_first[:, half : half + part]
    act_t = act_first.T
    crossed_t = crossed.T
    crossed_t_out[...] = crossed_t
    for low, high, who in ((send_low, send_high, 1 - core), (keep_low, keep_high, core)):
        offset = put_blocks(pack, row_pos, places, 0, matmul(act_t, halves[who]))
        put_blocks(pack, row_pos, places, offset, matmul(crossed_t, thirds[who]))
        split_parts(pack, low, high)


def middle_kernel(n_z, pos, *refs):
    sources, delta_first = refs[:6], refs[6]
    widened_out, reduced_out = refs[7:9]
    pooled_outs = refs[9 : 9 + n_z]
    rest = refs[9 + n_z :]
    targets = rest[:6]
    by_group, sems = rest[6:]
    load = Loads(sources, targets, sems)
    core, z_pos = pos[0], pos[2] // 2
    stacked = jnp.concatenate([load(0), load(1)], axis=1)
    cross_down, cross_up = load(2), load(3)
    reduced = matmul(stacked, cross_down).astype(bf16)
    widened = matmul(reduced, cross_up) + as_row(load(4))
    delta_crossed = matmul_rt(delta_first[...], load(5))
    delta_widened = (delta_crossed * stacked.astype(f32)).astype(bf16)
    widened_out[...] = delta_widened
    delta_reduced = matmul_rt(delta_widened, cross_up).astype(bf16)
    reduced_out[...] = delta_reduced
    delta_stacked = delta_crossed * (widened + 1.0) + matmul_rt(delta_reduced, cross_down)
    width = targets[0].shape[1]
    per_group = by_group.shape[2]
    for table in range(2 * n_z * per_group):
        group = table // per_group
        by_group[group // 2, group % 2, table % per_group] = delta_stacked[
            :, width * (table + 1) : width * (table + 2)
        ].astype(bf16)
    for which in range(n_z):
        pooled_outs[which][0] = by_group[z_pos ^ which, core]
        pooled_outs[which][1] = by_group[z_pos ^ which, 1 - core]


def back_kernel(pos, *refs):
    dense_feat, pooled, cross_down, crossed_t, delta_first, delta_widened, delta_reduced = refs[:7]
    small_in = refs[7]
    send_low, send_high, keep_low, keep_high = refs[10:14]
    half_delta, sixths, pack, small = refs[14:]
    core, row_pos = pos[0], pos[1]
    n_row = pack.shape[0]
    places = places_of(pos[2] // 2, pack.shape[1])
    rank = delta_reduced.shape[1]
    feat = delta_widened.shape[1]
    hid = delta_first.shape[1]
    part = hid // 2 - sixths.shape[2]
    half_delta[0] = delta_reduced[:, : rank // 2]
    half_delta[1] = delta_reduced[:, rank // 2 :]
    sixths[0] = delta_first[:, part : hid // 2]
    sixths[1] = delta_first[:, hid // 2 + part :]
    put_rows(small, 24, jnp.sum(delta_widened[...].astype(f32), axis=0, keepdims=True))
    small[0:24, :] = small_in[...]
    small[41:48, :] = jnp.zeros((7, LANES), f32)
    sums = jnp.concatenate([small[...]] * n_row, axis=0)
    stacked = jnp.concatenate([dense_feat[...], pooled[...]], axis=1)
    reduced_t = matmul(stacked, cross_down[...]).astype(bf16).T
    stacked_t = stacked.T
    for low, high, who in ((send_low, send_high, 1 - core), (keep_low, keep_high, core)):
        offset = put_blocks(pack, row_pos, places, 0, matmul(crossed_t[...], sixths[who]))
        offset = put_blocks(pack, row_pos, places, offset, matmul(stacked_t, half_delta[who]))
        start = pl.multiple_of(who * (feat - SPAN), LANES)
        offset = put_blocks(
            pack, row_pos, places, offset, matmul(reduced_t, delta_widened[:, pl.ds(start, SPAN)])
        )
        offset = put_blocks(pack, row_pos, places, offset, sums)
        tail = pack.shape[1] * pack.shape[2] - offset
        if tail:
            put_blocks(pack, row_pos, places, offset, jnp.zeros((n_row * tail, LANES), f32))
        split_parts(pack, low, high)


def select_kernel(n_z, *refs):
    out = refs[-1]
    for which in range(n_z):
        out[which] = refs[which][1]


def count_kernel(n_row, table, hot, n_z, pos, slots, *rest):
    direct, crossed, out = rest[:n_z], rest[n_z], rest[-1]
    block = out.shape[1]
    samples = crossed.shape[2]
    core, row_pos, z_pos = pos[0], pos[1], pos[2] // 2
    base = (pl.program_id(0) ^ row_pos) * block
    names = lax.broadcasted_iota(jnp.int16, (block, samples), 0)
    total = jnp.zeros((block, out.shape[2]), f32)
    one = jnp.ones((block, samples), bf16)
    zero = jnp.zeros((block, samples), bf16)
    for which in range(n_z):
        for held, who in ((direct[which][0, table], core), (crossed[which, table], 1 - core)):
            source = 2 * (z_pos ^ which) + who
            start = pl.multiple_of((source * n_row + row_pos) * samples, LANES)
            lines = slots[table, :, pl.ds(start, samples)] - base
            lines = jnp.where((lines >= 0) & (lines < block), lines, block).astype(jnp.int16)
            counts = zero
            for look in range(hot):
                line = jnp.broadcast_to(lines[look : look + 1, :], (block, samples))
                counts = counts + jnp.where(line == names, one, zero)
            total = total + matmul(counts, held)
    out[0] = total.astype(out.dtype)


def unpack_kernel(pos, *refs):
    parts = refs[0:8]
    g_down, g_up, g_first, g_second, g_small = refs[8:13]
    held = refs[13:15]
    core = pos[0]
    z_pos = pos[2] // 2
    for stream in range(2):
        lower, upper, lower_other, upper_other = parts[4 * stream : 4 * stream + 4]
        ref = held[stream]
        rows = lower.shape[1]
        n_z = 2 * lower.shape[0]
        z_bits = n_z.bit_length() - 1
        for who, pieces in ((core, (lower, upper)), (1 - core, (lower_other, upper_other))):
            for place in range(n_z):
                start = pl.multiple_of((reverse_bits(place, z_bits) ^ z_pos) * rows, 16)
                ref[who, pl.ds(start, rows), :] = pieces[place // (n_z // 2)][place % (n_z // 2)]
    front, back = held

    def take(ref, out, half, offset, columns):
        rows = out.shape[0]
        step = round_up(rows, 16)
        for column in columns:
            out[:, column * LANES : (column + 1) * LANES] = ref[
                half, offset : offset + rows, :
            ].astype(f32)
            offset += step
        return offset

    for half in range(2):
        blocks = g_second.shape[1] // LANES // 2
        offset = take(front, g_second, half, 0, range(half * blocks, (half + 1) * blocks))
        blocks = g_first.shape[1] // LANES // 2
        early = blocks - blocks // 4
        take(front, g_first, half, offset, range(half * blocks, half * blocks + early))
        offset = take(back, g_first, half, 0, range(half * blocks + early, (half + 1) * blocks))
        blocks = g_down.shape[1] // LANES // 2
        offset = take(back, g_down, half, offset, range(half * blocks, (half + 1) * blocks))
        blocks = g_up.shape[1] // LANES
        offset = take(back, g_up, half, offset, range(half * (blocks - 9), half * (blocks - 9) + 9))
    g_small[...] = back[0, offset : offset + 48, :].astype(f32)


def whole(memory=pltpu.VMEM):
    return pl.BlockSpec(memory_space=memory)


def cost(micros):
    return pl.CostEstimate(
        flops=int(micros * 1.0e9), transcendentals=0, bytes_accessed=int(micros * 3.0e6)
    )


def call(body, outs, scratch, in_specs, name, micros, mib):
    return pl.pallas_call(
        body,
        out_shape=outs,
        in_specs=in_specs,
        out_specs=[whole()] * len(outs),
        scratch_shapes=scratch,
        compiler_params=pltpu.CompilerParams(vmem_limit_bytes=mib * MIB),
        cost_estimate=cost(micros),
        name=name,
    )


def after(values, deps):
    return list(lax.optimization_barrier(tuple(values) + tuple(deps))[: len(values)])


def held_like(values):
    return [pltpu.VMEM(value.shape, value.dtype) for value in values]


def add_terms(terms):
    total = terms[0].astype(f32)
    for term in terms[1:]:
        total = total + term.astype(f32)
    return total


def local(
    dense_feat,
    pooled,
    labels,
    cross_down,
    cross_up,
    cross_bias,
    w_hidden1,
    bias1,
    w_hidden2,
    bias2,
    w_logit,
    lookup_slots,
):
    n_table = lax.axis_size("table")
    n_row = lax.axis_size("row")
    n_z = n_table // 2
    row_bits = n_row.bit_length() - 1
    z_bits = n_z.bit_length() - 1
    table_pos = lax.axis_index("table")
    row_pos = lax.axis_index("row")
    pos = jnp.stack([table_pos % 2, row_pos, table_pos]).astype(jnp.int32)
    batch, width = dense_feat.shape
    feat, rank = cross_down.shape
    hid = w_hidden1.shape[1]
    tab_grp, _, hot = lookup_slots.shape
    u_shard = batch * n_table * hot // 16

    def swap_cores(value):
        return lax.ppermute(value, "table", [(at, at ^ 1) for at in range(n_table)])

    def swap_z(value, which):
        return lax.ppermute(value, "table", [(at, at ^ (2 * which)) for at in range(n_table)])

    def swap_row(value, bit):
        return lax.ppermute(value, "row", [(at, at ^ (1 << bit)) for at in range(n_row)])

    late = hid // 8
    early = hid // 2 - late
    rows_front = (hid // 2 // LANES) * round_up(hid // n_row, 16)
    rows_front += (early // LANES) * round_up(feat // n_row, 16)
    rows_back = (late // LANES) * round_up(feat // n_row, 16)
    rows_back += (rank // 2 // LANES) * round_up(feat // n_row, 16)
    rows_back += 9 * round_up(rank // n_row, 16) + 48
    rows_front, rows_back = (round_up(rows, 16 * n_z) for rows in (rows_front, rows_back))

    def half_pack(rows):
        return jax.ShapeDtypeStruct((n_row, n_z // 2, rows // n_z, LANES), bf16)

    def pack_scratch(rows):
        return pltpu.VMEM((n_row, n_z, rows // n_z, LANES), bf16)

    def wide(*shape):
        return jax.ShapeDtypeStruct(shape, bf16)

    smem, hbm, vmem, anywhere = whole(pltpu.SMEM), whole(pltpu.HBM), whole(), whole(pl.ANY)

    sources = (
        dense_feat,
        pooled,
        cross_down,
        cross_up,
        cross_bias,
        w_hidden1,
        bias1,
        w_hidden2,
        bias2,
        w_logit,
        labels,
    )
    send_low, send_high, keep_low, keep_high, crossed_t, delta_first, small = call(
        front_kernel,
        [half_pack(rows_front)] * 4
        + [wide(feat, batch), wide(batch, hid), jax.ShapeDtypeStruct((24, LANES), f32)],
        held_like(sources)
        + [
            pltpu.VMEM((2, batch, hid // 2), bf16),
            pltpu.VMEM((2, batch, early), bf16),
            pack_scratch(rows_front),
            pltpu.SemaphoreType.DMA((len(sources),)),
        ],
        [smem] + [hbm] * len(sources),
        "front",
        10,
        60,
    )(pos, *sources)
    got_low, got_high = swap_cores(send_low), swap_cores(send_high)

    sources = (dense_feat, pooled, cross_down, cross_up, cross_bias, w_hidden1)
    outs = call(
        functools.partial(middle_kernel, n_z),
        [wide(batch, feat), wide(batch, rank)] + [wide(2, tab_grp, batch, width)] * n_z,
        held_like(sources)
        + [
            pltpu.VMEM((n_z, 2, tab_grp, batch, width), bf16),
            pltpu.SemaphoreType.DMA((len(sources),)),
        ],
        [smem] + [hbm] * len(sources) + [vmem],
        "middle",
        7,
        40,
    )(pos, *sources, delta_first)
    delta_widened, delta_reduced = outs[:2]
    pooled_out = outs[2:]

    low_first = tuple(range(row_bits))
    high_first = low_first[::-1]

    class Terms:
        def __init__(self, arrays):
            self.items = [(array, ()) for array in arrays]

        def tie(self, deps):
            arrays = after([array for array, _ in self.items], deps)
            self.items = [(array, path) for array, (_, path) in zip(arrays, self.items)]

        def total(self, *extra):
            parts = []
            for array, path in self.items:
                for pick in path + extra:
                    array = pick(array)
                parts.append(array)
            return add_terms(parts)

        def narrow(self, pick, got):
            self.items = [(array, path + (pick,)) for array, path in self.items] + [(got, ())]

    def index_of(index, axis):
        return lambda array: lax.index_in_dim(array, index, axis, keepdims=False)

    def rows_of(start, stop):
        return lambda array: array[start:stop]

    class Halving(Terms):
        def __init__(self, arrays, order):
            super().__init__([array.reshape((2,) * row_bits + array.shape[1:]) for array in arrays])
            self.order, self.left = order, list(range(row_bits - 1, -1, -1))

        def step(self, at, deps=()):
            bit = self.order[at]
            axis = self.left.index(bit)
            self.left.remove(bit)
            if deps:
                self.tie(deps)
            sent = self.total(index_of(1, axis)).astype(bf16)
            self.narrow(index_of(0, axis), swap_row(sent, bit))
            return sent

    class Dense:
        def __init__(self, keep_low, got_low, keep_high, got_high):
            self.low = Halving([keep_low, got_low], low_first)
            self.high = Halving([keep_high, got_high], high_first)

        def row_step(self, at, deps=()):
            sent = self.low.step(at, deps)
            return [sent, self.high.step(at, deps)]

        def z_step(self, stage, deps):
            if stage == 0:
                self.high.tie(deps)
                sent = self.high.total().astype(bf16)
                self.low.items.append((swap_z(sent, 1), ()))
            else:
                middle = n_z >> (stage + 1)
                self.low.tie(deps)
                sent = self.low.total(rows_of(middle, None)).astype(bf16)
                self.low.narrow(rows_of(0, middle), swap_z(sent, 1 << stage))
            return [sent]

        def z_back(self, deps):
            self.low.tie(deps)
            own = self.low.total().astype(bf16)
            first = own
            for stage in range(z_bits - 1, 0, -1):
                own = jnp.concatenate([own, swap_z(own, 1 << stage)], axis=0)
            far = swap_z(own, 1)
            self.pieces = [own, far, swap_cores(own), swap_cores(far)]
            return [first]

    one = Dense(keep_low, got_low, keep_high, got_high)
    sent = one.row_step(0)

    values = [pooled_out[0]] + [swap_z(pooled_out[which], which) for which in range(1, n_z)]

    send_low, send_high, keep_low, keep_high = call(
        back_kernel,
        [half_pack(rows_back)] * 4,
        [
            pltpu.VMEM((2, batch, rank // 2), bf16),
            pltpu.VMEM((2, batch, late), bf16),
            pack_scratch(rows_back),
            pltpu.VMEM((48, LANES), f32),
        ],
        [smem] + [vmem] * 8 + [anywhere] * 2,
        "back",
        6,
        36,
    )(
        pos,
        dense_feat,
        pooled,
        cross_down,
        crossed_t,
        delta_first,
        delta_widened,
        delta_reduced,
        small,
        *sent,
    )
    two = Dense(keep_low, swap_cores(send_low), keep_high, swap_cores(send_high))
    last = [send_low]
    for at in range(1, row_bits):
        last = one.row_step(at, last)

    far_values = call(
        functools.partial(select_kernel, n_z),
        [wide(n_z, tab_grp, batch, width)],
        [],
        [vmem] * n_z + [anywhere] * len(last),
        "select",
        1,
        8,
    )(*values, *last)[0]
    values.append(swap_cores(far_values))
    last = two.row_step(0, [far_values])
    last = one.z_step(0, last)

    slots = jnp.transpose(lookup_slots, (0, 2, 1))
    shares = []
    for table in range(tab_grp):
        sums = pl.pallas_call(
            functools.partial(count_kernel, n_row, table, hot, n_z),
            out_shape=wide(n_row, u_shard, width),
            grid=(n_row,),
            in_specs=[smem] + [vmem] * (2 + n_z) + [anywhere],
            out_specs=pl.BlockSpec((1, u_shard, width), lambda at: (at, 0, 0)),
            compiler_params=pltpu.CompilerParams(vmem_limit_bytes=16 * MIB),
            cost_estimate=cost(6),
            name="counts",
        )(pos, slots, *values, last[0])
        last = [sums]
        shares.append(Halving([sums], high_first if table % 2 else low_first))
        if table == 0:
            for stage in range(1, z_bits):
                last = one.z_step(stage, last)
            for at in range(1, row_bits):
                last = two.row_step(at, last)
    for share in shares:
        share.step(0, last)
    last = one.z_back(last)
    last = two.z_step(0, last)
    for share in shares:
        for at in range(1, row_bits):
            share.step(at, last)
    row_grads = jnp.stack([share.total() for share in shares])
    for stage in range(1, z_bits):
        last = two.z_step(stage, last)
    two.z_back(last)

    g_down, g_up, g_first, g_second, g_small = call(
        unpack_kernel,
        [
            jax.ShapeDtypeStruct((feat // n_row, rank), f32),
            jax.ShapeDtypeStruct((rank // n_row, feat), f32),
            jax.ShapeDtypeStruct((feat // n_row, hid), f32),
            jax.ShapeDtypeStruct((hid // n_row, hid), f32),
            jax.ShapeDtypeStruct((48, LANES), f32),
        ],
        [pltpu.VMEM((2, rows, LANES), bf16) for rows in (rows_front, rows_back)],
        [smem] + [vmem] * 8,
        "unpack",
        4,
        24,
    )(pos, *one.pieces, *two.pieces)

    flat = g_small.reshape(-1)

    def part(start, length):
        share = length // n_row
        return lax.dynamic_slice(flat, (start * LANES + row_pos * share,), (share,))

    return (
        row_grads,
        g_down,
        g_up,
        part(24, feat),
        g_first,
        part(0, hid),
        g_second,
        part(8, hid),
        part(16, hid),
    )


def solution(mesh):
    in_specs = (
        P(("table", "row"), None),
        P(("table", "row"), None),
        P(("table", "row")),
        P(),
        P(),
        P(),
        P(),
        P(),
        P(),
        P(),
        P(),
        P("table", None, None),
    )
    out_specs = (
        P("table", "row", None),
        P("row", None),
        P("row", None),
        P("row"),
        P("row", None),
        P("row"),
        P("row", None),
        P("row"),
        P("row"),
    )
    return jax.shard_map(local, mesh=mesh, in_specs=in_specs, out_specs=out_specs, check_vma=False)
```

```python
import functools

import jax
import jax.numpy as jnp
from jax import lax
from jax.experimental import pallas as pl
from jax.experimental.pallas import tpu as pltpu
from jax.sharding import PartitionSpec as P

loss_scale = 16.0
LANES = 128
SPAN = 9 * LANES
MIB = 1024 * 1024
bf16 = jnp.bfloat16
f32 = jnp.float32


def round_up(value, unit):
    return -(-value // unit) * unit


def matmul(left, right):
    return jnp.dot(left, right, preferred_element_type=f32)


def matmul_rt(left, right):
    return lax.dot_general(left, right, (((1,), (1,)), ((), ())), preferred_element_type=f32)


def reverse_bits(value, bits):
    out = 0
    for bit in range(bits):
        out = out | (((value >> bit) & 1) << (bits - 1 - bit))
    return out


def places_of(z_pos, n_z):
    bits = n_z.bit_length() - 1
    return [reverse_bits(z_pos ^ quarter, bits) for quarter in range(n_z)]


def put_blocks(ref, row_pos, places, offset, value):
    shards, n_half, rows_q = ref.shape[1], ref.shape[2], ref.shape[3]
    rows = value.shape[0] // shards
    step = round_up(rows, 16)
    blocks = value.shape[1] // LANES
    for shard in range(shards):
        slot = shard ^ row_pos
        for block in range(blocks):
            done = 0
            while done < rows:
                quarter, at = divmod(offset + block * step + done, rows_q)
                length = min(rows - done, rows_q - at)
                place = places[quarter]
                ref[lax.div(place, n_half), slot, lax.rem(place, n_half), at : at + length, :] = value[
                    shard * rows + done : shard * rows + done + length,
                    block * LANES : (block + 1) * LANES,
                ].astype(ref.dtype)
                done += length
    return offset + blocks * step


def put_rows(ref, offset, value):
    for block in range(value.shape[1] // LANES):
        ref[offset + block : offset + block + 1, :] = value[:, block * LANES : (block + 1) * LANES]


def position():
    table_pos = lax.axis_index("table")
    return lax.rem(table_pos, 2), lax.axis_index("row"), table_pos


class Loads:
    def __init__(self, sources, targets, sems):
        self.copies = [
            pltpu.make_async_copy(source, target, sems.at[at])
            for at, (source, target) in enumerate(zip(sources, targets))
        ]
        self.targets = targets
        self.ready = set()
        for copy in self.copies:
            copy.start()

    def __call__(self, at):
        if at not in self.ready:
            self.copies[at].wait()
            self.ready.add(at)
        return self.targets[at][...]


def as_row(value):
    return value.reshape(1, value.shape[-1])


def front_kernel(*refs):
    sources, outs, targets = refs[:11], refs[11:16], refs[16:27]
    halves, thirds, sems = refs[27:]
    send, keep, crossed_t_out, first_out, small = outs
    load = Loads(sources, targets, sems)
    core, row_pos, table_pos = position()
    places = places_of(lax.div(table_pos, 2), 2 * send.shape[2])
    stacked = jnp.concatenate([load(0), load(1)], axis=1)
    reduced = matmul(stacked, load(2)).astype(bf16)
    widened = matmul(reduced, load(3)) + as_row(load(4))
    wide = stacked.astype(f32)
    crossed = (wide * widened + wide).astype(bf16)
    pre_first = matmul(crossed, load(5)) + as_row(load(6))
    sig_first = jax.nn.sigmoid(pre_first)
    act_first = (pre_first * sig_first).astype(bf16)
    slope_first = sig_first * (1.0 + pre_first * (1.0 - sig_first))
    w_hidden2 = load(7)
    pre_second = matmul(act_first, w_hidden2) + as_row(load(8))
    sig_second = jax.nn.sigmoid(pre_second)
    act_second = (pre_second * sig_second).astype(bf16).astype(f32)
    slope_second = sig_second * (1.0 + pre_second * (1.0 - sig_second))
    w_logit = as_row(load(9))
    logits = jnp.sum(act_second * w_logit, axis=1, keepdims=True)
    labels = as_row(load(10))
    count = labels.shape[1]
    same = lax.broadcasted_iota(jnp.int32, (count, count), 0) == lax.broadcasted_iota(
        jnp.int32, (count, count), 1
    )
    label_col = jnp.sum(jnp.where(same, labels.astype(f32), 0.0), axis=1, keepdims=True)
    delta_logit = loss_scale * (jax.nn.sigmoid(logits) - label_col)
    delta_second = (delta_logit * w_logit * slope_second).astype(bf16)
    put_rows(small, 16, jnp.sum(act_second * delta_logit, axis=0, keepdims=True))
    put_rows(small, 8, jnp.sum(delta_second.astype(f32), axis=0, keepdims=True))
    half = halves.shape[2]
    halves[0] = delta_second[:, :half]
    halves[1] = delta_second[:, half:]
    delta_first = (matmul_rt(delta_second, w_hidden2) * slope_first).astype(bf16)
    first_out[...] = delta_first
    put_rows(small, 0, jnp.sum(delta_first.astype(f32), axis=0, keepdims=True))
    part = thirds.shape[2]
    thirds[0] = delta_first[:, :part]
    thirds[1] = delta_first[:, half : half + part]
    act_t = act_first.T
    crossed_t = crossed.T
    crossed_t_out[...] = crossed_t
    for ref, who in ((send, 1 - core), (keep, core)):
        offset = put_blocks(ref, row_pos, places, 0, matmul(act_t, halves[who]))
        put_blocks(ref, row_pos, places, offset, matmul(crossed_t, thirds[who]))


def middle_kernel(n_z, *refs):
    sources, delta_first = refs[:6], refs[6]
    widened_out, reduced_out = refs[7:9]
    pooled_outs = refs[9 : 9 + n_z]
    rest = refs[9 + n_z :]
    targets = rest[:6]
    by_group, sems = rest[6:]
    load = Loads(sources, targets, sems)
    core, _, table_pos = position()
    z_pos = lax.div(table_pos, 2)
    stacked = jnp.concatenate([load(0), load(1)], axis=1)
    cross_down, cross_up = load(2), load(3)
    reduced = matmul(stacked, cross_down).astype(bf16)
    widened = matmul(reduced, cross_up) + as_row(load(4))
    delta_crossed = matmul_rt(delta_first[...], load(5))
    delta_widened = (delta_crossed * stacked.astype(f32)).astype(bf16)
    widened_out[...] = delta_widened
    delta_reduced = matmul_rt(delta_widened, cross_up).astype(bf16)
    reduced_out[...] = delta_reduced
    delta_stacked = delta_crossed * (widened + 1.0) + matmul_rt(delta_reduced, cross_down)
    width = targets[0].shape[1]
    per_group = by_group.shape[2]
    for table in range(2 * n_z * per_group):
        group = table // per_group
        by_group[group // 2, group % 2, table % per_group] = delta_stacked[
            :, width * (table + 1) : width * (table + 2)
        ].astype(bf16)
    for which in range(n_z):
        pooled_outs[which][0] = by_group[z_pos ^ which, core]
        pooled_outs[which][1] = by_group[z_pos ^ which, 1 - core]


def back_kernel(*refs):
    dense_feat, pooled, cross_down, crossed_t, delta_first, delta_widened, delta_reduced = refs[:7]
    small_in = refs[7]
    send, keep = refs[10:12]
    half_delta, sixths, small = refs[12:]
    core, row_pos, table_pos = position()
    n_row = send.shape[1]
    places = places_of(lax.div(table_pos, 2), 2 * send.shape[2])
    rank = delta_reduced.shape[1]
    feat = delta_widened.shape[1]
    hid = delta_first.shape[1]
    part = hid // 2 - sixths.shape[2]
    half_delta[0] = delta_reduced[:, : rank // 2]
    half_delta[1] = delta_reduced[:, rank // 2 :]
    sixths[0] = delta_first[:, part : hid // 2]
    sixths[1] = delta_first[:, hid // 2 + part :]
    put_rows(small, 24, jnp.sum(delta_widened[...].astype(f32), axis=0, keepdims=True))
    small[0:24, :] = small_in[...]
    small[41:48, :] = jnp.zeros((7, LANES), f32)
    sums = jnp.concatenate([small[...]] * n_row, axis=0)
    stacked = jnp.concatenate([dense_feat[...], pooled[...]], axis=1)
    reduced_t = matmul(stacked, cross_down[...]).astype(bf16).T
    stacked_t = stacked.T
    for ref, who in ((send, 1 - core), (keep, core)):
        offset = put_blocks(ref, row_pos, places, 0, matmul(crossed_t[...], sixths[who]))
        offset = put_blocks(ref, row_pos, places, offset, matmul(stacked_t, half_delta[who]))
        start = pl.multiple_of(who * (feat - SPAN), LANES)
        offset = put_blocks(
            ref, row_pos, places, offset, matmul(reduced_t, delta_widened[:, pl.ds(start, SPAN)])
        )
        offset = put_blocks(ref, row_pos, places, offset, sums)
        tail = 2 * ref.shape[2] * ref.shape[3] - offset
        if tail:
            put_blocks(ref, row_pos, places, offset, jnp.zeros((n_row * tail, LANES), f32))


def select_kernel(n_z, *refs):
    out = refs[-1]
    for which in range(n_z):
        out[which] = refs[which][1]


def count_kernel(n_row, table, hot, n_z, slots, *rest):
    direct, crossed, out = rest[:n_z], rest[n_z], rest[-1]
    block = out.shape[1]
    samples = crossed.shape[2]
    core, row_pos, table_pos = position()
    z_pos = lax.div(table_pos, 2)
    base = (pl.program_id(0) ^ row_pos) * block
    names = lax.broadcasted_iota(jnp.int16, (block, samples), 0)
    total = jnp.zeros((block, out.shape[2]), f32)
    one = jnp.ones((block, samples), bf16)
    zero = jnp.zeros((block, samples), bf16)
    for which in range(n_z):
        for held, who in ((direct[which][0, table], core), (crossed[which, table], 1 - core)):
            source = 2 * (z_pos ^ which) + who
            start = pl.multiple_of((source * n_row + row_pos) * samples, LANES)
            lines = slots[table, :, pl.ds(start, samples)] - base
            lines = jnp.where((lines >= 0) & (lines < block), lines, block).astype(jnp.int16)
            counts = zero
            for look in range(hot):
                line = jnp.broadcast_to(lines[look : look + 1, :], (block, samples))
                counts = counts + jnp.where(line == names, one, zero)
            total = total + matmul(counts, held)
    out[0] = total.astype(out.dtype)


def unpack_kernel(*refs):
    parts = refs[0:8]
    g_down, g_up, g_first, g_second = refs[8:12]
    small_outs = refs[12:16]
    held, small = refs[16:18], refs[18]
    core, row_pos, table_pos = position()
    z_pos = lax.div(table_pos, 2)
    for stream in range(2):
        lower, upper, lower_other, upper_other = parts[4 * stream : 4 * stream + 4]
        ref = held[stream]
        rows = lower.shape[1]
        n_z = 2 * lower.shape[0]
        z_bits = n_z.bit_length() - 1
        for who, pieces in ((core, (lower, upper)), (1 - core, (lower_other, upper_other))):
            for place in range(n_z):
                start = pl.multiple_of((reverse_bits(place, z_bits) ^ z_pos) * rows, 16)
                ref[who, pl.ds(start, rows), :] = pieces[place // (n_z // 2)][place % (n_z // 2)]
    front, back = held

    def take(ref, out, half, offset, columns):
        rows = out.shape[0]
        step = round_up(rows, 16)
        for column in columns:
            out[:, column * LANES : (column + 1) * LANES] = ref[
                half, offset : offset + rows, :
            ].astype(f32)
            offset += step
        return offset

    for half in range(2):
        blocks = g_second.shape[1] // LANES // 2
        offset = take(front, g_second, half, 0, range(half * blocks, (half + 1) * blocks))
        blocks = g_first.shape[1] // LANES // 2
        early = blocks - blocks // 4
        take(front, g_first, half, offset, range(half * blocks, half * blocks + early))
        offset = take(back, g_first, half, 0, range(half * blocks + early, (half + 1) * blocks))
        blocks = g_down.shape[1] // LANES // 2
        offset = take(back, g_down, half, offset, range(half * blocks, (half + 1) * blocks))
        blocks = g_up.shape[1] // LANES
        offset = take(back, g_up, half, offset, range(half * (blocks - 9), half * (blocks - 9) + 9))
    small[0:48, :] = back[0, offset : offset + 48, :].astype(f32)
    small[48:, :] = jnp.zeros((small.shape[0] - 48, LANES), f32)
    for out, first in zip(small_outs, (24, 0, 8, 16)):
        share = out.shape[0]
        begin = row_pos * share
        row, lane = lax.div(begin, LANES), lax.rem(begin, LANES)
        lanes = lax.broadcasted_iota(jnp.int32, (1, LANES), 1)
        for start in range(0, share, LANES):
            length = min(LANES, share - start)
            this = small[pl.ds(first + row + start // LANES, 1), :]
            later = small[pl.ds(first + row + start // LANES + 1, 1), :]
            both = jnp.where(lanes < lane, later, this)
            turned = pltpu.roll(both, lax.rem(LANES - lane, LANES), 1)
            out[start : start + length] = turned.reshape(LANES)[:length]


def whole(memory=pltpu.VMEM):
    return pl.BlockSpec(memory_space=memory)


def no_cost():
    return pl.CostEstimate(flops=0, transcendentals=0, bytes_accessed=0)


def call(body, outs, scratch, in_specs, name, mib):
    return pl.pallas_call(
        body,
        out_shape=outs,
        in_specs=in_specs,
        out_specs=[whole()] * len(outs),
        scratch_shapes=scratch,
        compiler_params=pltpu.CompilerParams(vmem_limit_bytes=mib * MIB),
        cost_estimate=no_cost(),
        name=name,
    )


def after(values, deps):
    return list(lax.optimization_barrier(tuple(values) + tuple(deps))[: len(values)])


def held_like(values):
    return [pltpu.VMEM(value.shape, value.dtype) for value in values]


def add_terms(terms):
    total = terms[0].astype(f32)
    for term in terms[1:]:
        total = total + term.astype(f32)
    return total


def local(
    dense_feat,
    pooled,
    labels,
    cross_down,
    cross_up,
    cross_bias,
    w_hidden1,
    bias1,
    w_hidden2,
    bias2,
    w_logit,
    lookup_slots,
):
    n_table = lax.axis_size("table")
    n_row = lax.axis_size("row")
    n_z = n_table // 2
    row_bits = n_row.bit_length() - 1
    z_bits = n_z.bit_length() - 1
    batch, width = dense_feat.shape
    feat, rank = cross_down.shape
    hid = w_hidden1.shape[1]
    tab_grp, _, hot = lookup_slots.shape
    u_shard = batch * n_table * hot // 16

    def swap_cores(value):
        return lax.ppermute(value, "table", [(at, at ^ 1) for at in range(n_table)])

    def swap_z(value, which):
        return lax.ppermute(value, "table", [(at, at ^ (2 * which)) for at in range(n_table)])

    def swap_row(value, bit):
        return lax.ppermute(value, "row", [(at, at ^ (1 << bit)) for at in range(n_row)])

    late = hid // 8
    early = hid // 2 - late
    rows_front = (hid // 2 // LANES) * round_up(hid // n_row, 16)
    rows_front += (early // LANES) * round_up(feat // n_row, 16)
    rows_back = (late // LANES) * round_up(feat // n_row, 16)
    rows_back += (rank // 2 // LANES) * round_up(feat // n_row, 16)
    rows_back += 9 * round_up(rank // n_row, 16) + 48
    rows_front, rows_back = (round_up(rows, 16 * n_z) for rows in (rows_front, rows_back))

    def packed(rows):
        return jax.ShapeDtypeStruct((2, n_row, n_z // 2, rows // n_z, LANES), bf16)

    def wide(*shape):
        return jax.ShapeDtypeStruct(shape, bf16)

    hbm, vmem, anywhere = whole(pltpu.HBM), whole(), whole(pl.ANY)

    sources = (
        dense_feat,
        pooled,
        cross_down,
        cross_up,
        cross_bias,
        w_hidden1,
        bias1,
        w_hidden2,
        bias2,
        w_logit,
        labels,
    )
    send, keep, crossed_t, delta_first, small = call(
        front_kernel,
        [packed(rows_front)] * 2
        + [wide(feat, batch), wide(batch, hid), jax.ShapeDtypeStruct((24, LANES), f32)],
        held_like(sources)
        + [
            pltpu.VMEM((2, batch, hid // 2), bf16),
            pltpu.VMEM((2, batch, early), bf16),
            pltpu.SemaphoreType.DMA((len(sources),)),
        ],
        [hbm] * len(sources),
        "front",
        60,
    )(*sources)
    got = swap_cores(send)

    sources = (dense_feat, pooled, cross_down, cross_up, cross_bias, w_hidden1)
    outs = call(
        functools.partial(middle_kernel, n_z),
        [wide(batch, feat), wide(batch, rank)] + [wide(2, tab_grp, batch, width)] * n_z,
        held_like(sources)
        + [
            pltpu.VMEM((n_z, 2, tab_grp, batch, width), bf16),
            pltpu.SemaphoreType.DMA((len(sources),)),
        ],
        [hbm] * len(sources) + [vmem],
        "middle",
        60,
    )(*sources, delta_first)
    delta_widened, delta_reduced = outs[:2]
    pooled_out = outs[2:]

    low_first = tuple(range(row_bits))
    high_first = low_first[::-1]

    class Terms:
        def __init__(self, arrays):
            self.items = [(array, ()) for array in arrays]

        def tie(self, deps):
            arrays = after([array for array, _ in self.items], deps)
            self.items = [(array, path) for array, (_, path) in zip(arrays, self.items)]

        def total(self, *extra):
            parts = []
            for array, path in self.items:
                for pick in path + extra:
                    array = pick(array)
                parts.append(array)
            return add_terms(parts)

        def narrow(self, pick, got):
            self.items = [(array, path + (pick,)) for array, path in self.items] + [(got, ())]

    def index_of(index, axis):
        return lambda array: lax.index_in_dim(array, index, axis, keepdims=False)

    def rows_of(start, stop):
        return lambda array: array[start:stop]

    class Halving(Terms):
        def __init__(self, arrays, order, half=None):
            dims = 0 if half is None else 1
            super().__init__(
                [
                    array.reshape(array.shape[:dims] + (2,) * row_bits + array.shape[dims + 1 :])
                    for array in arrays
                ]
            )
            if half is not None:
                self.items = [(array, (index_of(half, 0),)) for array, _ in self.items]
            self.order, self.left = order, list(range(row_bits - 1, -1, -1))

        def step(self, at, deps=()):
            bit = self.order[at]
            axis = self.left.index(bit)
            self.left.remove(bit)
            if deps:
                self.tie(deps)
            sent = self.total(index_of(1, axis)).astype(bf16)
            self.narrow(index_of(0, axis), swap_row(sent, bit))
            return sent

    class Dense:
        def __init__(self, keep, got):
            self.low = Halving([keep, got], low_first, 0)
            self.high = Halving([keep, got], high_first, 1)

        def row_step(self, at, deps=()):
            sent = self.low.step(at, deps)
            return [sent, self.high.step(at, deps)]

        def z_step(self, stage, deps):
            if stage == 0:
                self.high.tie(deps)
                sent = self.high.total().astype(bf16)
                self.low.items.append((swap_z(sent, 1), ()))
            else:
                middle = n_z >> (stage + 1)
                self.low.tie(deps)
                sent = self.low.total(rows_of(middle, None)).astype(bf16)
                self.low.narrow(rows_of(0, middle), swap_z(sent, 1 << stage))
            return [sent]

        def z_back(self, deps):
            self.low.tie(deps)
            own = self.low.total().astype(bf16)
            first = own
            for stage in range(z_bits - 1, 0, -1):
                own = jnp.concatenate([own, swap_z(own, 1 << stage)], axis=0)
            far = swap_z(own, 1)
            self.pieces = [own, far, swap_cores(own), swap_cores(far)]
            return [first]

    one = Dense(keep, got)
    sent = one.row_step(0)
    values = [pooled_out[0]] + [swap_z(pooled_out[which], which) for which in range(1, n_z)]

    send, keep = call(
        back_kernel,
        [packed(rows_back)] * 2,
        [
            pltpu.VMEM((2, batch, rank // 2), bf16),
            pltpu.VMEM((2, batch, late), bf16),
            pltpu.VMEM((48, LANES), f32),
        ],
        [vmem] * 8 + [anywhere] * 2,
        "back",
        36,
    )(
        dense_feat,
        pooled,
        cross_down,
        crossed_t,
        delta_first,
        delta_widened,
        delta_reduced,
        small,
        *sent,
    )
    two = Dense(keep, swap_cores(send))

    far_values = call(
        functools.partial(select_kernel, n_z),
        [wide(n_z, tab_grp, batch, width)],
        [],
        [vmem] * n_z + [anywhere],
        "select",
        8,
    )(*values, keep)[0]
    values.append(swap_cores(far_values))
    last = [far_values]
    for at in range(1, row_bits):
        last = one.row_step(at, last)
    last = two.row_step(0, last)

    slots = jnp.transpose(lookup_slots, (0, 2, 1))
    shares = []
    for table in range(tab_grp):
        sums = pl.pallas_call(
            functools.partial(count_kernel, n_row, table, hot, n_z),
            out_shape=wide(n_row, u_shard, width),
            grid=(n_row,),
            in_specs=[vmem] * (2 + n_z) + [anywhere],
            out_specs=pl.BlockSpec((1, u_shard, width), lambda at: (at, 0, 0)),
            compiler_params=pltpu.CompilerParams(vmem_limit_bytes=16 * MIB),
            cost_estimate=no_cost(),
            name="counts",
        )(slots, *values, last[0])
        shares.append(Halving([sums], high_first if table % 2 else low_first))
        last = [sums]
        if table == 0:
            last = one.z_step(0, last)
    for at in range(1, row_bits):
        last = two.row_step(at, last)
    for stage in range(1, z_bits):
        last = one.z_step(stage, last)
    for share in shares:
        share.step(0, last)
    last = two.z_step(0, last)
    last = one.z_back(last)
    for share in shares:
        for at in range(1, row_bits):
            share.step(at, last)
    for stage in range(1, z_bits):
        last = two.z_step(stage, last)
    for share in shares:
        share.tie(last)
    row_grads = jnp.stack([share.total() for share in shares])
    two.z_back([row_grads])

    g_down, g_up, g_first, g_second, g_cbias, g_bias1, g_bias2, g_logit = call(
        unpack_kernel,
        [
            jax.ShapeDtypeStruct((feat // n_row, rank), f32),
            jax.ShapeDtypeStruct((rank // n_row, feat), f32),
            jax.ShapeDtypeStruct((feat // n_row, hid), f32),
            jax.ShapeDtypeStruct((hid // n_row, hid), f32),
            jax.ShapeDtypeStruct((feat // n_row,), f32),
        ]
        + [jax.ShapeDtypeStruct((hid // n_row,), f32)] * 3,
        [pltpu.VMEM((2, rows, LANES), bf16) for rows in (rows_front, rows_back)]
        + [pltpu.VMEM((56, LANES), f32)],
        [vmem] * 8,
        "unpack",
        24,
    )(*one.pieces, *two.pieces)
    return (row_grads, g_down, g_up, g_cbias, g_first, g_bias1, g_second, g_bias2, g_logit)


def solution(mesh):
    in_specs = (
        P(("table", "row"), None),
        P(("table", "row"), None),
        P(("table", "row")),
        P(),
        P(),
        P(),
        P(),
        P(),
        P(),
        P(),
        P(),
        P("table", None, None),
    )
    out_specs = (
        P("table", "row", None),
        P("row", None),
        P("row", None),
        P("row"),
        P("row", None),
        P("row"),
        P("row", None),
        P("row"),
        P("row"),
    )
    return jax.shard_map(local, mesh=mesh, in_specs=in_specs, out_specs=out_specs, check_vma=False)
```

```python
import functools
import itertools

import jax
import jax.numpy as jnp
from jax import lax
from jax.experimental import pallas as pl
from jax.experimental.pallas import tpu as pltpu
from jax.sharding import PartitionSpec as P

loss_scale = 16.0
LANES = 128
SPAN = 9 * LANES
MIB = 1024 * 1024
bf16 = jnp.bfloat16
f32 = jnp.float32


def round_up(value, unit):
    return -(-value // unit) * unit


def matmul(left, right):
    return jnp.dot(left, right, preferred_element_type=f32)


def matmul_rt(left, right):
    return lax.dot_general(left, right, (((1,), (1,)), ((), ())), preferred_element_type=f32)


def reverse_bits(value, bits):
    out = 0
    for bit in range(bits):
        out = out | (((value >> bit) & 1) << (bits - 1 - bit))
    return out


def places_of(z_pos, n_z):
    bits = n_z.bit_length() - 1
    return [reverse_bits(z_pos ^ quarter, bits) for quarter in range(n_z)]


def put_blocks(ref, row_pos, places, offset, value):
    shards, n_half, rows_q = ref.shape[1], ref.shape[2], ref.shape[3]
    rows = value.shape[0] // shards
    step = round_up(rows, 16)
    blocks = value.shape[1] // LANES
    for shard in range(shards):
        slot = shard ^ row_pos
        for block in range(blocks):
            done = 0
            while done < rows:
                quarter, at = divmod(offset + block * step + done, rows_q)
                length = min(rows - done, rows_q - at)
                place = places[quarter]
                ref[lax.div(place, n_half), slot, lax.rem(place, n_half), at : at + length, :] = value[
                    shard * rows + done : shard * rows + done + length,
                    block * LANES : (block + 1) * LANES,
                ].astype(ref.dtype)
                done += length
    return offset + blocks * step


def put_rows(ref, offset, value):
    for block in range(value.shape[1] // LANES):
        ref[offset + block : offset + block + 1, :] = value[:, block * LANES : (block + 1) * LANES]


def position():
    table_pos = lax.axis_index("table")
    return lax.rem(table_pos, 2), lax.axis_index("row"), table_pos


class Loads:
    def __init__(self, sources, targets, sems):
        self.copies = [
            pltpu.make_async_copy(source, target, sems.at[at])
            for at, (source, target) in enumerate(zip(sources, targets))
        ]
        self.targets = targets
        self.ready = set()
        for copy in self.copies:
            copy.start()

    def __call__(self, at):
        if at not in self.ready:
            self.copies[at].wait()
            self.ready.add(at)
        return self.targets[at][...]


def as_row(value):
    return value.reshape(1, value.shape[-1])


def front_kernel(*refs):
    sources, outs, targets = refs[:11], refs[11:16], refs[16:27]
    halves, thirds, sems = refs[27:]
    send, keep, crossed_t_out, first_out, small = outs
    load = Loads(sources, targets, sems)
    core, row_pos, table_pos = position()
    places = places_of(lax.div(table_pos, 2), 2 * send.shape[2])
    stacked = jnp.concatenate([load(0), load(1)], axis=1)
    reduced = matmul(stacked, load(2)).astype(bf16)
    widened = matmul(reduced, load(3)) + as_row(load(4))
    wide = stacked.astype(f32)
    crossed = (wide * widened + wide).astype(bf16)
    pre_first = matmul(crossed, load(5)) + as_row(load(6))
    sig_first = jax.nn.sigmoid(pre_first)
    act_first = (pre_first * sig_first).astype(bf16)
    slope_first = sig_first * (1.0 + pre_first * (1.0 - sig_first))
    w_hidden2 = load(7)
    pre_second = matmul(act_first, w_hidden2) + as_row(load(8))
    sig_second = jax.nn.sigmoid(pre_second)
    act_second = (pre_second * sig_second).astype(bf16).astype(f32)
    slope_second = sig_second * (1.0 + pre_second * (1.0 - sig_second))
    w_logit = as_row(load(9))
    logits = jnp.sum(act_second * w_logit, axis=1, keepdims=True)
    labels = as_row(load(10))
    count = labels.shape[1]
    same = lax.broadcasted_iota(jnp.int32, (count, count), 0) == lax.broadcasted_iota(
        jnp.int32, (count, count), 1
    )
    label_col = jnp.sum(jnp.where(same, labels.astype(f32), 0.0), axis=1, keepdims=True)
    delta_logit = loss_scale * (jax.nn.sigmoid(logits) - label_col)
    delta_second = (delta_logit * w_logit * slope_second).astype(bf16)
    put_rows(small, 16, jnp.sum(act_second * delta_logit, axis=0, keepdims=True))
    put_rows(small, 8, jnp.sum(delta_second.astype(f32), axis=0, keepdims=True))
    half = halves.shape[2]
    halves[0] = delta_second[:, :half]
    halves[1] = delta_second[:, half:]
    delta_first = (matmul_rt(delta_second, w_hidden2) * slope_first).astype(bf16)
    first_out[...] = delta_first
    put_rows(small, 0, jnp.sum(delta_first.astype(f32), axis=0, keepdims=True))
    part = thirds.shape[2]
    thirds[0] = delta_first[:, :part]
    thirds[1] = delta_first[:, half : half + part]
    act_t = act_first.T
    crossed_t = crossed.T
    crossed_t_out[...] = crossed_t
    for ref, who in ((send, 1 - core), (keep, core)):
        offset = put_blocks(ref, row_pos, places, 0, matmul(act_t, halves[who]))
        put_blocks(ref, row_pos, places, offset, matmul(crossed_t, thirds[who]))


def middle_kernel(n_z, *refs):
    sources, delta_first = refs[:6], refs[6]
    widened_out, reduced_out = refs[7:9]
    pooled_outs = refs[9 : 9 + n_z]
    rest = refs[9 + n_z :]
    targets = rest[:6]
    by_group, sems = rest[6:]
    load = Loads(sources, targets, sems)
    core, _, table_pos = position()
    z_pos = lax.div(table_pos, 2)
    stacked = jnp.concatenate([load(0), load(1)], axis=1)
    cross_down, cross_up = load(2), load(3)
    reduced = matmul(stacked, cross_down).astype(bf16)
    widened = matmul(reduced, cross_up) + as_row(load(4))
    delta_crossed = matmul_rt(delta_first[...], load(5))
    delta_widened = (delta_crossed * stacked.astype(f32)).astype(bf16)
    widened_out[...] = delta_widened
    delta_reduced = matmul_rt(delta_widened, cross_up).astype(bf16)
    reduced_out[...] = delta_reduced
    delta_stacked = delta_crossed * (widened + 1.0) + matmul_rt(delta_reduced, cross_down)
    width = targets[0].shape[1]
    per_group = by_group.shape[2]
    for table in range(2 * n_z * per_group):
        group = table // per_group
        by_group[group // 2, group % 2, table % per_group] = delta_stacked[
            :, width * (table + 1) : width * (table + 2)
        ].astype(bf16)
    for which in range(n_z):
        pooled_outs[which][0] = by_group[z_pos ^ which, core]
        pooled_outs[which][1] = by_group[z_pos ^ which, 1 - core]


def back_kernel(*refs):
    dense_feat, pooled, cross_down, crossed_t, delta_first, delta_widened, delta_reduced = refs[:7]
    small_in = refs[7]
    send, keep = refs[8:10]
    half_delta, sixths, small = refs[10:]
    core, row_pos, table_pos = position()
    n_row = send.shape[1]
    places = places_of(lax.div(table_pos, 2), 2 * send.shape[2])
    rank = delta_reduced.shape[1]
    feat = delta_widened.shape[1]
    hid = delta_first.shape[1]
    part = hid // 2 - sixths.shape[2]
    half_delta[0] = delta_reduced[:, : rank // 2]
    half_delta[1] = delta_reduced[:, rank // 2 :]
    sixths[0] = delta_first[:, part : hid // 2]
    sixths[1] = delta_first[:, hid // 2 + part :]
    put_rows(small, 24, jnp.sum(delta_widened[...].astype(f32), axis=0, keepdims=True))
    small[0:24, :] = small_in[...]
    small[41:48, :] = jnp.zeros((7, LANES), f32)
    sums = jnp.concatenate([small[...]] * n_row, axis=0)
    stacked = jnp.concatenate([dense_feat[...], pooled[...]], axis=1)
    reduced_t = matmul(stacked, cross_down[...]).astype(bf16).T
    stacked_t = stacked.T
    for ref, who in ((send, 1 - core), (keep, core)):
        offset = put_blocks(ref, row_pos, places, 0, matmul(crossed_t[...], sixths[who]))
        offset = put_blocks(ref, row_pos, places, offset, matmul(stacked_t, half_delta[who]))
        start = pl.multiple_of(who * (feat - SPAN), LANES)
        offset = put_blocks(
            ref, row_pos, places, offset, matmul(reduced_t, delta_widened[:, pl.ds(start, SPAN)])
        )
        offset = put_blocks(ref, row_pos, places, offset, sums)
        tail = 2 * ref.shape[2] * ref.shape[3] - offset
        if tail:
            put_blocks(ref, row_pos, places, offset, jnp.zeros((n_row * tail, LANES), f32))


def select_kernel(n_z, *refs):
    for which in range(n_z):
        out = refs[len(refs) - 2 + which // (n_z // 2)]
        out[which % (n_z // 2)] = refs[which][1]


def count_kernel(n_row, table, hot, n_z, slots, *rest):
    direct, crossed, out = rest[:n_z], rest[n_z : n_z + 2], rest[-1]
    near = n_z // 2
    block = out.shape[1]
    samples = crossed[0].shape[2]
    core, row_pos, table_pos = position()
    z_pos = lax.div(table_pos, 2)
    base = (pl.program_id(0) ^ row_pos) * block
    names = lax.broadcasted_iota(jnp.int16, (block, samples), 0)
    total = jnp.zeros((block, out.shape[2]), f32)
    one = jnp.ones((block, samples), bf16)
    zero = jnp.zeros((block, samples), bf16)
    for which in range(n_z):
        far = crossed[which // near]
        for held, who in ((direct[which][0, table], core), (far[which % near, table], 1 - core)):
            source = 2 * (z_pos ^ which) + who
            start = pl.multiple_of((source * n_row + row_pos) * samples, LANES)
            lines = slots[table, :, pl.ds(start, samples)] - base
            lines = jnp.where((lines >= 0) & (lines < block), lines, block).astype(jnp.int16)
            counts = zero
            for look in range(hot):
                line = jnp.broadcast_to(lines[look : look + 1, :], (block, samples))
                counts = counts + jnp.where(line == names, one, zero)
            total = total + matmul(counts, held)
    out[0] = total.astype(out.dtype)


def unpack_kernel(*refs):
    parts = refs[0:8]
    g_down, g_up, g_first, g_second = refs[8:12]
    small_outs = refs[12:16]
    held, small = refs[16:18], refs[18]
    core, row_pos, table_pos = position()
    z_pos = lax.div(table_pos, 2)
    for stream in range(2):
        lower, upper, lower_other, upper_other = parts[4 * stream : 4 * stream + 4]
        ref = held[stream]
        rows = lower.shape[1]
        n_z = 2 * lower.shape[0]
        z_bits = n_z.bit_length() - 1
        for who, pieces in ((core, (lower, upper)), (1 - core, (lower_other, upper_other))):
            for place in range(n_z):
                start = pl.multiple_of((reverse_bits(place, z_bits) ^ z_pos) * rows, 16)
                ref[who, pl.ds(start, rows), :] = pieces[place // (n_z // 2)][place % (n_z // 2)]
    front, back = held

    def take(ref, out, half, offset, columns):
        rows = out.shape[0]
        step = round_up(rows, 16)
        for column in columns:
            out[:, column * LANES : (column + 1) * LANES] = ref[
                half, offset : offset + rows, :
            ].astype(f32)
            offset += step
        return offset

    for half in range(2):
        blocks = g_second.shape[1] // LANES // 2
        offset = take(front, g_second, half, 0, range(half * blocks, (half + 1) * blocks))
        blocks = g_first.shape[1] // LANES // 2
        early = blocks - blocks // 4
        take(front, g_first, half, offset, range(half * blocks, half * blocks + early))
        offset = take(back, g_first, half, 0, range(half * blocks + early, (half + 1) * blocks))
        blocks = g_down.shape[1] // LANES // 2
        offset = take(back, g_down, half, offset, range(half * blocks, (half + 1) * blocks))
        blocks = g_up.shape[1] // LANES
        offset = take(back, g_up, half, offset, range(half * (blocks - 9), half * (blocks - 9) + 9))
    small[0:48, :] = back[0, offset : offset + 48, :].astype(f32)
    small[48:, :] = jnp.zeros((small.shape[0] - 48, LANES), f32)
    for out, first in zip(small_outs, (24, 0, 8, 16)):
        share = out.shape[0]
        begin = row_pos * share
        row, lane = lax.div(begin, LANES), lax.rem(begin, LANES)
        lanes = lax.broadcasted_iota(jnp.int32, (1, LANES), 1)
        for start in range(0, share, LANES):
            length = min(LANES, share - start)
            this = small[pl.ds(first + row + start // LANES, 1), :]
            later = small[pl.ds(first + row + start // LANES + 1, 1), :]
            both = jnp.where(lanes < lane, later, this)
            turned = pltpu.roll(both, lax.rem(LANES - lane, LANES), 1)
            out[start : start + length] = turned.reshape(LANES)[:length]


def whole(memory=pltpu.VMEM):
    return pl.BlockSpec(memory_space=memory)


def no_cost():
    return pl.CostEstimate(flops=0, transcendentals=0, bytes_accessed=0)


def call(body, outs, scratch, in_specs, name, mib):
    return pl.pallas_call(
        body,
        out_shape=outs,
        in_specs=in_specs,
        out_specs=[whole()] * len(outs),
        scratch_shapes=scratch,
        compiler_params=pltpu.CompilerParams(vmem_limit_bytes=mib * MIB),
        cost_estimate=no_cost(),
        name=name,
    )


def after(values, deps):
    return list(lax.optimization_barrier(tuple(values) + tuple(deps))[: len(values)])


def held_like(values):
    return [pltpu.VMEM(value.shape, value.dtype) for value in values]


def sum_rows_kernel(plan, *refs):
    out = refs[-1]
    for table, terms in enumerate(plan):
        total = None
        for which, picks in terms:
            part = refs[which][picks].astype(f32)
            total = part if total is None else total + part
        out[table] = total


def sum_rows(groups, deps):
    arrays = [array for items in groups for array, _ in items]
    plan, count = [], 0
    for items in groups:
        plan.append([(count + at, tuple(picks)) for at, (_, picks) in enumerate(items)])
        count += len(items)
    kept = [pick.stop - pick.start for pick in groups[0][0][1] if isinstance(pick, slice)]
    return call(
        functools.partial(sum_rows_kernel, plan),
        [jax.ShapeDtypeStruct((len(groups), *kept), f32)],
        [],
        [whole()] * len(arrays) + [whole(pl.ANY)] * len(deps),
        "rows",
        24,
    )(*arrays, *deps)[0]


def sum_kernel(plan, n_in, *refs):
    outs = refs[len(refs) - len(plan) :]
    for out, terms in zip(outs, plan):
        rows = out.shape[-2]
        chunk = next(size for size in (64, 48, 80, 32, 16, 8, rows) if rows % size == 0)

        def one_chunk(at, carry, out=out, terms=terms, chunk=chunk):
            window = pl.ds(pl.multiple_of(at * chunk, chunk), chunk)
            for lead in itertools.product(*[range(size) for size in out.shape[:-2]]):
                total = None
                for which, picks in terms:
                    axes, place = iter(lead), []
                    for pick in picks[:-2]:
                        place.append(pick.start + next(axes) if isinstance(pick, slice) else pick)
                    part = refs[which][(*place, window, slice(None))].astype(f32)
                    total = part if total is None else total + part
                out[(*lead, window, slice(None))] = total.astype(out.dtype)
            return carry

        lax.fori_loop(0, rows // chunk, one_chunk, 0)


def take_sums(groups, deps, dtype=bf16):
    arrays, plan, shapes = [], [], []
    for items in groups:
        terms = []
        for array, picks in items:
            found = [at for at, known in enumerate(arrays) if known is array]
            if not found:
                arrays.append(array)
            terms.append((found[0] if found else len(arrays) - 1, tuple(picks)))
        plan.append(terms)
        kept = [pick.stop - pick.start for pick in items[0][1] if isinstance(pick, slice)]
        shapes.append(jax.ShapeDtypeStruct(tuple(kept), dtype))
    return call(
        functools.partial(sum_kernel, plan, len(arrays)),
        shapes,
        [],
        [whole()] * len(arrays) + [whole(pl.ANY)] * len(deps),
        "sums",
        24,
    )(*arrays, *deps)


def local(
    dense_feat,
    pooled,
    labels,
    cross_down,
    cross_up,
    cross_bias,
    w_hidden1,
    bias1,
    w_hidden2,
    bias2,
    w_logit,
    lookup_slots,
):
    n_table = lax.axis_size("table")
    n_row = lax.axis_size("row")
    n_z = n_table // 2
    row_bits = n_row.bit_length() - 1
    z_bits = n_z.bit_length() - 1
    batch, width = dense_feat.shape
    feat, rank = cross_down.shape
    hid = w_hidden1.shape[1]
    tab_grp, _, hot = lookup_slots.shape
    u_shard = batch * n_table * hot // 16

    def swap_cores(value):
        return lax.ppermute(value, "table", [(at, at ^ 1) for at in range(n_table)])

    def swap_z(value, which):
        return lax.ppermute(value, "table", [(at, at ^ (2 * which)) for at in range(n_table)])

    def swap_row(value, bit):
        return lax.ppermute(value, "row", [(at, at ^ (1 << bit)) for at in range(n_row)])

    late = hid // 8
    early = hid // 2 - late
    rows_front = (hid // 2 // LANES) * round_up(hid // n_row, 16)
    rows_front += (early // LANES) * round_up(feat // n_row, 16)
    rows_back = (late // LANES) * round_up(feat // n_row, 16)
    rows_back += (rank // 2 // LANES) * round_up(feat // n_row, 16)
    rows_back += 9 * round_up(rank // n_row, 16) + 48
    rows_front, rows_back = (round_up(rows, 16 * n_z) for rows in (rows_front, rows_back))

    def packed(rows):
        return jax.ShapeDtypeStruct((2, n_row, n_z // 2, rows // n_z, LANES), bf16)

    def wide(*shape):
        return jax.ShapeDtypeStruct(shape, bf16)

    hbm, vmem, anywhere = whole(pltpu.HBM), whole(), whole(pl.ANY)

    sources = (
        dense_feat,
        pooled,
        cross_down,
        cross_up,
        cross_bias,
        w_hidden1,
        bias1,
        w_hidden2,
        bias2,
        w_logit,
        labels,
    )
    send1, keep1, crossed_t, delta_first, small = call(
        front_kernel,
        [packed(rows_front)] * 2
        + [wide(feat, batch), wide(batch, hid), jax.ShapeDtypeStruct((24, LANES), f32)],
        held_like(sources)
        + [
            pltpu.VMEM((2, batch, hid // 2), bf16),
            pltpu.VMEM((2, batch, early), bf16),
            pltpu.SemaphoreType.DMA((len(sources),)),
        ],
        [hbm] * len(sources),
        "front",
        60,
    )(*sources)
    got1 = swap_cores(send1)

    sources = (dense_feat, pooled, cross_down, cross_up, cross_bias, w_hidden1)
    outs = call(
        functools.partial(middle_kernel, n_z),
        [wide(batch, feat), wide(batch, rank)] + [wide(2, tab_grp, batch, width)] * n_z,
        held_like(sources)
        + [
            pltpu.VMEM((n_z, 2, tab_grp, batch, width), bf16),
            pltpu.SemaphoreType.DMA((len(sources),)),
        ],
        [hbm] * len(sources) + [vmem],
        "middle",
        60,
    )(*sources, delta_first)
    delta_widened, delta_reduced = outs[:2]
    pooled_out = outs[2:]

    low_first = tuple(range(row_bits))
    high_first = low_first[::-1]

    class Terms:
        def __init__(self, arrays, picks):
            self.items = []
            for array in arrays:
                self.add(array, picks)

        def add(self, array, picks=()):
            whole_axes = [slice(0, size) for size in array.shape[len(picks) :]]
            self.items.append((array, list(picks) + whole_axes))

        def narrowed(self, axis, what):
            items = []
            for array, picks in self.items:
                at = [number for number, pick in enumerate(picks) if isinstance(pick, slice)][axis]
                items.append((array, picks[:at] + [what] + picks[at + 1 :]))
            return items

        def far_near(self, axis, near, far):
            sent = self.narrowed(axis, far)
            self.items = self.narrowed(axis, near)
            return sent

    class Halving(Terms):
        def __init__(self, arrays, order, picks=()):
            dims = len(picks)
            arrays = [
                array.reshape(array.shape[:dims] + (2,) * row_bits + array.shape[dims + 1 :])
                for array in arrays
            ]
            super().__init__(arrays, picks)
            self.order, self.left = order, list(range(row_bits - 1, -1, -1))

        def part(self, at):
            axis = self.left.index(self.order[at])
            self.left.remove(self.order[at])
            return self.far_near(axis, 0, 1)

    def row_step(streams, at, deps):
        sent = take_sums([stream.part(at) for stream in streams], deps)
        for stream, value in zip(streams, sent):
            stream.add(swap_row(value, stream.order[at]))
        return list(sent)

    class Dense:
        def __init__(self, keep, got):
            self.low = Halving([keep, got], low_first, [0])
            self.high = Halving([keep, got], high_first, [1])

        def row_step(self, at, deps):
            deps = [*deps, self.low.items[-1][0], self.high.items[-1][0]]
            return row_step((self.low, self.high), at, deps)

        def z_step(self, stage, deps):
            middle = n_z >> (stage + 1)
            items, deps = self.high.items, [*deps, self.low.items[-1][0]]
            if stage > 0:
                items = self.low.far_near(0, slice(0, middle), slice(middle, 2 * middle))
            (sent,) = take_sums([items], deps)
            self.low.add(swap_z(sent, 1 << stage))
            return [sent]

        def z_own(self, deps):
            (self.own,) = take_sums([self.low.items], deps)
            self.back = swap_z(self.own, 1 << (z_bits - 1)) if z_bits > 1 else None
            return [self.own]

        def z_back(self, deps):
            for stage in range(z_bits - 1, 0, -1):
                if stage < z_bits - 1:
                    self.back = swap_z(self.own, 1 << stage)
                (back,) = after([self.back], deps)
                self.own = jnp.concatenate([self.own, back], axis=0)
            far = swap_z(self.own, 1)
            self.pieces = [self.own, far, swap_cores(self.own), swap_cores(far)]
            return [self.own]

    send2, keep2 = call(
        back_kernel,
        [packed(rows_back)] * 2,
        [
            pltpu.VMEM((2, batch, rank // 2), bf16),
            pltpu.VMEM((2, batch, late), bf16),
            pltpu.VMEM((48, LANES), f32),
        ],
        [vmem] * 8,
        "back",
        36,
    )(
        dense_feat,
        pooled,
        cross_down,
        crossed_t,
        delta_first,
        delta_widened,
        delta_reduced,
        small,
    )

    got2 = swap_cores(send2)

    one, two = Dense(keep1, got1), Dense(keep2, got2)
    last = one.row_step(0, [keep2])
    two.row_step(0, last)
    values, chain = {0: pooled_out[0]}, [n_z // 2]
    chain += [which for which in range(n_z - 1, 0, -1) if which != n_z // 2]
    for at, which in enumerate(chain):
        moved = pooled_out[which]
        if at > 0:
            (moved,) = after([moved], [values[chain[at - 1]]])
        values[which] = swap_z(moved, which)
    last = [values[chain[0]]]
    for at in range(1, row_bits):
        last = one.row_step(at, last)
    last = [*last, values[chain[min(1, len(chain) - 1)]]]
    for at in range(1, row_bits):
        last = two.row_step(at, last)
    last = one.z_step(0, last)
    values = [values[which] for which in range(n_z)]
    far_values = call(
        functools.partial(select_kernel, n_z),
        [wide(n_z // 2, tab_grp, batch, width)] * 2,
        [],
        [vmem] * n_z + [anywhere],
        "select",
        8,
    )(*values, last[0])
    values += [swap_cores(value) for value in far_values]
    slots = jnp.transpose(lookup_slots, (0, 2, 1))
    last, shares = [far_values[0]], []
    for table in range(tab_grp):
        sums = pl.pallas_call(
            functools.partial(count_kernel, n_row, table, hot, n_z),
            out_shape=wide(n_row, u_shard, width),
            grid=(n_row,),
            in_specs=[vmem] * (3 + n_z) + [anywhere],
            out_specs=pl.BlockSpec((1, u_shard, width), lambda at: (at, 0, 0)),
            compiler_params=pltpu.CompilerParams(vmem_limit_bytes=16 * MIB),
            cost_estimate=no_cost(),
            name="counts",
        )(slots, *values, last[0])
        shares.append(Halving([sums], high_first if table % 2 else low_first))
        last = [sums]
        if table == 0:
            for stage in range(1, z_bits):
                last = one.z_step(stage, last)
            last = two.z_step(0, last)
    for stage in range(1, z_bits):
        last = two.z_step(stage, last)
    last = one.z_own(last)
    last = row_step(shares, 0, last)
    last = two.z_own(last)
    last = one.z_back(last)
    for at in range(1, row_bits):
        last = row_step(shares, at, last)
    row_grads = sum_rows([share.items for share in shares], last)
    two.z_back([row_grads])

    g_down, g_up, g_first, g_second, g_cbias, g_bias1, g_bias2, g_logit = call(
        unpack_kernel,
        [
            jax.ShapeDtypeStruct((feat // n_row, rank), f32),
            jax.ShapeDtypeStruct((rank // n_row, feat), f32),
            jax.ShapeDtypeStruct((feat // n_row, hid), f32),
            jax.ShapeDtypeStruct((hid // n_row, hid), f32),
            jax.ShapeDtypeStruct((feat // n_row,), f32),
        ]
        + [jax.ShapeDtypeStruct((hid // n_row,), f32)] * 3,
        [pltpu.VMEM((2, rows, LANES), bf16) for rows in (rows_front, rows_back)]
        + [pltpu.VMEM((56, LANES), f32)],
        [vmem] * 8,
        "unpack",
        24,
    )(*one.pieces, *two.pieces)
    return (row_grads, g_down, g_up, g_cbias, g_first, g_bias1, g_second, g_bias2, g_logit)


def solution(mesh):
    in_specs = (
        P(("table", "row"), None),
        P(("table", "row"), None),
        P(("table", "row")),
        P(),
        P(),
        P(),
        P(),
        P(),
        P(),
        P(),
        P(),
        P("table", None, None),
    )
    out_specs = (
        P("table", "row", None),
        P("row", None),
        P("row", None),
        P("row"),
        P("row", None),
        P("row"),
        P("row", None),
        P("row"),
        P("row"),
    )
    return jax.shard_map(local, mesh=mesh, in_specs=in_specs, out_specs=out_specs, check_vma=False)
```

```python
import functools
import itertools

import jax
import jax.numpy as jnp
from jax import lax
from jax.experimental import pallas as pl
from jax.experimental.pallas import tpu as pltpu
from jax.sharding import PartitionSpec as P

loss_scale = 16.0
LANES = 128
SPAN = 9 * LANES
MIB = 1024 * 1024
bf16 = jnp.bfloat16
f32 = jnp.float32


def round_up(value, unit):
    return -(-value // unit) * unit


def matmul(left, right):
    return jnp.dot(left, right, preferred_element_type=f32)


def matmul_rt(left, right):
    return lax.dot_general(left, right, (((1,), (1,)), ((), ())), preferred_element_type=f32)


def reverse_bits(value, bits):
    out = 0
    for bit in range(bits):
        out = out | (((value >> bit) & 1) << (bits - 1 - bit))
    return out


def places_of(z_pos, n_z):
    bits = n_z.bit_length() - 1
    return [reverse_bits(z_pos ^ quarter, bits) for quarter in range(n_z)]


def put_blocks(ref, row_pos, places, offset, value):
    shards, n_half, rows_q = ref.shape[1], ref.shape[2], ref.shape[3]
    rows = value.shape[0] // shards
    step = round_up(rows, 16)
    blocks = value.shape[1] // LANES
    for shard in range(shards):
        slot = shard ^ row_pos
        for block in range(blocks):
            done = 0
            while done < rows:
                quarter, at = divmod(offset + block * step + done, rows_q)
                length = min(rows - done, rows_q - at)
                place = places[quarter]
                ref[lax.div(place, n_half), slot, lax.rem(place, n_half), at : at + length, :] = value[
                    shard * rows + done : shard * rows + done + length,
                    block * LANES : (block + 1) * LANES,
                ].astype(ref.dtype)
                done += length
    return offset + blocks * step


def put_rows(ref, offset, value):
    for block in range(value.shape[1] // LANES):
        ref[offset + block : offset + block + 1, :] = value[:, block * LANES : (block + 1) * LANES]


def position():
    table_pos = lax.axis_index("table")
    return lax.rem(table_pos, 2), lax.axis_index("row"), table_pos


class Loads:
    def __init__(self, sources, targets, sems, first):
        self.copies = [
            pltpu.make_async_copy(source, target, sems.at[at])
            for at, (source, target) in enumerate(zip(sources, targets))
        ]
        self.targets, self.first = targets, first
        self.ready = set()
        for copy in self.copies[:first]:
            copy.start()

    def more(self):
        for copy in self.copies[self.first :]:
            copy.start()

    def __call__(self, at):
        if at not in self.ready:
            self.copies[at].wait()
            self.ready.add(at)
        return self.targets[at][...]


def as_row(value):
    return value.reshape(1, value.shape[-1])


def front_kernel(*refs):
    sources, outs, targets = refs[:11], refs[11:16], refs[16:27]
    halves, thirds, sems = refs[27:]
    send, keep, crossed_t_out, first_out, small = outs
    load = Loads(sources, targets, sems, 5)
    core, row_pos, table_pos = position()
    places = places_of(lax.div(table_pos, 2), 2 * send.shape[2])
    stacked = jnp.concatenate([load(0), load(1)], axis=1)
    cross_down = load(2)
    load.more()
    reduced = matmul(stacked, cross_down).astype(bf16)
    widened = matmul(reduced, load(3)) + as_row(load(4))
    wide = stacked.astype(f32)
    crossed = (wide * widened + wide).astype(bf16)
    pre_first = matmul(crossed, load(5)) + as_row(load(6))
    sig_first = jax.nn.sigmoid(pre_first)
    act_first = (pre_first * sig_first).astype(bf16)
    slope_first = sig_first * (1.0 + pre_first * (1.0 - sig_first))
    w_hidden2 = load(7)
    pre_second = matmul(act_first, w_hidden2) + as_row(load(8))
    sig_second = jax.nn.sigmoid(pre_second)
    act_second = (pre_second * sig_second).astype(bf16).astype(f32)
    slope_second = sig_second * (1.0 + pre_second * (1.0 - sig_second))
    w_logit = as_row(load(9))
    logits = jnp.sum(act_second * w_logit, axis=1, keepdims=True)
    labels = as_row(load(10))
    count = labels.shape[1]
    same = lax.broadcasted_iota(jnp.int32, (count, count), 0) == lax.broadcasted_iota(
        jnp.int32, (count, count), 1
    )
    label_col = jnp.sum(jnp.where(same, labels.astype(f32), 0.0), axis=1, keepdims=True)
    delta_logit = loss_scale * (jax.nn.sigmoid(logits) - label_col)
    delta_second = (delta_logit * w_logit * slope_second).astype(bf16)
    put_rows(small, 16, jnp.sum(act_second * delta_logit, axis=0, keepdims=True))
    put_rows(small, 8, jnp.sum(delta_second.astype(f32), axis=0, keepdims=True))
    half = halves.shape[2]
    halves[0] = delta_second[:, :half]
    halves[1] = delta_second[:, half:]
    delta_first = (matmul_rt(delta_second, w_hidden2) * slope_first).astype(bf16)
    first_out[...] = delta_first
    put_rows(small, 0, jnp.sum(delta_first.astype(f32), axis=0, keepdims=True))
    part = thirds.shape[2]
    thirds[0] = delta_first[:, :part]
    thirds[1] = delta_first[:, half : half + part]
    act_t = act_first.T
    crossed_t = crossed.T
    crossed_t_out[...] = crossed_t
    for ref, who in ((send, 1 - core), (keep, core)):
        offset = put_blocks(ref, row_pos, places, 0, matmul(act_t, halves[who]))
        put_blocks(ref, row_pos, places, offset, matmul(crossed_t, thirds[who]))


def middle_kernel(n_z, *refs):
    sources, send, keep = refs[:9], refs[9], refs[10]
    pooled_outs = refs[11 : 11 + n_z]
    rest = refs[11 + n_z :]
    targets = rest[:9]
    by_group, wide_delta, half_delta, sixths, small, sems = rest[9:]
    load = Loads(sources, targets, sems, 6)
    core, row_pos, table_pos = position()
    z_pos = lax.div(table_pos, 2)
    places = places_of(z_pos, 2 * send.shape[2])
    stacked = jnp.concatenate([load(0), load(1)], axis=1)
    cross_down = load(2)
    load.more()
    reduced = matmul(stacked, cross_down).astype(bf16)
    cross_up = load(3)
    widened = matmul(reduced, cross_up) + as_row(load(4))
    delta_first = load(5)
    delta_crossed = matmul_rt(delta_first, load(6))
    delta_widened = (delta_crossed * stacked.astype(f32)).astype(bf16)
    wide_delta[...] = delta_widened
    delta_reduced = matmul_rt(delta_widened, cross_up).astype(bf16)
    delta_stacked = delta_crossed * (widened + 1.0) + matmul_rt(delta_reduced, cross_down)
    width = targets[0].shape[1]
    per_group = by_group.shape[2]
    for table in range(2 * n_z * per_group):
        group = table // per_group
        by_group[group // 2, group % 2, table % per_group] = delta_stacked[
            :, width * (table + 1) : width * (table + 2)
        ].astype(bf16)
    for which in range(n_z):
        pooled_outs[which][0] = by_group[z_pos ^ which, core]
        pooled_outs[which][1] = by_group[z_pos ^ which, 1 - core]

    n_row, rank, feat = send.shape[1], delta_reduced.shape[1], delta_widened.shape[1]
    hid = delta_first.shape[1]
    part = hid // 2 - sixths.shape[2]
    half_delta[0] = delta_reduced[:, : rank // 2]
    half_delta[1] = delta_reduced[:, rank // 2 :]
    sixths[0] = delta_first[:, part : hid // 2]
    sixths[1] = delta_first[:, hid // 2 + part :]
    put_rows(small, 24, jnp.sum(delta_widened.astype(f32), axis=0, keepdims=True))
    small[0:24, :] = load(8)
    small[41:48, :] = jnp.zeros((7, LANES), f32)
    sums = jnp.concatenate([small[...]] * n_row, axis=0)
    crossed_t, reduced_t, stacked_t = load(7), reduced.T, stacked.T
    for ref, who in ((send, 1 - core), (keep, core)):
        offset = put_blocks(ref, row_pos, places, 0, matmul(crossed_t, sixths[who]))
        offset = put_blocks(ref, row_pos, places, offset, matmul(stacked_t, half_delta[who]))
        start = pl.multiple_of(who * (feat - SPAN), LANES)
        offset = put_blocks(
            ref, row_pos, places, offset, matmul(reduced_t, wide_delta[:, pl.ds(start, SPAN)])
        )
        offset = put_blocks(ref, row_pos, places, offset, sums)
        tail = 2 * ref.shape[2] * ref.shape[3] - offset
        if tail:
            put_blocks(ref, row_pos, places, offset, jnp.zeros((n_row * tail, LANES), f32))


def select_kernel(n_z, *refs):
    for which in range(n_z):
        out = refs[len(refs) - 2 + which // (n_z // 2)]
        out[which % (n_z // 2)] = refs[which][1]


def count_kernel(n_row, table, hot, n_z, slots, *rest):
    direct, crossed, out = rest[:n_z], rest[n_z : n_z + 2], rest[-1]
    near = n_z // 2
    block = out.shape[1]
    samples = crossed[0].shape[2]
    core, row_pos, table_pos = position()
    z_pos = lax.div(table_pos, 2)
    base = (pl.program_id(0) ^ row_pos) * block
    names = lax.broadcasted_iota(jnp.int16, (block, samples), 0)
    total = jnp.zeros((block, out.shape[2]), f32)
    one = jnp.ones((block, samples), bf16)
    zero = jnp.zeros((block, samples), bf16)
    for which in range(n_z):
        far = crossed[which // near]
        for held, who in ((direct[which][0, table], core), (far[which % near, table], 1 - core)):
            source = 2 * (z_pos ^ which) + who
            start = pl.multiple_of((source * n_row + row_pos) * samples, LANES)
            lines = slots[table, :, pl.ds(start, samples)] - base
            lines = jnp.where((lines >= 0) & (lines < block), lines, block).astype(jnp.int16)
            counts = zero
            for look in range(hot):
                line = jnp.broadcast_to(lines[look : look + 1, :], (block, samples))
                counts = counts + jnp.where(line == names, one, zero)
            total = total + matmul(counts, held)
    out[0] = total.astype(out.dtype)


def unpack_kernel(*refs):
    parts = refs[0:8]
    g_down, g_up, g_first, g_second = refs[8:12]
    small_outs = refs[12:16]
    held, small = refs[16:18], refs[18]
    core, row_pos, table_pos = position()
    z_pos = lax.div(table_pos, 2)
    for stream in range(2):
        lower, upper, lower_other, upper_other = parts[4 * stream : 4 * stream + 4]
        ref = held[stream]
        rows = lower.shape[1]
        n_z = 2 * lower.shape[0]
        z_bits = n_z.bit_length() - 1
        for who, pieces in ((core, (lower, upper)), (1 - core, (lower_other, upper_other))):
            for place in range(n_z):
                start = pl.multiple_of((reverse_bits(place, z_bits) ^ z_pos) * rows, 16)
                ref[who, pl.ds(start, rows), :] = pieces[place // (n_z // 2)][place % (n_z // 2)]
    front, back = held

    def take(ref, out, half, offset, columns):
        rows = out.shape[0]
        step = round_up(rows, 16)
        for column in columns:
            out[:, column * LANES : (column + 1) * LANES] = ref[
                half, offset : offset + rows, :
            ].astype(f32)
            offset += step
        return offset

    for half in range(2):
        blocks = g_second.shape[1] // LANES // 2
        offset = take(front, g_second, half, 0, range(half * blocks, (half + 1) * blocks))
        blocks = g_first.shape[1] // LANES // 2
        early = blocks - blocks // 4
        take(front, g_first, half, offset, range(half * blocks, half * blocks + early))
        offset = take(back, g_first, half, 0, range(half * blocks + early, (half + 1) * blocks))
        blocks = g_down.shape[1] // LANES // 2
        offset = take(back, g_down, half, offset, range(half * blocks, (half + 1) * blocks))
        blocks = g_up.shape[1] // LANES
        offset = take(back, g_up, half, offset, range(half * (blocks - 9), half * (blocks - 9) + 9))
    small[0:48, :] = back[0, offset : offset + 48, :].astype(f32)
    small[48:, :] = jnp.zeros((small.shape[0] - 48, LANES), f32)
    for out, first in zip(small_outs, (24, 0, 8, 16)):
        share = out.shape[0]
        begin = row_pos * share
        row, lane = lax.div(begin, LANES), lax.rem(begin, LANES)
        lanes = lax.broadcasted_iota(jnp.int32, (1, LANES), 1)
        for start in range(0, share, LANES):
            length = min(LANES, share - start)
            this = small[pl.ds(first + row + start // LANES, 1), :]
            later = small[pl.ds(first + row + start // LANES + 1, 1), :]
            both = jnp.where(lanes < lane, later, this)
            turned = pltpu.roll(both, lax.rem(LANES - lane, LANES), 1)
            out[start : start + length] = turned.reshape(LANES)[:length]


def whole(memory=pltpu.VMEM):
    return pl.BlockSpec(memory_space=memory)


def no_cost():
    return pl.CostEstimate(flops=0, transcendentals=0, bytes_accessed=0)


def call(body, outs, scratch, in_specs, name, mib):
    return pl.pallas_call(
        body,
        out_shape=outs,
        in_specs=in_specs,
        out_specs=[whole()] * len(outs),
        scratch_shapes=scratch,
        compiler_params=pltpu.CompilerParams(vmem_limit_bytes=mib * MIB),
        cost_estimate=no_cost(),
        name=name,
    )


def after(values, deps):
    return list(lax.optimization_barrier(tuple(values) + tuple(deps))[: len(values)])


def held_like(values):
    return [pltpu.VMEM(value.shape, value.dtype) for value in values]


def sum_rows_kernel(plan, *refs):
    out = refs[-1]
    for table, terms in enumerate(plan):
        total = None
        for which, picks in terms:
            part = refs[which][picks].astype(f32)
            total = part if total is None else total + part
        out[table] = total


def sum_rows(groups, deps):
    arrays = [array for items in groups for array, _ in items]
    plan, count = [], 0
    for items in groups:
        plan.append([(count + at, tuple(picks)) for at, (_, picks) in enumerate(items)])
        count += len(items)
    kept = [pick.stop - pick.start for pick in groups[0][0][1] if isinstance(pick, slice)]
    return call(
        functools.partial(sum_rows_kernel, plan),
        [jax.ShapeDtypeStruct((len(groups), *kept), f32)],
        [],
        [whole()] * len(arrays) + [whole(pl.ANY)] * len(deps),
        "rows",
        24,
    )(*arrays, *deps)[0]


def sum_kernel(plan, n_in, *refs):
    outs = refs[len(refs) - len(plan) :]
    for out, terms in zip(outs, plan):
        rows = out.shape[-2]
        chunk = next(size for size in (64, 48, 80, 32, 16, 8, rows) if rows % size == 0)

        def one_chunk(at, carry, out=out, terms=terms, chunk=chunk):
            window = pl.ds(pl.multiple_of(at * chunk, chunk), chunk)
            for lead in itertools.product(*[range(size) for size in out.shape[:-2]]):
                total = None
                for which, picks in terms:
                    axes, place = iter(lead), []
                    for pick in picks[:-2]:
                        place.append(pick.start + next(axes) if isinstance(pick, slice) else pick)
                    part = refs[which][(*place, window, slice(None))].astype(f32)
                    total = part if total is None else total + part
                out[(*lead, window, slice(None))] = total.astype(out.dtype)
            return carry

        lax.fori_loop(0, rows // chunk, one_chunk, 0)


def take_sums(groups, deps, dtype=bf16):
    arrays, plan, shapes = [], [], []
    for items in groups:
        terms = []
        for array, picks in items:
            found = [at for at, known in enumerate(arrays) if known is array]
            if not found:
                arrays.append(array)
            terms.append((found[0] if found else len(arrays) - 1, tuple(picks)))
        plan.append(terms)
        kept = [pick.stop - pick.start for pick in items[0][1] if isinstance(pick, slice)]
        shapes.append(jax.ShapeDtypeStruct(tuple(kept), dtype))
    return call(
        functools.partial(sum_kernel, plan, len(arrays)),
        shapes,
        [],
        [whole()] * len(arrays) + [whole(pl.ANY)] * len(deps),
        "sums",
        24,
    )(*arrays, *deps)


def local(
    dense_feat,
    pooled,
    labels,
    cross_down,
    cross_up,
    cross_bias,
    w_hidden1,
    bias1,
    w_hidden2,
    bias2,
    w_logit,
    lookup_slots,
):
    n_table = lax.axis_size("table")
    n_row = lax.axis_size("row")
    n_z = n_table // 2
    row_bits = n_row.bit_length() - 1
    z_bits = n_z.bit_length() - 1
    batch, width = dense_feat.shape
    feat, rank = cross_down.shape
    hid = w_hidden1.shape[1]
    tab_grp, _, hot = lookup_slots.shape
    u_shard = batch * n_table * hot // 16

    def swap_cores(value):
        return lax.ppermute(value, "table", [(at, at ^ 1) for at in range(n_table)])

    def swap_z(value, which):
        return lax.ppermute(value, "table", [(at, at ^ (2 * which)) for at in range(n_table)])

    def swap_row(value, bit):
        return lax.ppermute(value, "row", [(at, at ^ (1 << bit)) for at in range(n_row)])

    late = hid // 8
    early = hid // 2 - late
    rows_front = (hid // 2 // LANES) * round_up(hid // n_row, 16)
    rows_front += (early // LANES) * round_up(feat // n_row, 16)
    rows_back = (late // LANES) * round_up(feat // n_row, 16)
    rows_back += (rank // 2 // LANES) * round_up(feat // n_row, 16)
    rows_back += 9 * round_up(rank // n_row, 16) + 48
    rows_front, rows_back = (round_up(rows, 16 * n_z) for rows in (rows_front, rows_back))

    def packed(rows):
        return jax.ShapeDtypeStruct((2, n_row, n_z // 2, rows // n_z, LANES), bf16)

    def wide(*shape):
        return jax.ShapeDtypeStruct(shape, bf16)

    hbm, vmem, anywhere = whole(pltpu.HBM), whole(), whole(pl.ANY)

    sources = (
        dense_feat,
        pooled,
        cross_down,
        cross_up,
        cross_bias,
        w_hidden1,
        bias1,
        w_hidden2,
        bias2,
        w_logit,
        labels,
    )
    send1, keep1, crossed_t, delta_first, small = call(
        front_kernel,
        [packed(rows_front)] * 2
        + [wide(feat, batch), wide(batch, hid), jax.ShapeDtypeStruct((24, LANES), f32)],
        held_like(sources)
        + [
            pltpu.VMEM((2, batch, hid // 2), bf16),
            pltpu.VMEM((2, batch, early), bf16),
            pltpu.SemaphoreType.DMA((len(sources),)),
        ],
        [hbm] * len(sources),
        "front",
        60,
    )(*sources)
    got1 = swap_cores(send1)

    sources = (
        dense_feat,
        pooled,
        cross_down,
        cross_up,
        cross_bias,
        delta_first,
        w_hidden1,
        crossed_t,
        small,
    )
    send2, keep2, *pooled_out = call(
        functools.partial(middle_kernel, n_z),
        [packed(rows_back)] * 2 + [wide(2, tab_grp, batch, width)] * n_z,
        held_like(sources)
        + [
            pltpu.VMEM((n_z, 2, tab_grp, batch, width), bf16),
            pltpu.VMEM((batch, feat), bf16),
            pltpu.VMEM((2, batch, rank // 2), bf16),
            pltpu.VMEM((2, batch, late), bf16),
            pltpu.VMEM((48, LANES), f32),
            pltpu.SemaphoreType.DMA((len(sources),)),
        ],
        [hbm] * len(sources),
        "middle",
        60,
    )(*sources)
    got2 = swap_cores(send2)

    low_first = tuple(range(row_bits))
    high_first = low_first[::-1]

    class Terms:
        def __init__(self, arrays, picks):
            self.items = []
            for array in arrays:
                self.add(array, picks)

        def add(self, array, picks=()):
            whole_axes = [slice(0, size) for size in array.shape[len(picks) :]]
            self.items.append((array, list(picks) + whole_axes))

        def narrowed(self, axis, what):
            items = []
            for array, picks in self.items:
                at = [number for number, pick in enumerate(picks) if isinstance(pick, slice)][axis]
                items.append((array, picks[:at] + [what] + picks[at + 1 :]))
            return items

        def far_near(self, axis, near, far):
            sent = self.narrowed(axis, far)
            self.items = self.narrowed(axis, near)
            return sent

    class Halving(Terms):
        def __init__(self, arrays, order, picks=()):
            dims = len(picks)
            arrays = [
                array.reshape(array.shape[:dims] + (2,) * row_bits + array.shape[dims + 1 :])
                for array in arrays
            ]
            super().__init__(arrays, picks)
            self.order, self.left = order, list(range(row_bits - 1, -1, -1))

        def part(self, at):
            axis = self.left.index(self.order[at])
            self.left.remove(self.order[at])
            return self.far_near(axis, 0, 1)

    def row_step(streams, at, deps):
        sent = take_sums([stream.part(at) for stream in streams], deps)
        for stream, value in zip(streams, sent):
            stream.add(swap_row(value, stream.order[at]))
        return list(sent)

    class Dense:
        def __init__(self, keep, got):
            self.low = Halving([keep, got], low_first, [0])
            self.high = Halving([keep, got], high_first, [1])

        def row_step(self, at, deps):
            deps = [*deps, self.low.items[-1][0], self.high.items[-1][0]]
            return row_step((self.low, self.high), at, deps)

        def z_step(self, stage, deps):
            middle = n_z >> (stage + 1)
            items, deps = self.high.items, [*deps, self.low.items[-1][0]]
            if stage > 0:
                items = self.low.far_near(0, slice(0, middle), slice(middle, 2 * middle))
            (sent,) = take_sums([items], deps)
            self.low.add(swap_z(sent, 1 << stage))
            return [sent]

        def z_own(self, deps):
            (self.own,) = take_sums([self.low.items], deps)
            self.back = swap_z(self.own, 1 << (z_bits - 1)) if z_bits > 1 else None
            return [self.own]

        def z_back(self, deps):
            for stage in range(z_bits - 1, 0, -1):
                if stage < z_bits - 1:
                    self.back = swap_z(self.own, 1 << stage)
                (back,) = after([self.back], deps)
                self.own = jnp.concatenate([self.own, back], axis=0)
            far = swap_z(self.own, 1)
            self.pieces = [self.own, far, swap_cores(self.own), swap_cores(far)]
            return [self.own]

    one, two = Dense(keep1, got1), Dense(keep2, got2)
    one.row_step(0, [keep2])
    values, chain = {0: pooled_out[0]}, [n_z // 2]
    chain += [which for which in range(n_z - 1, 0, -1) if which != n_z // 2]
    for at, which in enumerate(chain):
        moved = pooled_out[which]
        if at > 0:
            (moved,) = after([moved], [values[chain[at - 1]]])
        values[which] = swap_z(moved, which)
    last = [values[chain[0]]]
    for at in range(1, row_bits):
        last = one.row_step(at, last)
    last = two.row_step(0, last)
    last = one.z_step(0, last)
    for stage in range(1, z_bits):
        last = one.z_step(stage, last)
    last = [*last, values[chain[min(1, len(chain) - 1)]]]
    for at in range(1, row_bits):
        last = two.row_step(at, last)
    values = [values[which] for which in range(n_z)]
    far_values = call(
        functools.partial(select_kernel, n_z),
        [wide(n_z // 2, tab_grp, batch, width)] * 2,
        [],
        [vmem] * n_z + [anywhere],
        "select",
        8,
    )(*values, last[0])
    values += [swap_cores(value) for value in far_values]
    slots = jnp.transpose(lookup_slots, (0, 2, 1))
    last, shares = [far_values[0]], []
    for table in range(tab_grp):
        sums = pl.pallas_call(
            functools.partial(count_kernel, n_row, table, hot, n_z),
            out_shape=wide(n_row, u_shard, width),
            grid=(n_row,),
            in_specs=[vmem] * (3 + n_z) + [anywhere],
            out_specs=pl.BlockSpec((1, u_shard, width), lambda at: (at, 0, 0)),
            compiler_params=pltpu.CompilerParams(vmem_limit_bytes=16 * MIB),
            cost_estimate=no_cost(),
            name="counts",
        )(slots, *values, last[0])
        shares.append(Halving([sums], high_first if table % 2 else low_first))
        last = [sums]
        if table == 0:
            last = two.z_step(0, last)
    last = one.z_own(last)
    last = row_step(shares, 0, last)
    for stage in range(1, z_bits):
        last = two.z_step(stage, last)
    for at in range(1, row_bits):
        last = row_step(shares, at, last)
    last = two.z_own(last)
    last = one.z_back(last)
    row_grads = sum_rows([share.items for share in shares], last)
    two.z_back([row_grads])

    g_down, g_up, g_first, g_second, g_cbias, g_bias1, g_bias2, g_logit = call(
        unpack_kernel,
        [
            jax.ShapeDtypeStruct((feat // n_row, rank), f32),
            jax.ShapeDtypeStruct((rank // n_row, feat), f32),
            jax.ShapeDtypeStruct((feat // n_row, hid), f32),
            jax.ShapeDtypeStruct((hid // n_row, hid), f32),
            jax.ShapeDtypeStruct((feat // n_row,), f32),
        ]
        + [jax.ShapeDtypeStruct((hid // n_row,), f32)] * 3,
        [pltpu.VMEM((2, rows, LANES), bf16) for rows in (rows_front, rows_back)]
        + [pltpu.VMEM((56, LANES), f32)],
        [vmem] * 8,
        "unpack",
        24,
    )(*one.pieces, *two.pieces)
    return (row_grads, g_down, g_up, g_cbias, g_first, g_bias1, g_second, g_bias2, g_logit)


def solution(mesh):
    in_specs = (
        P(("table", "row"), None),
        P(("table", "row"), None),
        P(("table", "row")),
        P(),
        P(),
        P(),
        P(),
        P(),
        P(),
        P(),
        P(),
        P("table", None, None),
    )
    out_specs = (
        P("table", "row", None),
        P("row", None),
        P("row", None),
        P("row"),
        P("row", None),
        P("row"),
        P("row", None),
        P("row"),
        P("row"),
    )
    return jax.shard_map(local, mesh=mesh, in_specs=in_specs, out_specs=out_specs, check_vma=False)
```

```python
import functools
import itertools

import jax
import jax.numpy as jnp
from jax import lax
from jax.experimental import pallas as pl
from jax.experimental.pallas import tpu as pltpu
from jax.sharding import PartitionSpec as P

loss_scale = 16.0
LANES = 128
SPAN = 9 * LANES
MIB = 1024 * 1024
bf16 = jnp.bfloat16
f32 = jnp.float32


def round_up(value, unit):
    return -(-value // unit) * unit


def matmul(left, right):
    return jnp.dot(left, right, preferred_element_type=f32)


def matmul_rt(left, right):
    return lax.dot_general(left, right, (((1,), (1,)), ((), ())), preferred_element_type=f32)


def reverse_bits(value, bits):
    out = 0
    for bit in range(bits):
        out = out | (((value >> bit) & 1) << (bits - 1 - bit))
    return out


def places_of(z_pos, n_z):
    bits = n_z.bit_length() - 1
    return [reverse_bits(z_pos ^ quarter, bits) for quarter in range(n_z)]


def put_blocks(ref, row_pos, places, offset, value):
    shards, n_half, rows_q = ref.shape[1], ref.shape[2], ref.shape[3]
    rows = value.shape[0] // shards
    step = round_up(rows, 16)
    blocks = value.shape[1] // LANES
    for shard in range(shards):
        slot = shard ^ row_pos
        for block in range(blocks):
            done = 0
            while done < rows:
                quarter, at = divmod(offset + block * step + done, rows_q)
                length = min(rows - done, rows_q - at)
                place = places[quarter]
                ref[lax.div(place, n_half), slot, lax.rem(place, n_half), at : at + length, :] = value[
                    shard * rows + done : shard * rows + done + length,
                    block * LANES : (block + 1) * LANES,
                ].astype(ref.dtype)
                done += length
    return offset + blocks * step


def put_rows(ref, offset, value):
    for block in range(value.shape[1] // LANES):
        ref[offset + block : offset + block + 1, :] = value[:, block * LANES : (block + 1) * LANES]


def position():
    table_pos = lax.axis_index("table")
    return lax.rem(table_pos, 2), lax.axis_index("row"), table_pos


class Loads:
    def __init__(self, sources, targets, sems):
        self.copies = [
            pltpu.make_async_copy(source, target, sems.at[at])
            for at, (source, target) in enumerate(zip(sources, targets))
        ]
        self.targets = targets
        self.ready = set()
        for copy in self.copies:
            copy.start()

    def __call__(self, at):
        if at not in self.ready:
            self.copies[at].wait()
            self.ready.add(at)
        return self.targets[at][...]


def as_row(value):
    return value.reshape(1, value.shape[-1])


def front_kernel(*refs):
    sources, outs, targets = refs[:11], refs[11:16], refs[16:27]
    halves, thirds, sems = refs[27:]
    send, keep, crossed_t_out, first_out, small = outs
    load = Loads(sources, targets, sems)
    core, row_pos, table_pos = position()
    places = places_of(lax.div(table_pos, 2), 2 * send.shape[2])
    stacked = jnp.concatenate([load(0), load(1)], axis=1)
    cross_down = load(2)
    reduced = matmul(stacked, cross_down).astype(bf16)
    widened = matmul(reduced, load(3)) + as_row(load(4))
    wide = stacked.astype(f32)
    crossed = (wide * widened + wide).astype(bf16)
    pre_first = matmul(crossed, load(5)) + as_row(load(6))
    sig_first = jax.nn.sigmoid(pre_first)
    act_first = (pre_first * sig_first).astype(bf16)
    slope_first = sig_first * (1.0 + pre_first * (1.0 - sig_first))
    w_hidden2 = load(7)
    pre_second = matmul(act_first, w_hidden2) + as_row(load(8))
    sig_second = jax.nn.sigmoid(pre_second)
    act_second = (pre_second * sig_second).astype(bf16).astype(f32)
    slope_second = sig_second * (1.0 + pre_second * (1.0 - sig_second))
    w_logit = as_row(load(9))
    logits = jnp.sum(act_second * w_logit, axis=1, keepdims=True)
    labels = as_row(load(10))
    count = labels.shape[1]
    same = lax.broadcasted_iota(jnp.int32, (count, count), 0) == lax.broadcasted_iota(
        jnp.int32, (count, count), 1
    )
    label_col = jnp.sum(jnp.where(same, labels.astype(f32), 0.0), axis=1, keepdims=True)
    delta_logit = loss_scale * (jax.nn.sigmoid(logits) - label_col)
    delta_second = (delta_logit * w_logit * slope_second).astype(bf16)
    put_rows(small, 16, jnp.sum(act_second * delta_logit, axis=0, keepdims=True))
    put_rows(small, 8, jnp.sum(delta_second.astype(f32), axis=0, keepdims=True))
    half = halves.shape[2]
    halves[0] = delta_second[:, :half]
    halves[1] = delta_second[:, half:]
    delta_first = (matmul_rt(delta_second, w_hidden2) * slope_first).astype(bf16)
    first_out[...] = delta_first
    put_rows(small, 0, jnp.sum(delta_first.astype(f32), axis=0, keepdims=True))
    part = thirds.shape[2]
    thirds[0] = delta_first[:, :part]
    thirds[1] = delta_first[:, half : half + part]
    act_t = act_first.T
    crossed_t = crossed.T
    crossed_t_out[...] = crossed_t
    for ref, who in ((send, 1 - core), (keep, core)):
        offset = put_blocks(ref, row_pos, places, 0, matmul(act_t, halves[who]))
        put_blocks(ref, row_pos, places, offset, matmul(crossed_t, thirds[who]))


def middle_kernel(n_z, *refs):
    sources, send, keep = refs[:9], refs[9], refs[10]
    pooled_outs = refs[11 : 11 + n_z]
    rest = refs[11 + n_z :]
    targets = rest[:9]
    by_group, wide_delta, half_delta, sixths, small, sems = rest[9:]
    load = Loads(sources, targets, sems)
    core, row_pos, table_pos = position()
    z_pos = lax.div(table_pos, 2)
    places = places_of(z_pos, 2 * send.shape[2])
    stacked = jnp.concatenate([load(0), load(1)], axis=1)
    cross_down = load(2)
    reduced = matmul(stacked, cross_down).astype(bf16)
    cross_up = load(3)
    widened = matmul(reduced, cross_up) + as_row(load(4))
    delta_first = load(5)
    delta_crossed = matmul_rt(delta_first, load(6))
    delta_widened = (delta_crossed * stacked.astype(f32)).astype(bf16)
    wide_delta[...] = delta_widened
    delta_reduced = matmul_rt(delta_widened, cross_up).astype(bf16)
    delta_stacked = delta_crossed * (widened + 1.0) + matmul_rt(delta_reduced, cross_down)
    width = targets[0].shape[1]
    per_group = by_group.shape[2]
    for table in range(2 * n_z * per_group):
        group = table // per_group
        by_group[group // 2, group % 2, table % per_group] = delta_stacked[
            :, width * (table + 1) : width * (table + 2)
        ].astype(bf16)
    for which in range(n_z):
        pooled_outs[which][0] = by_group[z_pos ^ which, core]
        pooled_outs[which][1] = by_group[z_pos ^ which, 1 - core]

    n_row, rank, feat = send.shape[1], delta_reduced.shape[1], delta_widened.shape[1]
    hid = delta_first.shape[1]
    part = hid // 2 - sixths.shape[2]
    half_delta[0] = delta_reduced[:, : rank // 2]
    half_delta[1] = delta_reduced[:, rank // 2 :]
    sixths[0] = delta_first[:, part : hid // 2]
    sixths[1] = delta_first[:, hid // 2 + part :]
    put_rows(small, 24, jnp.sum(delta_widened.astype(f32), axis=0, keepdims=True))
    small[0:24, :] = load(8)
    small[41:48, :] = jnp.zeros((7, LANES), f32)
    sums = jnp.concatenate([small[...]] * n_row, axis=0)
    crossed_t, reduced_t, stacked_t = load(7), reduced.T, stacked.T
    for ref, who in ((send, 1 - core), (keep, core)):
        offset = put_blocks(ref, row_pos, places, 0, matmul(crossed_t, sixths[who]))
        offset = put_blocks(ref, row_pos, places, offset, matmul(stacked_t, half_delta[who]))
        start = pl.multiple_of(who * (feat - SPAN), LANES)
        offset = put_blocks(
            ref, row_pos, places, offset, matmul(reduced_t, wide_delta[:, pl.ds(start, SPAN)])
        )
        offset = put_blocks(ref, row_pos, places, offset, sums)
        tail = 2 * ref.shape[2] * ref.shape[3] - offset
        if tail:
            put_blocks(ref, row_pos, places, offset, jnp.zeros((n_row * tail, LANES), f32))


def select_kernel(n_z, *refs):
    for which in range(n_z):
        out = refs[len(refs) - 2 + which // (n_z // 2)]
        out[which % (n_z // 2)] = refs[which][1]


def count_kernel(n_row, table, hot, n_z, slots, *rest):
    direct, crossed, out = rest[:n_z], rest[n_z : n_z + 2], rest[-1]
    near = n_z // 2
    block = out.shape[1]
    samples = crossed[0].shape[2]
    core, row_pos, table_pos = position()
    z_pos = lax.div(table_pos, 2)
    base = (pl.program_id(0) ^ row_pos) * block
    names = lax.broadcasted_iota(jnp.int16, (block, samples), 0)
    total = jnp.zeros((block, out.shape[2]), f32)
    one = jnp.ones((block, samples), bf16)
    zero = jnp.zeros((block, samples), bf16)
    for which in range(n_z):
        far = crossed[which // near]
        for held, who in ((direct[which][0, table], core), (far[which % near, table], 1 - core)):
            source = 2 * (z_pos ^ which) + who
            start = pl.multiple_of((source * n_row + row_pos) * samples, LANES)
            lines = slots[table, :, pl.ds(start, samples)] - base
            lines = jnp.where((lines >= 0) & (lines < block), lines, block).astype(jnp.int16)
            counts = zero
            for look in range(hot):
                line = jnp.broadcast_to(lines[look : look + 1, :], (block, samples))
                counts = counts + jnp.where(line == names, one, zero)
            total = total + matmul(counts, held)
    out[0] = total.astype(out.dtype)


def unpack_kernel(*refs):
    parts = refs[0:8]
    g_down, g_up, g_first, g_second = refs[8:12]
    small_outs = refs[12:16]
    held, small = refs[16:18], refs[18]
    core, row_pos, table_pos = position()
    z_pos = lax.div(table_pos, 2)
    for stream in range(2):
        lower, upper, lower_other, upper_other = parts[4 * stream : 4 * stream + 4]
        ref = held[stream]
        rows = lower.shape[1]
        n_z = 2 * lower.shape[0]
        z_bits = n_z.bit_length() - 1
        for who, pieces in ((core, (lower, upper)), (1 - core, (lower_other, upper_other))):
            for place in range(n_z):
                start = pl.multiple_of((reverse_bits(place, z_bits) ^ z_pos) * rows, 16)
                ref[who, pl.ds(start, rows), :] = pieces[place // (n_z // 2)][place % (n_z // 2)]
    front, back = held

    def take(ref, out, half, offset, columns):
        rows = out.shape[0]
        step = round_up(rows, 16)
        for column in columns:
            out[:, column * LANES : (column + 1) * LANES] = ref[
                half, offset : offset + rows, :
            ].astype(f32)
            offset += step
        return offset

    for half in range(2):
        blocks = g_second.shape[1] // LANES // 2
        offset = take(front, g_second, half, 0, range(half * blocks, (half + 1) * blocks))
        blocks = g_first.shape[1] // LANES // 2
        early = blocks - blocks // 4
        take(front, g_first, half, offset, range(half * blocks, half * blocks + early))
        offset = take(back, g_first, half, 0, range(half * blocks + early, (half + 1) * blocks))
        blocks = g_down.shape[1] // LANES // 2
        offset = take(back, g_down, half, offset, range(half * blocks, (half + 1) * blocks))
        blocks = g_up.shape[1] // LANES
        offset = take(back, g_up, half, offset, range(half * (blocks - 9), half * (blocks - 9) + 9))
    small[0:48, :] = back[0, offset : offset + 48, :].astype(f32)
    small[48:, :] = jnp.zeros((small.shape[0] - 48, LANES), f32)
    for out, first in zip(small_outs, (24, 0, 8, 16)):
        share = out.shape[0]
        begin = row_pos * share
        row, lane = lax.div(begin, LANES), lax.rem(begin, LANES)
        lanes = lax.broadcasted_iota(jnp.int32, (1, LANES), 1)
        for start in range(0, share, LANES):
            length = min(LANES, share - start)
            this = small[pl.ds(first + row + start // LANES, 1), :]
            later = small[pl.ds(first + row + start // LANES + 1, 1), :]
            both = jnp.where(lanes < lane, later, this)
            turned = pltpu.roll(both, lax.rem(LANES - lane, LANES), 1)
            out[start : start + length] = turned.reshape(LANES)[:length]


def whole(memory=pltpu.VMEM):
    return pl.BlockSpec(memory_space=memory)


def no_cost():
    return pl.CostEstimate(flops=0, transcendentals=0, bytes_accessed=0)


def call(body, outs, scratch, in_specs, name, mib):
    return pl.pallas_call(
        body,
        out_shape=outs,
        in_specs=in_specs,
        out_specs=[whole()] * len(outs),
        scratch_shapes=scratch,
        compiler_params=pltpu.CompilerParams(vmem_limit_bytes=mib * MIB),
        cost_estimate=no_cost(),
        name=name,
    )


def after(values, deps):
    return list(lax.optimization_barrier(tuple(values) + tuple(deps))[: len(values)])


def held_like(values):
    return [pltpu.VMEM(value.shape, value.dtype) for value in values]


def sum_rows_kernel(plan, *refs):
    out = refs[-1]
    for table, terms in enumerate(plan):
        total = None
        for which, picks in terms:
            part = refs[which][picks].astype(f32)
            total = part if total is None else total + part
        out[table] = total


def sum_rows(groups, deps):
    arrays = [array for items in groups for array, _ in items]
    plan, count = [], 0
    for items in groups:
        plan.append([(count + at, tuple(picks)) for at, (_, picks) in enumerate(items)])
        count += len(items)
    kept = [pick.stop - pick.start for pick in groups[0][0][1] if isinstance(pick, slice)]
    return call(
        functools.partial(sum_rows_kernel, plan),
        [jax.ShapeDtypeStruct((len(groups), *kept), f32)],
        [],
        [whole()] * len(arrays) + [whole(pl.ANY)] * len(deps),
        "rows",
        24,
    )(*arrays, *deps)[0]


def sum_kernel(plan, n_in, *refs):
    outs = refs[len(refs) - len(plan) :]
    for out, terms in zip(outs, plan):
        rows = out.shape[-2]
        chunk = next(size for size in (64, 48, 80, 32, 16, 8, rows) if rows % size == 0)

        def one_chunk(at, carry, out=out, terms=terms, chunk=chunk):
            window = pl.ds(pl.multiple_of(at * chunk, chunk), chunk)
            for lead in itertools.product(*[range(size) for size in out.shape[:-2]]):
                total = None
                for which, picks in terms:
                    axes, place = iter(lead), []
                    for pick in picks[:-2]:
                        place.append(pick.start + next(axes) if isinstance(pick, slice) else pick)
                    part = refs[which][(*place, window, slice(None))].astype(f32)
                    total = part if total is None else total + part
                out[(*lead, window, slice(None))] = total.astype(out.dtype)
            return carry

        lax.fori_loop(0, rows // chunk, one_chunk, 0)


def take_sums(groups, deps, dtype=bf16):
    arrays, plan, shapes = [], [], []
    for items in groups:
        terms = []
        for array, picks in items:
            found = [at for at, known in enumerate(arrays) if known is array]
            if not found:
                arrays.append(array)
            terms.append((found[0] if found else len(arrays) - 1, tuple(picks)))
        plan.append(terms)
        kept = [pick.stop - pick.start for pick in items[0][1] if isinstance(pick, slice)]
        shapes.append(jax.ShapeDtypeStruct(tuple(kept), dtype))
    return call(
        functools.partial(sum_kernel, plan, len(arrays)),
        shapes,
        [],
        [whole()] * len(arrays) + [whole(pl.ANY)] * len(deps),
        "sums",
        24,
    )(*arrays, *deps)


def local(
    dense_feat,
    pooled,
    labels,
    cross_down,
    cross_up,
    cross_bias,
    w_hidden1,
    bias1,
    w_hidden2,
    bias2,
    w_logit,
    lookup_slots,
):
    n_table = lax.axis_size("table")
    n_row = lax.axis_size("row")
    n_z = n_table // 2
    row_bits = n_row.bit_length() - 1
    z_bits = n_z.bit_length() - 1
    batch, width = dense_feat.shape
    feat, rank = cross_down.shape
    hid = w_hidden1.shape[1]
    tab_grp, _, hot = lookup_slots.shape
    u_shard = batch * n_table * hot // 16

    def swap_cores(value):
        return lax.ppermute(value, "table", [(at, at ^ 1) for at in range(n_table)])

    def swap_z(value, which):
        return lax.ppermute(value, "table", [(at, at ^ (2 * which)) for at in range(n_table)])

    def swap_row(value, bit):
        return lax.ppermute(value, "row", [(at, at ^ (1 << bit)) for at in range(n_row)])

    late = hid // 8
    early = hid // 2 - late
    rows_front = (hid // 2 // LANES) * round_up(hid // n_row, 16)
    rows_front += (early // LANES) * round_up(feat // n_row, 16)
    rows_back = (late // LANES) * round_up(feat // n_row, 16)
    rows_back += (rank // 2 // LANES) * round_up(feat // n_row, 16)
    rows_back += 9 * round_up(rank // n_row, 16) + 48
    rows_front, rows_back = (round_up(rows, 16 * n_z) for rows in (rows_front, rows_back))

    def packed(rows):
        return jax.ShapeDtypeStruct((2, n_row, n_z // 2, rows // n_z, LANES), bf16)

    def wide(*shape):
        return jax.ShapeDtypeStruct(shape, bf16)

    hbm, vmem, anywhere = whole(pltpu.HBM), whole(), whole(pl.ANY)

    sources = (
        dense_feat,
        pooled,
        cross_down,
        cross_up,
        cross_bias,
        w_hidden1,
        bias1,
        w_hidden2,
        bias2,
        w_logit,
        labels,
    )
    send1, keep1, crossed_t, delta_first, small = call(
        front_kernel,
        [packed(rows_front)] * 2
        + [wide(feat, batch), wide(batch, hid), jax.ShapeDtypeStruct((24, LANES), f32)],
        held_like(sources)
        + [
            pltpu.VMEM((2, batch, hid // 2), bf16),
            pltpu.VMEM((2, batch, early), bf16),
            pltpu.SemaphoreType.DMA((len(sources),)),
        ],
        [hbm] * len(sources),
        "front",
        60,
    )(*sources)
    got1 = swap_cores(send1)

    sources = (
        dense_feat,
        pooled,
        cross_down,
        cross_up,
        cross_bias,
        delta_first,
        w_hidden1,
        crossed_t,
        small,
    )
    send2, keep2, *pooled_out = call(
        functools.partial(middle_kernel, n_z),
        [packed(rows_back)] * 2 + [wide(2, tab_grp, batch, width)] * n_z,
        held_like(sources)
        + [
            pltpu.VMEM((n_z, 2, tab_grp, batch, width), bf16),
            pltpu.VMEM((batch, feat), bf16),
            pltpu.VMEM((2, batch, rank // 2), bf16),
            pltpu.VMEM((2, batch, late), bf16),
            pltpu.VMEM((48, LANES), f32),
            pltpu.SemaphoreType.DMA((len(sources),)),
        ],
        [hbm] * len(sources),
        "middle",
        60,
    )(*sources)
    got2 = swap_cores(send2)

    low_first = tuple(range(row_bits))
    high_first = low_first[::-1]

    class Terms:
        def __init__(self, arrays, picks):
            self.items = []
            for array in arrays:
                self.add(array, picks)

        def add(self, array, picks=()):
            whole_axes = [slice(0, size) for size in array.shape[len(picks) :]]
            self.items.append((array, list(picks) + whole_axes))

        def narrowed(self, axis, what):
            items = []
            for array, picks in self.items:
                at = [number for number, pick in enumerate(picks) if isinstance(pick, slice)][axis]
                items.append((array, picks[:at] + [what] + picks[at + 1 :]))
            return items

        def far_near(self, axis, near, far):
            sent = self.narrowed(axis, far)
            self.items = self.narrowed(axis, near)
            return sent

    class Halving(Terms):
        def __init__(self, arrays, order, picks=()):
            dims = len(picks)
            arrays = [
                array.reshape(array.shape[:dims] + (2,) * row_bits + array.shape[dims + 1 :])
                for array in arrays
            ]
            super().__init__(arrays, picks)
            self.order, self.left = order, list(range(row_bits - 1, -1, -1))

        def part(self, at):
            axis = self.left.index(self.order[at])
            self.left.remove(self.order[at])
            return self.far_near(axis, 0, 1)

    def row_step(streams, at, deps):
        sent = take_sums([stream.part(at) for stream in streams], deps)
        for stream, value in zip(streams, sent):
            stream.add(swap_row(value, stream.order[at]))
        return list(sent)

    class Dense:
        def __init__(self, keep, got):
            self.low = Halving([keep, got], low_first, [0])
            self.high = Halving([keep, got], high_first, [1])

        def row_step(self, at, deps):
            if at > 0:
                deps = [*deps, self.low.items[-1][0], self.high.items[-1][0]]
            return row_step((self.low, self.high), at, deps)

        def z_step(self, stage, deps):
            middle = n_z >> (stage + 1)
            items, deps = self.high.items, [*deps, self.low.items[-1][0]]
            if stage > 0:
                items = self.low.far_near(0, slice(0, middle), slice(middle, 2 * middle))
            (sent,) = take_sums([items], deps)
            self.low.add(swap_z(sent, 1 << stage))
            return [sent]

        def z_own(self, deps):
            (self.own,) = take_sums([self.low.items], deps)
            self.back = swap_z(self.own, 1 << (z_bits - 1)) if z_bits > 1 else None
            return [self.own]

        def z_back(self, deps):
            for stage in range(z_bits - 1, 0, -1):
                if stage < z_bits - 1:
                    self.back = swap_z(self.own, 1 << stage)
                (back,) = after([self.back], deps)
                self.own = jnp.concatenate([self.own, back], axis=0)
            far = swap_z(self.own, 1)
            self.pieces = [self.own, far, swap_cores(self.own), swap_cores(far)]
            return [self.own]

    (got1,) = after([got1], [pooled_out[0]])
    one, two = Dense(keep1, got1), Dense(keep2, got2)
    one.row_step(0, [])
    values, half = {0: pooled_out[0]}, n_z // 2
    for which in [half, *range(1, half)]:
        values[which] = swap_z(pooled_out[which], which)
    for which in range(half + 1, n_z):
        (moved,) = after([pooled_out[which]], [values[half], values[which - half]])
        values[which] = swap_z(moved, which)
    last = [values[which] for which in range(1, half + 1)]
    for at in range(1, row_bits):
        last = one.row_step(at, last)
    last = two.row_step(0, last)
    last = one.z_step(0, last)
    values = [values[which] for which in range(n_z)]
    far_values = call(
        functools.partial(select_kernel, n_z),
        [wide(n_z // 2, tab_grp, batch, width)] * 2,
        [],
        [vmem] * n_z + [anywhere],
        "select",
        8,
    )(*values, last[0])
    values += [swap_cores(value) for value in far_values]
    slots = jnp.transpose(lookup_slots, (0, 2, 1))
    last, shares = [far_values[0]], []
    for table in range(tab_grp):
        sums = pl.pallas_call(
            functools.partial(count_kernel, n_row, table, hot, n_z),
            out_shape=wide(n_row, u_shard, width),
            grid=(n_row,),
            in_specs=[vmem] * (3 + n_z) + [anywhere],
            out_specs=pl.BlockSpec((1, u_shard, width), lambda at: (at, 0, 0)),
            compiler_params=pltpu.CompilerParams(vmem_limit_bytes=16 * MIB),
            cost_estimate=no_cost(),
            name="counts",
        )(slots, *values, last[0])
        shares.append(Halving([sums], high_first if table % 2 else low_first))
        last = [sums]
        if table == 0:
            for at in range(1, row_bits):
                last = two.row_step(at, last)
            for stage in range(1, z_bits):
                last = one.z_step(stage, last)
            last = two.z_step(0, last)
    last = row_step(shares, 0, last)
    last = one.z_own(last)
    for stage in range(1, z_bits):
        last = two.z_step(stage, last)
    for at in range(1, row_bits):
        last = row_step(shares, at, last)
    last = two.z_own(last)
    last = one.z_back(last)
    row_grads = sum_rows([share.items for share in shares], last)
    two.z_back([row_grads])

    g_down, g_up, g_first, g_second, g_cbias, g_bias1, g_bias2, g_logit = call(
        unpack_kernel,
        [
            jax.ShapeDtypeStruct((feat // n_row, rank), f32),
            jax.ShapeDtypeStruct((rank // n_row, feat), f32),
            jax.ShapeDtypeStruct((feat // n_row, hid), f32),
            jax.ShapeDtypeStruct((hid // n_row, hid), f32),
            jax.ShapeDtypeStruct((feat // n_row,), f32),
        ]
        + [jax.ShapeDtypeStruct((hid // n_row,), f32)] * 3,
        [pltpu.VMEM((2, rows, LANES), bf16) for rows in (rows_front, rows_back)]
        + [pltpu.VMEM((56, LANES), f32)],
        [vmem] * 8,
        "unpack",
        24,
    )(*one.pieces, *two.pieces)
    return (row_grads, g_down, g_up, g_cbias, g_first, g_bias1, g_second, g_bias2, g_logit)


def solution(mesh):
    in_specs = (
        P(("table", "row"), None),
        P(("table", "row"), None),
        P(("table", "row")),
        P(),
        P(),
        P(),
        P(),
        P(),
        P(),
        P(),
        P(),
        P("table", None, None),
    )
    out_specs = (
        P("table", "row", None),
        P("row", None),
        P("row", None),
        P("row"),
        P("row", None),
        P("row"),
        P("row", None),
        P("row"),
        P("row"),
    )
    return jax.shard_map(local, mesh=mesh, in_specs=in_specs, out_specs=out_specs, check_vma=False)
```

```python
import functools
import itertools

import jax
import jax.numpy as jnp
from jax import lax
from jax.experimental import pallas as pl
from jax.experimental.pallas import tpu as pltpu
from jax.sharding import PartitionSpec as P

loss_scale = 16.0
LANES = 128
SPAN = 9 * LANES
MIB = 1024 * 1024
bf16 = jnp.bfloat16
f32 = jnp.float32


def round_up(value, unit):
    return -(-value // unit) * unit


def matmul(left, right):
    return jnp.dot(left, right, preferred_element_type=f32)


def matmul_rt(left, right):
    return lax.dot_general(left, right, (((1,), (1,)), ((), ())), preferred_element_type=f32)


def reverse_bits(value, bits):
    out = 0
    for bit in range(bits):
        out = out | (((value >> bit) & 1) << (bits - 1 - bit))
    return out


def places_of(z_pos, n_z):
    bits = n_z.bit_length() - 1
    return [reverse_bits(z_pos ^ quarter, bits) for quarter in range(n_z)]


def put_blocks(ref, row_pos, places, offset, value):
    shards, n_half, rows_q = ref.shape[1], ref.shape[2], ref.shape[3]
    rows = value.shape[0] // shards
    step = round_up(rows, 16)
    blocks = value.shape[1] // LANES
    for shard in range(shards):
        slot = shard ^ row_pos
        for block in range(blocks):
            done = 0
            while done < rows:
                quarter, at = divmod(offset + block * step + done, rows_q)
                length = min(rows - done, rows_q - at)
                place = places[quarter]
                ref[lax.div(place, n_half), slot, lax.rem(place, n_half), at : at + length, :] = value[
                    shard * rows + done : shard * rows + done + length,
                    block * LANES : (block + 1) * LANES,
                ].astype(ref.dtype)
                done += length
    return offset + blocks * step


def put_rows(ref, offset, value):
    for block in range(value.shape[1] // LANES):
        ref[offset + block : offset + block + 1, :] = value[:, block * LANES : (block + 1) * LANES]


def position():
    table_pos = lax.axis_index("table")
    return lax.rem(table_pos, 2), lax.axis_index("row"), table_pos


class Loads:
    def __init__(self, sources, targets, sems):
        self.copies = [
            pltpu.make_async_copy(source, target, sems.at[at])
            for at, (source, target) in enumerate(zip(sources, targets))
        ]
        self.targets = targets
        self.ready = set()
        for copy in self.copies:
            copy.start()

    def __call__(self, at):
        if at not in self.ready:
            self.copies[at].wait()
            self.ready.add(at)
        return self.targets[at][...]


def as_row(value):
    return value.reshape(1, value.shape[-1])


def front_kernel(*refs):
    sources, outs, targets = refs[:11], refs[11:16], refs[16:27]
    halves, thirds, sems = refs[27:]
    send, keep, crossed_t_out, first_out, small = outs
    load = Loads(sources, targets, sems)
    core, row_pos, table_pos = position()
    places = places_of(lax.div(table_pos, 2), 2 * send.shape[2])
    stacked = jnp.concatenate([load(0), load(1)], axis=1)
    cross_down = load(2)
    reduced = matmul(stacked, cross_down).astype(bf16)
    widened = matmul(reduced, load(3)) + as_row(load(4))
    wide = stacked.astype(f32)
    crossed = (wide * widened + wide).astype(bf16)
    pre_first = matmul(crossed, load(5)) + as_row(load(6))
    sig_first = jax.nn.sigmoid(pre_first)
    act_first = (pre_first * sig_first).astype(bf16)
    slope_first = sig_first * (1.0 + pre_first * (1.0 - sig_first))
    w_hidden2 = load(7)
    pre_second = matmul(act_first, w_hidden2) + as_row(load(8))
    sig_second = jax.nn.sigmoid(pre_second)
    act_second = (pre_second * sig_second).astype(bf16).astype(f32)
    slope_second = sig_second * (1.0 + pre_second * (1.0 - sig_second))
    w_logit = as_row(load(9))
    logits = jnp.sum(act_second * w_logit, axis=1, keepdims=True)
    labels = as_row(load(10))
    count = labels.shape[1]
    same = lax.broadcasted_iota(jnp.int32, (count, count), 0) == lax.broadcasted_iota(
        jnp.int32, (count, count), 1
    )
    label_col = jnp.sum(jnp.where(same, labels.astype(f32), 0.0), axis=1, keepdims=True)
    delta_logit = loss_scale * (jax.nn.sigmoid(logits) - label_col)
    delta_second = (delta_logit * w_logit * slope_second).astype(bf16)
    put_rows(small, 16, jnp.sum(act_second * delta_logit, axis=0, keepdims=True))
    put_rows(small, 8, jnp.sum(delta_second.astype(f32), axis=0, keepdims=True))
    half = halves.shape[2]
    halves[0] = delta_second[:, :half]
    halves[1] = delta_second[:, half:]
    delta_first = (matmul_rt(delta_second, w_hidden2) * slope_first).astype(bf16)
    first_out[...] = delta_first
    put_rows(small, 0, jnp.sum(delta_first.astype(f32), axis=0, keepdims=True))
    part = thirds.shape[2]
    thirds[0] = delta_first[:, :part]
    thirds[1] = delta_first[:, half : half + part]
    act_t = act_first.T
    crossed_t = crossed.T
    crossed_t_out[...] = crossed_t
    for ref, who in ((send, 1 - core), (keep, core)):
        offset = put_blocks(ref, row_pos, places, 0, matmul(act_t, halves[who]))
        put_blocks(ref, row_pos, places, offset, matmul(crossed_t, thirds[who]))


def middle_kernel(n_z, *refs):
    sources, send, keep = refs[:9], refs[9], refs[10]
    pooled_outs = refs[11 : 11 + n_z]
    rest = refs[11 + n_z :]
    targets = rest[:9]
    by_group, wide_delta, half_delta, sixths, small, sems = rest[9:]
    load = Loads(sources, targets, sems)
    core, row_pos, table_pos = position()
    z_pos = lax.div(table_pos, 2)
    places = places_of(z_pos, 2 * send.shape[2])
    stacked = jnp.concatenate([load(0), load(1)], axis=1)
    cross_down = load(2)
    reduced = matmul(stacked, cross_down).astype(bf16)
    cross_up = load(3)
    widened = matmul(reduced, cross_up) + as_row(load(4))
    delta_first = load(5)
    delta_crossed = matmul_rt(delta_first, load(6))
    delta_widened = (delta_crossed * stacked.astype(f32)).astype(bf16)
    wide_delta[...] = delta_widened
    delta_reduced = matmul_rt(delta_widened, cross_up).astype(bf16)
    delta_stacked = delta_crossed * (widened + 1.0) + matmul_rt(delta_reduced, cross_down)
    width = targets[0].shape[1]
    per_group = by_group.shape[2]
    for table in range(2 * n_z * per_group):
        group = table // per_group
        by_group[group // 2, group % 2, table % per_group] = delta_stacked[
            :, width * (table + 1) : width * (table + 2)
        ].astype(bf16)
    for which in range(n_z):
        pooled_outs[which][0] = by_group[z_pos ^ which, core]
        pooled_outs[which][1] = by_group[z_pos ^ which, 1 - core]

    n_row, rank, feat = send.shape[1], delta_reduced.shape[1], delta_widened.shape[1]
    hid = delta_first.shape[1]
    part = hid // 2 - sixths.shape[2]
    half_delta[0] = delta_reduced[:, : rank // 2]
    half_delta[1] = delta_reduced[:, rank // 2 :]
    sixths[0] = delta_first[:, part : hid // 2]
    sixths[1] = delta_first[:, hid // 2 + part :]
    put_rows(small, 24, jnp.sum(delta_widened.astype(f32), axis=0, keepdims=True))
    small[0:24, :] = load(8)
    small[41:48, :] = jnp.zeros((7, LANES), f32)
    sums = jnp.concatenate([small[...]] * n_row, axis=0)
    crossed_t, reduced_t, stacked_t = load(7), reduced.T, stacked.T
    for ref, who in ((send, 1 - core), (keep, core)):
        offset = put_blocks(ref, row_pos, places, 0, matmul(crossed_t, sixths[who]))
        offset = put_blocks(ref, row_pos, places, offset, matmul(stacked_t, half_delta[who]))
        start = pl.multiple_of(who * (feat - SPAN), LANES)
        offset = put_blocks(
            ref, row_pos, places, offset, matmul(reduced_t, wide_delta[:, pl.ds(start, SPAN)])
        )
        offset = put_blocks(ref, row_pos, places, offset, sums)
        tail = 2 * ref.shape[2] * ref.shape[3] - offset
        if tail:
            put_blocks(ref, row_pos, places, offset, jnp.zeros((n_row * tail, LANES), f32))


def select_kernel(n_z, *refs):
    for which in range(n_z):
        out = refs[len(refs) - 2 + which // (n_z // 2)]
        out[which % (n_z // 2)] = refs[which][1]


def count_kernel(n_row, table, hot, n_z, slots, *rest):
    direct, crossed, out = rest[:n_z], rest[n_z : n_z + 2], rest[-1]
    near = n_z // 2
    block = out.shape[1]
    samples = crossed[0].shape[2]
    core, row_pos, table_pos = position()
    z_pos = lax.div(table_pos, 2)
    base = (pl.program_id(0) ^ row_pos) * block
    names = lax.broadcasted_iota(jnp.int16, (block, samples), 0)
    total = jnp.zeros((block, out.shape[2]), f32)
    one = jnp.ones((block, samples), bf16)
    zero = jnp.zeros((block, samples), bf16)
    for which in range(n_z):
        far = crossed[which // near]
        for held, who in ((direct[which][0, table], core), (far[which % near, table], 1 - core)):
            source = 2 * (z_pos ^ which) + who
            start = pl.multiple_of((source * n_row + row_pos) * samples, LANES)
            lines = slots[table, :, pl.ds(start, samples)] - base
            lines = jnp.where((lines >= 0) & (lines < block), lines, block).astype(jnp.int16)
            counts = zero
            for look in range(hot):
                line = jnp.broadcast_to(lines[look : look + 1, :], (block, samples))
                counts = counts + jnp.where(line == names, one, zero)
            total = total + matmul(counts, held)
    out[0] = total.astype(out.dtype)


def unpack_kernel(*refs):
    parts = refs[0:8]
    g_down, g_up, g_first, g_second = refs[8:12]
    small_outs = refs[12:16]
    held, small = refs[16:18], refs[18]
    core, row_pos, table_pos = position()
    z_pos = lax.div(table_pos, 2)
    for stream in range(2):
        lower, upper, lower_other, upper_other = parts[4 * stream : 4 * stream + 4]
        ref = held[stream]
        rows = lower.shape[1]
        n_z = 2 * lower.shape[0]
        z_bits = n_z.bit_length() - 1
        for who, pieces in ((core, (lower, upper)), (1 - core, (lower_other, upper_other))):
            for place in range(n_z):
                start = pl.multiple_of((reverse_bits(place, z_bits) ^ z_pos) * rows, 16)
                ref[who, pl.ds(start, rows), :] = pieces[place // (n_z // 2)][place % (n_z // 2)]
    front, back = held

    def take(ref, out, half, offset, columns):
        rows = out.shape[0]
        step = round_up(rows, 16)
        for column in columns:
            out[:, column * LANES : (column + 1) * LANES] = ref[
                half, offset : offset + rows, :
            ].astype(f32)
            offset += step
        return offset

    for half in range(2):
        blocks = g_second.shape[1] // LANES // 2
        offset = take(front, g_second, half, 0, range(half * blocks, (half + 1) * blocks))
        blocks = g_first.shape[1] // LANES // 2
        early = blocks - blocks // 4
        take(front, g_first, half, offset, range(half * blocks, half * blocks + early))
        offset = take(back, g_first, half, 0, range(half * blocks + early, (half + 1) * blocks))
        blocks = g_down.shape[1] // LANES // 2
        offset = take(back, g_down, half, offset, range(half * blocks, (half + 1) * blocks))
        blocks = g_up.shape[1] // LANES
        offset = take(back, g_up, half, offset, range(half * (blocks - 9), half * (blocks - 9) + 9))
    small[0:48, :] = back[0, offset : offset + 48, :].astype(f32)
    small[48:, :] = jnp.zeros((small.shape[0] - 48, LANES), f32)
    for out, first in zip(small_outs, (24, 0, 8, 16)):
        share = out.shape[0]
        begin = row_pos * share
        row, lane = lax.div(begin, LANES), lax.rem(begin, LANES)
        lanes = lax.broadcasted_iota(jnp.int32, (1, LANES), 1)
        for start in range(0, share, LANES):
            length = min(LANES, share - start)
            this = small[pl.ds(first + row + start // LANES, 1), :]
            later = small[pl.ds(first + row + start // LANES + 1, 1), :]
            both = jnp.where(lanes < lane, later, this)
            turned = pltpu.roll(both, lax.rem(LANES - lane, LANES), 1)
            out[start : start + length] = turned.reshape(LANES)[:length]


def whole(memory=pltpu.VMEM):
    return pl.BlockSpec(memory_space=memory)


def no_cost():
    return pl.CostEstimate(flops=0, transcendentals=0, bytes_accessed=0)


def call(body, outs, scratch, in_specs, name, mib):
    return pl.pallas_call(
        body,
        out_shape=outs,
        in_specs=in_specs,
        out_specs=[whole()] * len(outs),
        scratch_shapes=scratch,
        compiler_params=pltpu.CompilerParams(vmem_limit_bytes=mib * MIB),
        cost_estimate=no_cost(),
        name=name,
    )


def after(values, deps):
    return list(lax.optimization_barrier(tuple(values) + tuple(deps))[: len(values)])


def held_like(values):
    return [pltpu.VMEM(value.shape, value.dtype) for value in values]


def sum_rows_kernel(plan, *refs):
    out = refs[-1]
    for table, terms in enumerate(plan):
        total = None
        for which, picks in terms:
            part = refs[which][picks].astype(f32)
            total = part if total is None else total + part
        out[table] = total


def sum_rows(groups, deps):
    arrays = [array for items in groups for array, _ in items]
    plan, count = [], 0
    for items in groups:
        plan.append([(count + at, tuple(picks)) for at, (_, picks) in enumerate(items)])
        count += len(items)
    kept = [pick.stop - pick.start for pick in groups[0][0][1] if isinstance(pick, slice)]
    return call(
        functools.partial(sum_rows_kernel, plan),
        [jax.ShapeDtypeStruct((len(groups), *kept), f32)],
        [],
        [whole()] * len(arrays) + [whole(pl.ANY)] * len(deps),
        "rows",
        24,
    )(*arrays, *deps)[0]


def sum_kernel(plan, n_in, *refs):
    outs = refs[len(refs) - len(plan) :]
    for out, terms in zip(outs, plan):
        rows = out.shape[-2]
        chunk = next(size for size in (64, 48, 80, 32, 16, 8, rows) if rows % size == 0)

        def one_chunk(at, carry, out=out, terms=terms, chunk=chunk):
            window = pl.ds(pl.multiple_of(at * chunk, chunk), chunk)
            for lead in itertools.product(*[range(size) for size in out.shape[:-2]]):
                total = None
                for which, picks in terms:
                    axes, place = iter(lead), []
                    for pick in picks[:-2]:
                        place.append(pick.start + next(axes) if isinstance(pick, slice) else pick)
                    part = refs[which][(*place, window, slice(None))].astype(f32)
                    total = part if total is None else total + part
                out[(*lead, window, slice(None))] = total.astype(out.dtype)
            return carry

        lax.fori_loop(0, rows // chunk, one_chunk, 0)


def fetch_sum_kernel(plan, n_in, *refs):
    outs = refs[n_in : n_in + len(plan)]
    held, sems = refs[n_in + len(plan) : -1], refs[-1]
    copies, by_out = [], []
    for terms in plan:
        parts = []
        for which, picks in terms:
            at = len(copies)
            place = tuple(
                pl.ds(pick.start, pick.stop - pick.start) if isinstance(pick, slice) else pick
                for pick in picks
            )
            copies.append(pltpu.make_async_copy(refs[which].at[place], held[at], sems.at[at]))
            parts.append((at, tuple(slice(0, size) for size in held[at].shape)))
        by_out.append(parts)
    for copy in copies:
        copy.start()
    for out, parts in zip(outs, by_out):
        for at, _ in parts:
            copies[at].wait()
        sum_kernel([parts], 0, *held, out)


def fetch_sums(groups, deps):
    arrays, plan, shapes, scratch = [], [], [], []
    for items in groups:
        kept = tuple(pick.stop - pick.start for pick in items[0][1] if isinstance(pick, slice))
        shapes.append(jax.ShapeDtypeStruct(kept, bf16))
        terms = []
        for array, picks in items:
            found = [at for at, known in enumerate(arrays) if known is array]
            if not found:
                arrays.append(array)
            terms.append((found[0] if found else len(arrays) - 1, tuple(picks)))
            scratch.append(pltpu.VMEM(kept, array.dtype))
        plan.append(terms)
    n_in = len(arrays) + len(deps)
    return call(
        functools.partial(fetch_sum_kernel, plan, n_in),
        shapes,
        scratch + [pltpu.SemaphoreType.DMA((len(scratch),))],
        [whole(pltpu.HBM)] * len(arrays) + [whole(pl.ANY)] * len(deps),
        "first_sums",
        24,
    )(*arrays, *deps)


def take_sums(groups, deps, dtype=bf16):
    arrays, plan, shapes = [], [], []
    for items in groups:
        terms = []
        for array, picks in items:
            found = [at for at, known in enumerate(arrays) if known is array]
            if not found:
                arrays.append(array)
            terms.append((found[0] if found else len(arrays) - 1, tuple(picks)))
        plan.append(terms)
        kept = [pick.stop - pick.start for pick in items[0][1] if isinstance(pick, slice)]
        shapes.append(jax.ShapeDtypeStruct(tuple(kept), dtype))
    return call(
        functools.partial(sum_kernel, plan, len(arrays)),
        shapes,
        [],
        [whole()] * len(arrays) + [whole(pl.ANY)] * len(deps),
        "sums",
        24,
    )(*arrays, *deps)


def local(
    dense_feat,
    pooled,
    labels,
    cross_down,
    cross_up,
    cross_bias,
    w_hidden1,
    bias1,
    w_hidden2,
    bias2,
    w_logit,
    lookup_slots,
):
    n_table = lax.axis_size("table")
    n_row = lax.axis_size("row")
    n_z = n_table // 2
    row_bits = n_row.bit_length() - 1
    z_bits = n_z.bit_length() - 1
    batch, width = dense_feat.shape
    feat, rank = cross_down.shape
    hid = w_hidden1.shape[1]
    tab_grp, _, hot = lookup_slots.shape
    u_shard = batch * n_table * hot // 16

    def swap_cores(value):
        return lax.ppermute(value, "table", [(at, at ^ 1) for at in range(n_table)])

    def swap_z(value, which):
        return lax.ppermute(value, "table", [(at, at ^ (2 * which)) for at in range(n_table)])

    def swap_row(value, bit):
        return lax.ppermute(value, "row", [(at, at ^ (1 << bit)) for at in range(n_row)])

    late = hid // 8
    early = hid // 2 - late
    rows_front = (hid // 2 // LANES) * round_up(hid // n_row, 16)
    rows_front += (early // LANES) * round_up(feat // n_row, 16)
    rows_back = (late // LANES) * round_up(feat // n_row, 16)
    rows_back += (rank // 2 // LANES) * round_up(feat // n_row, 16)
    rows_back += 9 * round_up(rank // n_row, 16) + 48
    rows_front, rows_back = (round_up(rows, 16 * n_z) for rows in (rows_front, rows_back))

    def packed(rows):
        return jax.ShapeDtypeStruct((2, n_row, n_z // 2, rows // n_z, LANES), bf16)

    def wide(*shape):
        return jax.ShapeDtypeStruct(shape, bf16)

    hbm, vmem, anywhere = whole(pltpu.HBM), whole(), whole(pl.ANY)

    sources = (
        dense_feat,
        pooled,
        cross_down,
        cross_up,
        cross_bias,
        w_hidden1,
        bias1,
        w_hidden2,
        bias2,
        w_logit,
        labels,
    )
    send1, keep1, crossed_t, delta_first, small = call(
        front_kernel,
        [packed(rows_front)] * 2
        + [wide(feat, batch), wide(batch, hid), jax.ShapeDtypeStruct((24, LANES), f32)],
        held_like(sources)
        + [
            pltpu.VMEM((2, batch, hid // 2), bf16),
            pltpu.VMEM((2, batch, early), bf16),
            pltpu.SemaphoreType.DMA((len(sources),)),
        ],
        [hbm] * len(sources),
        "front",
        60,
    )(*sources)
    got1 = swap_cores(send1)

    sources = (
        dense_feat,
        pooled,
        cross_down,
        cross_up,
        cross_bias,
        delta_first,
        w_hidden1,
        crossed_t,
        small,
    )
    send2, keep2, *pooled_out = call(
        functools.partial(middle_kernel, n_z),
        [packed(rows_back)] * 2 + [wide(2, tab_grp, batch, width)] * n_z,
        held_like(sources)
        + [
            pltpu.VMEM((n_z, 2, tab_grp, batch, width), bf16),
            pltpu.VMEM((batch, feat), bf16),
            pltpu.VMEM((2, batch, rank // 2), bf16),
            pltpu.VMEM((2, batch, late), bf16),
            pltpu.VMEM((48, LANES), f32),
            pltpu.SemaphoreType.DMA((len(sources),)),
        ],
        [hbm] * len(sources),
        "middle",
        60,
    )(*sources)
    got2 = swap_cores(send2)

    low_first = tuple(range(row_bits))
    high_first = low_first[::-1]

    class Terms:
        def __init__(self, arrays, picks):
            self.items = []
            for array in arrays:
                self.add(array, picks)

        def add(self, array, picks=()):
            whole_axes = [slice(0, size) for size in array.shape[len(picks) :]]
            self.items.append((array, list(picks) + whole_axes))

        def narrowed(self, axis, what):
            items = []
            for array, picks in self.items:
                at = [number for number, pick in enumerate(picks) if isinstance(pick, slice)][axis]
                items.append((array, picks[:at] + [what] + picks[at + 1 :]))
            return items

        def far_near(self, axis, near, far):
            sent = self.narrowed(axis, far)
            self.items = self.narrowed(axis, near)
            return sent

    class Halving(Terms):
        def __init__(self, arrays, order, picks=()):
            dims = len(picks)
            arrays = [
                array.reshape(array.shape[:dims] + (2,) * row_bits + array.shape[dims + 1 :])
                for array in arrays
            ]
            super().__init__(arrays, picks)
            self.order, self.left = order, list(range(row_bits - 1, -1, -1))

        def part(self, at):
            axis = self.left.index(self.order[at])
            self.left.remove(self.order[at])
            return self.far_near(axis, 0, 1)

    def row_step(streams, at, deps):
        sent = take_sums([stream.part(at) for stream in streams], deps)
        for stream, value in zip(streams, sent):
            stream.add(swap_row(value, stream.order[at]))
        return list(sent)

    class Dense:
        def __init__(self, keep, got):
            self.low = Halving([keep, got], low_first, [0])
            self.high = Halving([keep, got], high_first, [1])

        def first_step(self, deps):
            halves = (self.low, self.high)
            sent = fetch_sums([half.part(0) for half in halves], deps)
            self.near = [half.items for half in halves]
            for half, value in zip(halves, sent):
                half.items = []
                half.add(swap_row(value, half.order[0]))
            return list(sent)

        def settle(self, deps):
            for half, value in zip((self.low, self.high), fetch_sums(self.near, deps)):
                half.add(value)
                half.items.reverse()

        def row_step(self, at, deps):
            deps = [*deps, self.low.items[-1][0], self.high.items[-1][0]]
            return row_step((self.low, self.high), at, deps)

        def z_step(self, stage, deps):
            middle = n_z >> (stage + 1)
            items, deps = self.high.items, [*deps, self.low.items[-1][0]]
            if stage > 0:
                items = self.low.far_near(0, slice(0, middle), slice(middle, 2 * middle))
            (sent,) = take_sums([items], deps)
            self.low.add(swap_z(sent, 1 << stage))
            return [sent]

        def z_own(self, deps):
            (self.own,) = take_sums([self.low.items], deps)
            self.back = swap_z(self.own, 1 << (z_bits - 1)) if z_bits > 1 else None
            return [self.own]

        def z_back(self, deps):
            for stage in range(z_bits - 1, 0, -1):
                if stage < z_bits - 1:
                    self.back = swap_z(self.own, 1 << stage)
                (back,) = after([self.back], deps)
                self.own = jnp.concatenate([self.own, back], axis=0)
            far = swap_z(self.own, 1)
            self.pieces = [self.own, far, swap_cores(self.own), swap_cores(far)]
            return [self.own]

    (got1,) = after([got1], [pooled_out[0]])
    one, two = Dense(keep1, got1), Dense(keep2, got2)
    one.first_step([])
    values, half = {0: pooled_out[0]}, n_z // 2
    for which in [half, *range(1, half)]:
        values[which] = swap_z(pooled_out[which], which)
    for which in range(half + 1, n_z):
        (moved,) = after([pooled_out[which]], [values[half], values[which - half]])
        values[which] = swap_z(moved, which)
    one.settle([values[1]])
    last = [values[which] for which in range(1, half + 1)]
    for at in range(1, row_bits):
        last = one.row_step(at, last)
    last = two.first_step(last)
    last = one.z_step(0, last)
    two.settle(last)
    values = [values[which] for which in range(n_z)]
    far_values = call(
        functools.partial(select_kernel, n_z),
        [wide(n_z // 2, tab_grp, batch, width)] * 2,
        [],
        [vmem] * n_z + [anywhere],
        "select",
        8,
    )(*values, last[0])
    values += [swap_cores(value) for value in far_values]
    slots = jnp.transpose(lookup_slots, (0, 2, 1))
    last, shares = [far_values[0]], []
    for table in range(tab_grp):
        sums = pl.pallas_call(
            functools.partial(count_kernel, n_row, table, hot, n_z),
            out_shape=wide(n_row, u_shard, width),
            grid=(n_row,),
            in_specs=[vmem] * (3 + n_z) + [anywhere],
            out_specs=pl.BlockSpec((1, u_shard, width), lambda at: (at, 0, 0)),
            compiler_params=pltpu.CompilerParams(vmem_limit_bytes=16 * MIB),
            cost_estimate=no_cost(),
            name="counts",
        )(slots, *values, last[0])
        shares.append(Halving([sums], high_first if table % 2 else low_first))
        last = [sums]
        if table == 0:
            for at in range(1, row_bits):
                last = two.row_step(at, last)
            for stage in range(1, z_bits):
                last = one.z_step(stage, last)
            last = two.z_step(0, last)
    last = row_step(shares, 0, last)
    last = one.z_own(last)
    for stage in range(1, z_bits):
        last = two.z_step(stage, last)
    for at in range(1, row_bits):
        last = row_step(shares, at, last)
    last = two.z_own(last)
    last = one.z_back(last)
    row_grads = sum_rows([share.items for share in shares], last)
    two.z_back([row_grads])

    g_down, g_up, g_first, g_second, g_cbias, g_bias1, g_bias2, g_logit = call(
        unpack_kernel,
        [
            jax.ShapeDtypeStruct((feat // n_row, rank), f32),
            jax.ShapeDtypeStruct((rank // n_row, feat), f32),
            jax.ShapeDtypeStruct((feat // n_row, hid), f32),
            jax.ShapeDtypeStruct((hid // n_row, hid), f32),
            jax.ShapeDtypeStruct((feat // n_row,), f32),
        ]
        + [jax.ShapeDtypeStruct((hid // n_row,), f32)] * 3,
        [pltpu.VMEM((2, rows, LANES), bf16) for rows in (rows_front, rows_back)]
        + [pltpu.VMEM((56, LANES), f32)],
        [vmem] * 8,
        "unpack",
        24,
    )(*one.pieces, *two.pieces)
    return (row_grads, g_down, g_up, g_cbias, g_first, g_bias1, g_second, g_bias2, g_logit)


def solution(mesh):
    in_specs = (
        P(("table", "row"), None),
        P(("table", "row"), None),
        P(("table", "row")),
        P(),
        P(),
        P(),
        P(),
        P(),
        P(),
        P(),
        P(),
        P("table", None, None),
    )
    out_specs = (
        P("table", "row", None),
        P("row", None),
        P("row", None),
        P("row"),
        P("row", None),
        P("row"),
        P("row", None),
        P("row"),
        P("row"),
    )
    return jax.shard_map(local, mesh=mesh, in_specs=in_specs, out_specs=out_specs, check_vma=False)
```

```python
import functools
import itertools

import jax
import jax.numpy as jnp
from jax import lax
from jax.experimental import pallas as pl
from jax.experimental.pallas import tpu as pltpu
from jax.sharding import PartitionSpec as P

loss_scale = 16.0
LANES = 128
SPAN = 9 * LANES
MIB = 1024 * 1024
bf16 = jnp.bfloat16
f32 = jnp.float32


def round_up(value, unit):
    return -(-value // unit) * unit


def matmul(left, right):
    return jnp.dot(left, right, preferred_element_type=f32)


def matmul_rt(left, right):
    return lax.dot_general(left, right, (((1,), (1,)), ((), ())), preferred_element_type=f32)


def reverse_bits(value, bits):
    out = 0
    for bit in range(bits):
        out = out | (((value >> bit) & 1) << (bits - 1 - bit))
    return out


def places_of(z_pos, n_z):
    bits = n_z.bit_length() - 1
    return [reverse_bits(z_pos ^ quarter, bits) for quarter in range(n_z)]


def put_blocks(ref, row_pos, places, offset, value):
    shards, n_half, rows_q = ref.shape[1], ref.shape[2], ref.shape[3]
    rows = value.shape[0] // shards
    step = round_up(rows, 16)
    blocks = value.shape[1] // LANES
    for shard in range(shards):
        slot = shard ^ row_pos
        for block in range(blocks):
            done = 0
            while done < rows:
                quarter, at = divmod(offset + block * step + done, rows_q)
                length = min(rows - done, rows_q - at)
                place = places[quarter]
                ref[lax.div(place, n_half), slot, lax.rem(place, n_half), at : at + length, :] = value[
                    shard * rows + done : shard * rows + done + length,
                    block * LANES : (block + 1) * LANES,
                ].astype(ref.dtype)
                done += length
    return offset + blocks * step


def put_rows(ref, offset, value):
    for block in range(value.shape[1] // LANES):
        ref[offset + block : offset + block + 1, :] = value[:, block * LANES : (block + 1) * LANES]


def position():
    table_pos = lax.axis_index("table")
    return lax.rem(table_pos, 2), lax.axis_index("row"), table_pos


class Loads:
    def __init__(self, sources, targets, sems):
        self.copies = [
            pltpu.make_async_copy(source, target, sems.at[at])
            for at, (source, target) in enumerate(zip(sources, targets))
        ]
        self.targets = targets
        self.ready = set()
        for copy in self.copies:
            copy.start()

    def __call__(self, at):
        if at not in self.ready:
            self.copies[at].wait()
            self.ready.add(at)
        return self.targets[at][...]


def as_row(value):
    return value.reshape(1, value.shape[-1])


def front_kernel(*refs):
    sources, outs, targets = refs[:11], refs[11:16], refs[16:27]
    halves, thirds, sems = refs[27:]
    send, keep, crossed_t_out, first_out, small = outs
    load = Loads(sources, targets, sems)
    core, row_pos, table_pos = position()
    places = places_of(lax.div(table_pos, 2), 2 * send.shape[2])
    stacked = jnp.concatenate([load(0), load(1)], axis=1)
    cross_down = load(2)
    reduced = matmul(stacked, cross_down).astype(bf16)
    widened = matmul(reduced, load(3)) + as_row(load(4))
    wide = stacked.astype(f32)
    crossed = (wide * widened + wide).astype(bf16)
    pre_first = matmul(crossed, load(5)) + as_row(load(6))
    sig_first = jax.nn.sigmoid(pre_first)
    act_first = (pre_first * sig_first).astype(bf16)
    slope_first = sig_first * (1.0 + pre_first * (1.0 - sig_first))
    w_hidden2 = load(7)
    pre_second = matmul(act_first, w_hidden2) + as_row(load(8))
    sig_second = jax.nn.sigmoid(pre_second)
    act_second = (pre_second * sig_second).astype(bf16).astype(f32)
    slope_second = sig_second * (1.0 + pre_second * (1.0 - sig_second))
    w_logit = as_row(load(9))
    logits = jnp.sum(act_second * w_logit, axis=1, keepdims=True)
    labels = as_row(load(10))
    count = labels.shape[1]
    same = lax.broadcasted_iota(jnp.int32, (count, count), 0) == lax.broadcasted_iota(
        jnp.int32, (count, count), 1
    )
    label_col = jnp.sum(jnp.where(same, labels.astype(f32), 0.0), axis=1, keepdims=True)
    delta_logit = loss_scale * (jax.nn.sigmoid(logits) - label_col)
    delta_second = (delta_logit * w_logit * slope_second).astype(bf16)
    put_rows(small, 16, jnp.sum(act_second * delta_logit, axis=0, keepdims=True))
    put_rows(small, 8, jnp.sum(delta_second.astype(f32), axis=0, keepdims=True))
    half = halves.shape[2]
    halves[0] = delta_second[:, :half]
    halves[1] = delta_second[:, half:]
    delta_first = (matmul_rt(delta_second, w_hidden2) * slope_first).astype(bf16)
    first_out[...] = delta_first
    put_rows(small, 0, jnp.sum(delta_first.astype(f32), axis=0, keepdims=True))
    part = thirds.shape[2]
    thirds[0] = delta_first[:, :part]
    thirds[1] = delta_first[:, half : half + part]
    act_t = act_first.T
    crossed_t = crossed.T
    crossed_t_out[...] = crossed_t
    for ref, who in ((send, 1 - core), (keep, core)):
        offset = put_blocks(ref, row_pos, places, 0, matmul(act_t, halves[who]))
        put_blocks(ref, row_pos, places, offset, matmul(crossed_t, thirds[who]))


def middle_kernel(n_z, *refs):
    sources, send, keep = refs[:9], refs[9], refs[10]
    pooled_outs = refs[11 : 11 + n_z]
    rest = refs[11 + n_z :]
    targets = rest[:9]
    by_group, wide_delta, half_delta, sixths, small, sems = rest[9:]
    load = Loads(sources, targets, sems)
    core, row_pos, table_pos = position()
    z_pos = lax.div(table_pos, 2)
    places = places_of(z_pos, 2 * send.shape[2])
    stacked = jnp.concatenate([load(0), load(1)], axis=1)
    cross_down = load(2)
    reduced = matmul(stacked, cross_down).astype(bf16)
    cross_up = load(3)
    widened = matmul(reduced, cross_up) + as_row(load(4))
    delta_first = load(5)
    delta_crossed = matmul_rt(delta_first, load(6))
    delta_widened = (delta_crossed * stacked.astype(f32)).astype(bf16)
    wide_delta[...] = delta_widened
    delta_reduced = matmul_rt(delta_widened, cross_up).astype(bf16)
    delta_stacked = delta_crossed * (widened + 1.0) + matmul_rt(delta_reduced, cross_down)
    width = targets[0].shape[1]
    per_group = by_group.shape[2]
    for table in range(2 * n_z * per_group):
        group = table // per_group
        by_group[group // 2, group % 2, table % per_group] = delta_stacked[
            :, width * (table + 1) : width * (table + 2)
        ].astype(bf16)
    for which in range(n_z):
        pooled_outs[which][0] = by_group[z_pos ^ which, core]
        pooled_outs[which][1] = by_group[z_pos ^ which, 1 - core]

    n_row, rank, feat = send.shape[1], delta_reduced.shape[1], delta_widened.shape[1]
    hid = delta_first.shape[1]
    part = hid // 2 - sixths.shape[2]
    half_delta[0] = delta_reduced[:, : rank // 2]
    half_delta[1] = delta_reduced[:, rank // 2 :]
    sixths[0] = delta_first[:, part : hid // 2]
    sixths[1] = delta_first[:, hid // 2 + part :]
    put_rows(small, 24, jnp.sum(delta_widened.astype(f32), axis=0, keepdims=True))
    small[0:24, :] = load(8)
    small[41:48, :] = jnp.zeros((7, LANES), f32)
    sums = jnp.concatenate([small[...]] * n_row, axis=0)
    crossed_t, reduced_t, stacked_t = load(7), reduced.T, stacked.T
    for ref, who in ((send, 1 - core), (keep, core)):
        offset = put_blocks(ref, row_pos, places, 0, matmul(crossed_t, sixths[who]))
        offset = put_blocks(ref, row_pos, places, offset, matmul(stacked_t, half_delta[who]))
        start = pl.multiple_of(who * (feat - SPAN), LANES)
        offset = put_blocks(
            ref, row_pos, places, offset, matmul(reduced_t, wide_delta[:, pl.ds(start, SPAN)])
        )
        offset = put_blocks(ref, row_pos, places, offset, sums)
        tail = 2 * ref.shape[2] * ref.shape[3] - offset
        if tail:
            put_blocks(ref, row_pos, places, offset, jnp.zeros((n_row * tail, LANES), f32))


def select_kernel(n_z, *refs):
    for which in range(n_z):
        out = refs[len(refs) - 2 + which // (n_z // 2)]
        out[which % (n_z // 2)] = refs[which][1]


def count_kernel(n_row, table, hot, n_z, slots, *rest):
    direct, crossed, out = rest[:n_z], rest[n_z : n_z + 2], rest[-1]
    near = n_z // 2
    block = out.shape[1]
    samples = crossed[0].shape[2]
    core, row_pos, table_pos = position()
    z_pos = lax.div(table_pos, 2)
    base = (pl.program_id(0) ^ row_pos) * block
    names = lax.broadcasted_iota(jnp.int16, (block, samples), 0)
    total = jnp.zeros((block, out.shape[2]), f32)
    one = jnp.ones((block, samples), bf16)
    zero = jnp.zeros((block, samples), bf16)
    for which in range(n_z):
        far = crossed[which // near]
        for held, who in ((direct[which][0, table], core), (far[which % near, table], 1 - core)):
            source = 2 * (z_pos ^ which) + who
            start = pl.multiple_of((source * n_row + row_pos) * samples, LANES)
            lines = slots[table, :, pl.ds(start, samples)] - base
            lines = jnp.where((lines >= 0) & (lines < block), lines, block).astype(jnp.int16)
            counts = zero
            for look in range(hot):
                line = jnp.broadcast_to(lines[look : look + 1, :], (block, samples))
                counts = counts + jnp.where(line == names, one, zero)
            total = total + matmul(counts, held)
    out[0] = total.astype(out.dtype)


def unpack_kernel(*refs):
    parts = refs[0:8]
    g_down, g_up, g_first, g_second = refs[8:12]
    small_outs = refs[12:16]
    held, small = refs[16:18], refs[18]
    core, row_pos, table_pos = position()
    z_pos = lax.div(table_pos, 2)
    for stream in range(2):
        lower, upper, lower_other, upper_other = parts[4 * stream : 4 * stream + 4]
        ref = held[stream]
        rows = lower.shape[1]
        n_z = 2 * lower.shape[0]
        z_bits = n_z.bit_length() - 1
        for who, pieces in ((core, (lower, upper)), (1 - core, (lower_other, upper_other))):
            for place in range(n_z):
                start = pl.multiple_of((reverse_bits(place, z_bits) ^ z_pos) * rows, 16)
                ref[who, pl.ds(start, rows), :] = pieces[place // (n_z // 2)][place % (n_z // 2)]
    front, back = held

    def take(ref, out, half, offset, columns):
        rows = out.shape[0]
        step = round_up(rows, 16)
        for column in columns:
            out[:, column * LANES : (column + 1) * LANES] = ref[
                half, offset : offset + rows, :
            ].astype(f32)
            offset += step
        return offset

    for half in range(2):
        blocks = g_second.shape[1] // LANES // 2
        offset = take(front, g_second, half, 0, range(half * blocks, (half + 1) * blocks))
        blocks = g_first.shape[1] // LANES // 2
        early = blocks - blocks // 4
        take(front, g_first, half, offset, range(half * blocks, half * blocks + early))
        offset = take(back, g_first, half, 0, range(half * blocks + early, (half + 1) * blocks))
        blocks = g_down.shape[1] // LANES // 2
        offset = take(back, g_down, half, offset, range(half * blocks, (half + 1) * blocks))
        blocks = g_up.shape[1] // LANES
        offset = take(back, g_up, half, offset, range(half * (blocks - 9), half * (blocks - 9) + 9))
    small[0:48, :] = back[0, offset : offset + 48, :].astype(f32)
    small[48:, :] = jnp.zeros((small.shape[0] - 48, LANES), f32)
    for out, first in zip(small_outs, (24, 0, 8, 16)):
        share = out.shape[0]
        begin = row_pos * share
        row, lane = lax.div(begin, LANES), lax.rem(begin, LANES)
        lanes = lax.broadcasted_iota(jnp.int32, (1, LANES), 1)
        for start in range(0, share, LANES):
            length = min(LANES, share - start)
            this = small[pl.ds(first + row + start // LANES, 1), :]
            later = small[pl.ds(first + row + start // LANES + 1, 1), :]
            both = jnp.where(lanes < lane, later, this)
            turned = pltpu.roll(both, lax.rem(LANES - lane, LANES), 1)
            out[start : start + length] = turned.reshape(LANES)[:length]


def whole(memory=pltpu.VMEM):
    return pl.BlockSpec(memory_space=memory)


def no_cost():
    return pl.CostEstimate(flops=0, transcendentals=0, bytes_accessed=0)


def call(body, outs, scratch, in_specs, name, mib):
    return pl.pallas_call(
        body,
        out_shape=outs,
        in_specs=in_specs,
        out_specs=[whole()] * len(outs),
        scratch_shapes=scratch,
        compiler_params=pltpu.CompilerParams(vmem_limit_bytes=mib * MIB),
        cost_estimate=no_cost(),
        name=name,
    )


def after(values, deps):
    return list(lax.optimization_barrier(tuple(values) + tuple(deps))[: len(values)])


def held_like(values):
    return [pltpu.VMEM(value.shape, value.dtype) for value in values]


def sum_rows_kernel(plan, *refs):
    out = refs[-1]
    for table, terms in enumerate(plan):
        total = None
        for which, picks in terms:
            part = refs[which][picks].astype(f32)
            total = part if total is None else total + part
        out[table] = total


def sum_rows(groups, deps):
    arrays = [array for items in groups for array, _ in items]
    plan, count = [], 0
    for items in groups:
        plan.append([(count + at, tuple(picks)) for at, (_, picks) in enumerate(items)])
        count += len(items)
    kept = [pick.stop - pick.start for pick in groups[0][0][1] if isinstance(pick, slice)]
    return call(
        functools.partial(sum_rows_kernel, plan),
        [jax.ShapeDtypeStruct((len(groups), *kept), f32)],
        [],
        [whole()] * len(arrays) + [whole(pl.ANY)] * len(deps),
        "rows",
        24,
    )(*arrays, *deps)[0]


def sum_kernel(plan, n_in, *refs):
    outs = refs[len(refs) - len(plan) :]
    for out, terms in zip(outs, plan):
        rows = out.shape[-2]
        chunk = next(size for size in (64, 48, 80, 32, 16, 8, rows) if rows % size == 0)

        def one_chunk(at, carry, out=out, terms=terms, chunk=chunk):
            window = pl.ds(pl.multiple_of(at * chunk, chunk), chunk)
            for lead in itertools.product(*[range(size) for size in out.shape[:-2]]):
                total = None
                for which, picks in terms:
                    axes, place = iter(lead), []
                    for pick in picks[:-2]:
                        place.append(pick.start + next(axes) if isinstance(pick, slice) else pick)
                    part = refs[which][(*place, window, slice(None))].astype(f32)
                    total = part if total is None else total + part
                out[(*lead, window, slice(None))] = total.astype(out.dtype)
            return carry

        lax.fori_loop(0, rows // chunk, one_chunk, 0)


def fetch_sum_kernel(plan, n_in, *refs):
    outs = refs[n_in : n_in + len(plan)]
    held, sems = refs[n_in + len(plan) : -1], refs[-1]
    copies, by_out = [], []
    for terms in plan:
        parts = []
        for which, picks in terms:
            at = len(copies)
            place = tuple(
                pl.ds(pick.start, pick.stop - pick.start) if isinstance(pick, slice) else pick
                for pick in picks
            )
            copies.append(pltpu.make_async_copy(refs[which].at[place], held[at], sems.at[at]))
            parts.append((at, tuple(slice(0, size) for size in held[at].shape)))
        by_out.append(parts)
    for copy in copies:
        copy.start()
    for out, parts in zip(outs, by_out):
        for at, _ in parts:
            copies[at].wait()
        sum_kernel([parts], 0, *held, out)


def fetch_sums(groups, deps):
    arrays, plan, shapes, scratch = [], [], [], []
    for items in groups:
        kept = tuple(pick.stop - pick.start for pick in items[0][1] if isinstance(pick, slice))
        shapes.append(jax.ShapeDtypeStruct(kept, bf16))
        terms = []
        for array, picks in items:
            found = [at for at, known in enumerate(arrays) if known is array]
            if not found:
                arrays.append(array)
            terms.append((found[0] if found else len(arrays) - 1, tuple(picks)))
            scratch.append(pltpu.VMEM(kept, array.dtype))
        plan.append(terms)
    n_in = len(arrays) + len(deps)
    return call(
        functools.partial(fetch_sum_kernel, plan, n_in),
        shapes,
        scratch + [pltpu.SemaphoreType.DMA((len(scratch),))],
        [whole(pltpu.HBM)] * len(arrays) + [whole(pl.ANY)] * len(deps),
        "first_sums",
        24,
    )(*arrays, *deps)


def take_sums(groups, deps, dtype=bf16):
    arrays, plan, shapes = [], [], []
    for items in groups:
        terms = []
        for array, picks in items:
            found = [at for at, known in enumerate(arrays) if known is array]
            if not found:
                arrays.append(array)
            terms.append((found[0] if found else len(arrays) - 1, tuple(picks)))
        plan.append(terms)
        kept = [pick.stop - pick.start for pick in items[0][1] if isinstance(pick, slice)]
        shapes.append(jax.ShapeDtypeStruct(tuple(kept), dtype))
    return call(
        functools.partial(sum_kernel, plan, len(arrays)),
        shapes,
        [],
        [whole()] * len(arrays) + [whole(pl.ANY)] * len(deps),
        "sums",
        24,
    )(*arrays, *deps)


def local(
    dense_feat,
    pooled,
    labels,
    cross_down,
    cross_up,
    cross_bias,
    w_hidden1,
    bias1,
    w_hidden2,
    bias2,
    w_logit,
    lookup_slots,
):
    n_table = lax.axis_size("table")
    n_row = lax.axis_size("row")
    n_z = n_table // 2
    row_bits = n_row.bit_length() - 1
    z_bits = n_z.bit_length() - 1
    batch, width = dense_feat.shape
    feat, rank = cross_down.shape
    hid = w_hidden1.shape[1]
    tab_grp, _, hot = lookup_slots.shape
    u_shard = batch * n_table * hot // 16

    def swap_cores(value):
        return lax.ppermute(value, "table", [(at, at ^ 1) for at in range(n_table)])

    def swap_z(value, which):
        return lax.ppermute(value, "table", [(at, at ^ (2 * which)) for at in range(n_table)])

    def swap_row(value, bit):
        return lax.ppermute(value, "row", [(at, at ^ (1 << bit)) for at in range(n_row)])

    late = hid // 8
    early = hid // 2 - late
    rows_front = (hid // 2 // LANES) * round_up(hid // n_row, 16)
    rows_front += (early // LANES) * round_up(feat // n_row, 16)
    rows_back = (late // LANES) * round_up(feat // n_row, 16)
    rows_back += (rank // 2 // LANES) * round_up(feat // n_row, 16)
    rows_back += 9 * round_up(rank // n_row, 16) + 48
    rows_front, rows_back = (round_up(rows, 16 * n_z) for rows in (rows_front, rows_back))

    def packed(rows):
        return jax.ShapeDtypeStruct((2, n_row, n_z // 2, rows // n_z, LANES), bf16)

    def wide(*shape):
        return jax.ShapeDtypeStruct(shape, bf16)

    hbm, vmem, anywhere = whole(pltpu.HBM), whole(), whole(pl.ANY)

    sources = (
        dense_feat,
        pooled,
        cross_down,
        cross_up,
        cross_bias,
        w_hidden1,
        bias1,
        w_hidden2,
        bias2,
        w_logit,
        labels,
    )
    send1, keep1, crossed_t, delta_first, small = call(
        front_kernel,
        [packed(rows_front)] * 2
        + [wide(feat, batch), wide(batch, hid), jax.ShapeDtypeStruct((24, LANES), f32)],
        held_like(sources)
        + [
            pltpu.VMEM((2, batch, hid // 2), bf16),
            pltpu.VMEM((2, batch, early), bf16),
            pltpu.SemaphoreType.DMA((len(sources),)),
        ],
        [hbm] * len(sources),
        "front",
        60,
    )(*sources)
    got1 = swap_cores(send1)

    sources = (
        dense_feat,
        pooled,
        cross_down,
        cross_up,
        cross_bias,
        delta_first,
        w_hidden1,
        crossed_t,
        small,
    )
    send2, keep2, *pooled_out = call(
        functools.partial(middle_kernel, n_z),
        [packed(rows_back)] * 2 + [wide(2, tab_grp, batch, width)] * n_z,
        held_like(sources)
        + [
            pltpu.VMEM((n_z, 2, tab_grp, batch, width), bf16),
            pltpu.VMEM((batch, feat), bf16),
            pltpu.VMEM((2, batch, rank // 2), bf16),
            pltpu.VMEM((2, batch, late), bf16),
            pltpu.VMEM((48, LANES), f32),
            pltpu.SemaphoreType.DMA((len(sources),)),
        ],
        [hbm] * len(sources),
        "middle",
        60,
    )(*sources)
    got2 = swap_cores(send2)

    low_first = tuple(range(row_bits))
    high_first = low_first[::-1]

    class Terms:
        def __init__(self, arrays, picks):
            self.items = []
            for array in arrays:
                self.add(array, picks)

        def add(self, array, picks=()):
            whole_axes = [slice(0, size) for size in array.shape[len(picks) :]]
            self.items.append((array, list(picks) + whole_axes))

        def narrowed(self, axis, what):
            items = []
            for array, picks in self.items:
                at = [number for number, pick in enumerate(picks) if isinstance(pick, slice)][axis]
                items.append((array, picks[:at] + [what] + picks[at + 1 :]))
            return items

        def far_near(self, axis, near, far):
            sent = self.narrowed(axis, far)
            self.items = self.narrowed(axis, near)
            return sent

    class Halving(Terms):
        def __init__(self, arrays, order, picks=()):
            dims = len(picks)
            arrays = [
                array.reshape(array.shape[:dims] + (2,) * row_bits + array.shape[dims + 1 :])
                for array in arrays
            ]
            super().__init__(arrays, picks)
            self.order, self.left = order, list(range(row_bits - 1, -1, -1))

        def part(self, at):
            axis = self.left.index(self.order[at])
            self.left.remove(self.order[at])
            return self.far_near(axis, 0, 1)

    def row_step(streams, at, deps):
        sent = take_sums([stream.part(at) for stream in streams], deps)
        for stream, value in zip(streams, sent):
            stream.add(swap_row(value, stream.order[at]))
        return list(sent)

    class Dense:
        def __init__(self, keep, got):
            self.low = Halving([keep, got], low_first, [0])
            self.high = Halving([keep, got], high_first, [1])

        def first_step(self, deps):
            halves = (self.low, self.high)
            sent = fetch_sums([half.part(0) for half in halves], deps)
            self.near = [half.items for half in halves]
            for half, value in zip(halves, sent):
                half.items = []
                half.add(swap_row(value, half.order[0]))
            return list(sent)

        def settle(self, deps):
            for half, value in zip((self.low, self.high), fetch_sums(self.near, deps)):
                half.add(value)
                half.items.reverse()

        def row_step(self, at, deps):
            deps = [*deps, self.low.items[-1][0], self.high.items[-1][0]]
            return row_step((self.low, self.high), at, deps)

        def z_step(self, stage, deps):
            middle = n_z >> (stage + 1)
            items, deps = self.high.items, [*deps, self.low.items[-1][0]]
            if stage > 0:
                items = self.low.far_near(0, slice(0, middle), slice(middle, 2 * middle))
            (sent,) = take_sums([items], deps)
            self.low.add(swap_z(sent, 1 << stage))
            return [sent]

        def z_own(self, deps):
            (self.own,) = take_sums([self.low.items], deps)
            self.back = swap_z(self.own, 1 << (z_bits - 1)) if z_bits > 1 else None
            return [self.own]

        def z_back(self, deps):
            for stage in range(z_bits - 1, 0, -1):
                if stage < z_bits - 1:
                    self.back = swap_z(self.own, 1 << stage)
                (back,) = after([self.back], deps)
                self.own = jnp.concatenate([self.own, back], axis=0)
            far = swap_z(self.own, 1)
            self.pieces = [self.own, far, swap_cores(self.own), swap_cores(far)]
            return [self.own]

    (got1,) = after([got1], [pooled_out[0]])
    one, two = Dense(keep1, got1), Dense(keep2, got2)
    one.first_step([])
    values, half = {0: pooled_out[0]}, n_z // 2
    for which in [half, *range(1, half)]:
        values[which] = swap_z(pooled_out[which], which)
    one.settle([values[1]])
    last = [values[which] for which in range(1, half + 1)]
    for at in range(1, row_bits):
        last = one.row_step(at, last)
    last = two.first_step(last)
    for which in range(half + 1, n_z):
        (moved,) = after([pooled_out[which]], [*last, values[which - half]])
        values[which] = swap_z(moved, which)
    last = one.z_step(0, last)
    two.settle(last)
    values = [values[which] for which in range(n_z)]
    last = [*last, *values[half + 1 :]]
    for at in range(1, row_bits):
        last = two.row_step(at, last)
    for stage in range(1, z_bits):
        last = one.z_step(stage, last)
    last = two.z_step(0, last)
    last = one.z_own(last)
    for stage in range(1, z_bits):
        last = two.z_step(stage, last)
    far_values = call(
        functools.partial(select_kernel, n_z),
        [wide(n_z // 2, tab_grp, batch, width)] * 2,
        [],
        [vmem] * n_z + [anywhere],
        "select",
        8,
    )(*values, last[0])
    values += [swap_cores(value) for value in far_values]
    slots = jnp.transpose(lookup_slots, (0, 2, 1))
    last, shares = [far_values[0]], []
    for table in range(tab_grp):
        sums = pl.pallas_call(
            functools.partial(count_kernel, n_row, table, hot, n_z),
            out_shape=wide(n_row, u_shard, width),
            grid=(n_row,),
            in_specs=[vmem] * (3 + n_z) + [anywhere],
            out_specs=pl.BlockSpec((1, u_shard, width), lambda at: (at, 0, 0)),
            compiler_params=pltpu.CompilerParams(vmem_limit_bytes=16 * MIB),
            cost_estimate=no_cost(),
            name="counts",
        )(slots, *values, last[0])
        shares.append(Halving([sums], high_first if table % 2 else low_first))
        last = [sums]
        if table == 0:
            last = two.z_own(last)
    last = row_step(shares, 0, last)
    last = two.z_back(last)
    last = one.z_back(last)
    for at in range(1, row_bits):
        last = row_step(shares, at, last)
    row_grads = sum_rows([share.items for share in shares], last)

    g_down, g_up, g_first, g_second, g_cbias, g_bias1, g_bias2, g_logit = call(
        unpack_kernel,
        [
            jax.ShapeDtypeStruct((feat // n_row, rank), f32),
            jax.ShapeDtypeStruct((rank // n_row, feat), f32),
            jax.ShapeDtypeStruct((feat // n_row, hid), f32),
            jax.ShapeDtypeStruct((hid // n_row, hid), f32),
            jax.ShapeDtypeStruct((feat // n_row,), f32),
        ]
        + [jax.ShapeDtypeStruct((hid // n_row,), f32)] * 3,
        [pltpu.VMEM((2, rows, LANES), bf16) for rows in (rows_front, rows_back)]
        + [pltpu.VMEM((56, LANES), f32)],
        [vmem] * 8,
        "unpack",
        24,
    )(*one.pieces, *two.pieces)
    return (row_grads, g_down, g_up, g_cbias, g_first, g_bias1, g_second, g_bias2, g_logit)


def solution(mesh):
    in_specs = (
        P(("table", "row"), None),
        P(("table", "row"), None),
        P(("table", "row")),
        P(),
        P(),
        P(),
        P(),
        P(),
        P(),
        P(),
        P(),
        P("table", None, None),
    )
    out_specs = (
        P("table", "row", None),
        P("row", None),
        P("row", None),
        P("row"),
        P("row", None),
        P("row"),
        P("row", None),
        P("row"),
        P("row"),
    )
    return jax.shard_map(local, mesh=mesh, in_specs=in_specs, out_specs=out_specs, check_vma=False)
```

```python
import functools
import itertools

import jax
import jax.numpy as jnp
from jax import lax
from jax.experimental import pallas as pl
from jax.experimental.pallas import tpu as pltpu
from jax.sharding import PartitionSpec as P

loss_scale = 16.0
LANES = 128
SPAN = 9 * LANES
MIB = 1024 * 1024
bf16 = jnp.bfloat16
f32 = jnp.float32


def round_up(value, unit):
    return -(-value // unit) * unit


def matmul(left, right):
    return jnp.dot(left, right, preferred_element_type=f32)


def matmul_rt(left, right):
    return lax.dot_general(left, right, (((1,), (1,)), ((), ())), preferred_element_type=f32)


def reverse_bits(value, bits):
    out = 0
    for bit in range(bits):
        out = out | (((value >> bit) & 1) << (bits - 1 - bit))
    return out


def places_of(z_pos, n_z):
    bits = n_z.bit_length() - 1
    return [reverse_bits(z_pos ^ quarter, bits) for quarter in range(n_z)]


def put_blocks(ref, row_pos, places, offset, value):
    shards, n_half, rows_q = ref.shape[1], ref.shape[2], ref.shape[3]
    rows = value.shape[0] // shards
    step = round_up(rows, 16)
    blocks = value.shape[1] // LANES
    for shard in range(shards):
        slot = shard ^ row_pos
        for block in range(blocks):
            done = 0
            while done < rows:
                quarter, at = divmod(offset + block * step + done, rows_q)
                length = min(rows - done, rows_q - at)
                place = places[quarter]
                ref[lax.div(place, n_half), slot, lax.rem(place, n_half), at : at + length, :] = value[
                    shard * rows + done : shard * rows + done + length,
                    block * LANES : (block + 1) * LANES,
                ].astype(ref.dtype)
                done += length
    return offset + blocks * step


def put_rows(ref, offset, value):
    for block in range(value.shape[1] // LANES):
        ref[offset + block : offset + block + 1, :] = value[:, block * LANES : (block + 1) * LANES]


def position():
    table_pos = lax.axis_index("table")
    return lax.rem(table_pos, 2), lax.axis_index("row"), table_pos


class Loads:
    def __init__(self, sources, targets, sems):
        self.copies = [
            pltpu.make_async_copy(source, target, sems.at[at])
            for at, (source, target) in enumerate(zip(sources, targets))
        ]
        self.targets = targets
        self.ready = set()
        for copy in self.copies:
            copy.start()

    def __call__(self, at):
        if at not in self.ready:
            self.copies[at].wait()
            self.ready.add(at)
        return self.targets[at][...]


def as_row(value):
    return value.reshape(1, value.shape[-1])


def front_kernel(*refs):
    sources, outs, targets = refs[:11], refs[11:16], refs[16:27]
    halves, thirds, sems = refs[27:]
    send, keep, crossed_t_out, first_out, small = outs
    load = Loads(sources, targets, sems)
    core, row_pos, table_pos = position()
    places = places_of(lax.div(table_pos, 2), 2 * send.shape[2])
    stacked = jnp.concatenate([load(0), load(1)], axis=1)
    cross_down = load(2)
    reduced = matmul(stacked, cross_down).astype(bf16)
    widened = matmul(reduced, load(3)) + as_row(load(4))
    wide = stacked.astype(f32)
    crossed = (wide * widened + wide).astype(bf16)
    pre_first = matmul(crossed, load(5)) + as_row(load(6))
    sig_first = jax.nn.sigmoid(pre_first)
    act_first = (pre_first * sig_first).astype(bf16)
    slope_first = sig_first * (1.0 + pre_first * (1.0 - sig_first))
    w_hidden2 = load(7)
    pre_second = matmul(act_first, w_hidden2) + as_row(load(8))
    sig_second = jax.nn.sigmoid(pre_second)
    act_second = (pre_second * sig_second).astype(bf16).astype(f32)
    slope_second = sig_second * (1.0 + pre_second * (1.0 - sig_second))
    w_logit = as_row(load(9))
    logits = jnp.sum(act_second * w_logit, axis=1, keepdims=True)
    labels = as_row(load(10))
    count = labels.shape[1]
    same = lax.broadcasted_iota(jnp.int32, (count, count), 0) == lax.broadcasted_iota(
        jnp.int32, (count, count), 1
    )
    label_col = jnp.sum(jnp.where(same, labels.astype(f32), 0.0), axis=1, keepdims=True)
    delta_logit = loss_scale * (jax.nn.sigmoid(logits) - label_col)
    delta_second = (delta_logit * w_logit * slope_second).astype(bf16)
    put_rows(small, 16, jnp.sum(act_second * delta_logit, axis=0, keepdims=True))
    put_rows(small, 8, jnp.sum(delta_second.astype(f32), axis=0, keepdims=True))
    half = halves.shape[2]
    halves[0] = delta_second[:, :half]
    halves[1] = delta_second[:, half:]
    delta_first = (matmul_rt(delta_second, w_hidden2) * slope_first).astype(bf16)
    first_out[...] = delta_first
    put_rows(small, 0, jnp.sum(delta_first.astype(f32), axis=0, keepdims=True))
    part = thirds.shape[2]
    thirds[0] = delta_first[:, :part]
    thirds[1] = delta_first[:, half : half + part]
    act_t = act_first.T
    crossed_t = crossed.T
    crossed_t_out[...] = crossed_t
    for ref, who in ((send, 1 - core), (keep, core)):
        offset = put_blocks(ref, row_pos, places, 0, matmul(act_t, halves[who]))
        put_blocks(ref, row_pos, places, offset, matmul(crossed_t, thirds[who]))


def middle_kernel(n_z, *refs):
    sources, send, keep = refs[:9], refs[9], refs[10]
    pooled_outs = refs[11 : 11 + n_z]
    rest = refs[11 + n_z :]
    targets = rest[:9]
    by_group, wide_delta, half_delta, sixths, small, sems = rest[9:]
    load = Loads(sources, targets, sems)
    core, row_pos, table_pos = position()
    z_pos = lax.div(table_pos, 2)
    places = places_of(z_pos, 2 * send.shape[2])
    stacked = jnp.concatenate([load(0), load(1)], axis=1)
    cross_down = load(2)
    reduced = matmul(stacked, cross_down).astype(bf16)
    cross_up = load(3)
    widened = matmul(reduced, cross_up) + as_row(load(4))
    delta_first = load(5)
    delta_crossed = matmul_rt(delta_first, load(6))
    delta_widened = (delta_crossed * stacked.astype(f32)).astype(bf16)
    wide_delta[...] = delta_widened
    delta_reduced = matmul_rt(delta_widened, cross_up).astype(bf16)
    delta_stacked = delta_crossed * (widened + 1.0) + matmul_rt(delta_reduced, cross_down)
    width = targets[0].shape[1]
    per_group = by_group.shape[2]
    for table in range(2 * n_z * per_group):
        group = table // per_group
        by_group[group // 2, group % 2, table % per_group] = delta_stacked[
            :, width * (table + 1) : width * (table + 2)
        ].astype(bf16)
    for which in range(n_z):
        pooled_outs[which][0] = by_group[z_pos ^ which, core]
        pooled_outs[which][1] = by_group[z_pos ^ which, 1 - core]

    n_row, rank, feat = send.shape[1], delta_reduced.shape[1], delta_widened.shape[1]
    hid = delta_first.shape[1]
    part = hid // 2 - sixths.shape[2]
    half_delta[0] = delta_reduced[:, : rank // 2]
    half_delta[1] = delta_reduced[:, rank // 2 :]
    sixths[0] = delta_first[:, part : hid // 2]
    sixths[1] = delta_first[:, hid // 2 + part :]
    put_rows(small, 24, jnp.sum(delta_widened.astype(f32), axis=0, keepdims=True))
    small[0:24, :] = load(8)
    small[41:48, :] = jnp.zeros((7, LANES), f32)
    sums = jnp.concatenate([small[...]] * n_row, axis=0)
    crossed_t, reduced_t, stacked_t = load(7), reduced.T, stacked.T
    for ref, who in ((send, 1 - core), (keep, core)):
        offset = put_blocks(ref, row_pos, places, 0, matmul(crossed_t, sixths[who]))
        offset = put_blocks(ref, row_pos, places, offset, matmul(stacked_t, half_delta[who]))
        start = pl.multiple_of(who * (feat - SPAN), LANES)
        offset = put_blocks(
            ref, row_pos, places, offset, matmul(reduced_t, wide_delta[:, pl.ds(start, SPAN)])
        )
        offset = put_blocks(ref, row_pos, places, offset, sums)
        tail = 2 * ref.shape[2] * ref.shape[3] - offset
        if tail:
            put_blocks(ref, row_pos, places, offset, jnp.zeros((n_row * tail, LANES), f32))


def select_kernel(n_z, *refs):
    for which in range(n_z):
        out = refs[len(refs) - 2 + which // (n_z // 2)]
        out[which % (n_z // 2)] = refs[which][1]


def count_kernel(n_row, table, hot, n_z, slots, *rest):
    direct, crossed, out = rest[:n_z], rest[n_z : n_z + 2], rest[-1]
    near = n_z // 2
    block = out.shape[1]
    samples = crossed[0].shape[2]
    core, row_pos, table_pos = position()
    z_pos = lax.div(table_pos, 2)
    base = (pl.program_id(0) ^ row_pos) * block
    names = lax.broadcasted_iota(jnp.int16, (block, samples), 0)
    total = jnp.zeros((block, out.shape[2]), f32)
    one = jnp.ones((block, samples), bf16)
    zero = jnp.zeros((block, samples), bf16)
    for which in range(n_z):
        far = crossed[which // near]
        for held, who in ((direct[which][0, table], core), (far[which % near, table], 1 - core)):
            source = 2 * (z_pos ^ which) + who
            start = pl.multiple_of((source * n_row + row_pos) * samples, LANES)
            lines = slots[table, :, pl.ds(start, samples)] - base
            lines = jnp.where((lines >= 0) & (lines < block), lines, block).astype(jnp.int16)
            counts = zero
            for look in range(hot):
                line = jnp.broadcast_to(lines[look : look + 1, :], (block, samples))
                counts = counts + jnp.where(line == names, one, zero)
            total = total + matmul(counts, held)
    out[0] = total.astype(out.dtype)


def unpack_kernel(*refs):
    parts = refs[0:8]
    g_down, g_up, g_first, g_second = refs[8:12]
    small_outs = refs[12:16]
    held, small = refs[16:18], refs[18]
    core, row_pos, table_pos = position()
    z_pos = lax.div(table_pos, 2)
    for stream in range(2):
        lower, upper, lower_other, upper_other = parts[4 * stream : 4 * stream + 4]
        ref = held[stream]
        rows = lower.shape[1]
        n_z = 2 * lower.shape[0]
        z_bits = n_z.bit_length() - 1
        for who, pieces in ((core, (lower, upper)), (1 - core, (lower_other, upper_other))):
            for place in range(n_z):
                start = pl.multiple_of((reverse_bits(place, z_bits) ^ z_pos) * rows, 16)
                ref[who, pl.ds(start, rows), :] = pieces[place // (n_z // 2)][place % (n_z // 2)]
    front, back = held

    def take(ref, out, half, offset, columns):
        rows = out.shape[0]
        step = round_up(rows, 16)
        for column in columns:
            out[:, column * LANES : (column + 1) * LANES] = ref[
                half, offset : offset + rows, :
            ].astype(f32)
            offset += step
        return offset

    for half in range(2):
        blocks = g_second.shape[1] // LANES // 2
        offset = take(front, g_second, half, 0, range(half * blocks, (half + 1) * blocks))
        blocks = g_first.shape[1] // LANES // 2
        early = blocks - blocks // 4
        take(front, g_first, half, offset, range(half * blocks, half * blocks + early))
        offset = take(back, g_first, half, 0, range(half * blocks + early, (half + 1) * blocks))
        blocks = g_down.shape[1] // LANES // 2
        offset = take(back, g_down, half, offset, range(half * blocks, (half + 1) * blocks))
        blocks = g_up.shape[1] // LANES
        offset = take(back, g_up, half, offset, range(half * (blocks - 9), half * (blocks - 9) + 9))
    small[0:48, :] = back[0, offset : offset + 48, :].astype(f32)
    small[48:, :] = jnp.zeros((small.shape[0] - 48, LANES), f32)
    for out, first in zip(small_outs, (24, 0, 8, 16)):
        share = out.shape[0]
        begin = row_pos * share
        row, lane = lax.div(begin, LANES), lax.rem(begin, LANES)
        lanes = lax.broadcasted_iota(jnp.int32, (1, LANES), 1)
        for start in range(0, share, LANES):
            length = min(LANES, share - start)
            this = small[pl.ds(first + row + start // LANES, 1), :]
            later = small[pl.ds(first + row + start // LANES + 1, 1), :]
            both = jnp.where(lanes < lane, later, this)
            turned = pltpu.roll(both, lax.rem(LANES - lane, LANES), 1)
            out[start : start + length] = turned.reshape(LANES)[:length]


def whole(memory=pltpu.VMEM):
    return pl.BlockSpec(memory_space=memory)


def no_cost():
    return pl.CostEstimate(flops=0, transcendentals=0, bytes_accessed=0)


def call(body, outs, scratch, in_specs, name, mib):
    return pl.pallas_call(
        body,
        out_shape=outs,
        in_specs=in_specs,
        out_specs=[whole()] * len(outs),
        scratch_shapes=scratch,
        compiler_params=pltpu.CompilerParams(vmem_limit_bytes=mib * MIB),
        cost_estimate=no_cost(),
        name=name,
    )


def after(values, deps):
    return list(lax.optimization_barrier(tuple(values) + tuple(deps))[: len(values)])


def held_like(values):
    return [pltpu.VMEM(value.shape, value.dtype) for value in values]


def sum_rows_kernel(plan, *refs):
    out = refs[-1]
    for table, terms in enumerate(plan):
        total = None
        for which, picks in terms:
            part = refs[which][picks].astype(f32)
            total = part if total is None else total + part
        out[table] = total


def sum_rows(groups, deps):
    arrays = [array for items in groups for array, _ in items]
    plan, count = [], 0
    for items in groups:
        plan.append([(count + at, tuple(picks)) for at, (_, picks) in enumerate(items)])
        count += len(items)
    kept = [pick.stop - pick.start for pick in groups[0][0][1] if isinstance(pick, slice)]
    return call(
        functools.partial(sum_rows_kernel, plan),
        [jax.ShapeDtypeStruct((len(groups), *kept), f32)],
        [],
        [whole()] * len(arrays) + [whole(pl.ANY)] * len(deps),
        "rows",
        24,
    )(*arrays, *deps)[0]


def sum_kernel(plan, n_in, *refs):
    outs = refs[len(refs) - len(plan) :]
    for out, terms in zip(outs, plan):
        rows = out.shape[-2]
        chunk = next(size for size in (64, 48, 80, 32, 16, 8, rows) if rows % size == 0)

        def one_chunk(at, carry, out=out, terms=terms, chunk=chunk):
            window = pl.ds(pl.multiple_of(at * chunk, chunk), chunk)
            for lead in itertools.product(*[range(size) for size in out.shape[:-2]]):
                total = None
                for which, picks in terms:
                    axes, place = iter(lead), []
                    for pick in picks[:-2]:
                        place.append(pick.start + next(axes) if isinstance(pick, slice) else pick)
                    part = refs[which][(*place, window, slice(None))].astype(f32)
                    total = part if total is None else total + part
                out[(*lead, window, slice(None))] = total.astype(out.dtype)
            return carry

        lax.fori_loop(0, rows // chunk, one_chunk, 0)


def fetch_sum_kernel(plan, n_in, *refs):
    outs = refs[n_in : n_in + len(plan)]
    held, sems = refs[n_in + len(plan) : -1], refs[-1]
    copies, by_out = [], []
    for terms in plan:
        parts = []
        for which, picks in terms:
            at = len(copies)
            place = tuple(
                pl.ds(pick.start, pick.stop - pick.start) if isinstance(pick, slice) else pick
                for pick in picks
            )
            copies.append(pltpu.make_async_copy(refs[which].at[place], held[at], sems.at[at]))
            parts.append((at, tuple(slice(0, size) for size in held[at].shape)))
        by_out.append(parts)
    for copy in copies:
        copy.start()
    for out, parts in zip(outs, by_out):
        for at, _ in parts:
            copies[at].wait()
        sum_kernel([parts], 0, *held, out)


def fetch_sums(groups, deps):
    arrays, plan, shapes, scratch = [], [], [], []
    for items in groups:
        kept = tuple(pick.stop - pick.start for pick in items[0][1] if isinstance(pick, slice))
        shapes.append(jax.ShapeDtypeStruct(kept, bf16))
        terms = []
        for array, picks in items:
            found = [at for at, known in enumerate(arrays) if known is array]
            if not found:
                arrays.append(array)
            terms.append((found[0] if found else len(arrays) - 1, tuple(picks)))
            scratch.append(pltpu.VMEM(kept, array.dtype))
        plan.append(terms)
    n_in = len(arrays) + len(deps)
    return call(
        functools.partial(fetch_sum_kernel, plan, n_in),
        shapes,
        scratch + [pltpu.SemaphoreType.DMA((len(scratch),))],
        [whole(pltpu.HBM)] * len(arrays) + [whole(pl.ANY)] * len(deps),
        "first_sums",
        24,
    )(*arrays, *deps)


def take_sums(groups, deps, dtype=bf16):
    arrays, plan, shapes = [], [], []
    for items in groups:
        terms = []
        for array, picks in items:
            found = [at for at, known in enumerate(arrays) if known is array]
            if not found:
                arrays.append(array)
            terms.append((found[0] if found else len(arrays) - 1, tuple(picks)))
        plan.append(terms)
        kept = [pick.stop - pick.start for pick in items[0][1] if isinstance(pick, slice)]
        shapes.append(jax.ShapeDtypeStruct(tuple(kept), dtype))
    return call(
        functools.partial(sum_kernel, plan, len(arrays)),
        shapes,
        [],
        [whole()] * len(arrays) + [whole(pl.ANY)] * len(deps),
        "sums",
        24,
    )(*arrays, *deps)


def local(
    dense_feat,
    pooled,
    labels,
    cross_down,
    cross_up,
    cross_bias,
    w_hidden1,
    bias1,
    w_hidden2,
    bias2,
    w_logit,
    lookup_slots,
):
    n_table = lax.axis_size("table")
    n_row = lax.axis_size("row")
    n_z = n_table // 2
    row_bits = n_row.bit_length() - 1
    z_bits = n_z.bit_length() - 1
    batch, width = dense_feat.shape
    feat, rank = cross_down.shape
    hid = w_hidden1.shape[1]
    tab_grp, _, hot = lookup_slots.shape
    u_shard = batch * n_table * hot // 16

    def swap_cores(value):
        return lax.ppermute(value, "table", [(at, at ^ 1) for at in range(n_table)])

    def swap_z(value, which):
        return lax.ppermute(value, "table", [(at, at ^ (2 * which)) for at in range(n_table)])

    def swap_row(value, bit):
        return lax.ppermute(value, "row", [(at, at ^ (1 << bit)) for at in range(n_row)])

    late = hid // 8
    early = hid // 2 - late
    rows_front = (hid // 2 // LANES) * round_up(hid // n_row, 16)
    rows_front += (early // LANES) * round_up(feat // n_row, 16)
    rows_back = (late // LANES) * round_up(feat // n_row, 16)
    rows_back += (rank // 2 // LANES) * round_up(feat // n_row, 16)
    rows_back += 9 * round_up(rank // n_row, 16) + 48
    rows_front, rows_back = (round_up(rows, 16 * n_z) for rows in (rows_front, rows_back))

    def packed(rows):
        return jax.ShapeDtypeStruct((2, n_row, n_z // 2, rows // n_z, LANES), bf16)

    def wide(*shape):
        return jax.ShapeDtypeStruct(shape, bf16)

    hbm, vmem, anywhere = whole(pltpu.HBM), whole(), whole(pl.ANY)

    sources = (
        dense_feat,
        pooled,
        cross_down,
        cross_up,
        cross_bias,
        w_hidden1,
        bias1,
        w_hidden2,
        bias2,
        w_logit,
        labels,
    )
    send1, keep1, crossed_t, delta_first, small = call(
        front_kernel,
        [packed(rows_front)] * 2
        + [wide(feat, batch), wide(batch, hid), jax.ShapeDtypeStruct((24, LANES), f32)],
        held_like(sources)
        + [
            pltpu.VMEM((2, batch, hid // 2), bf16),
            pltpu.VMEM((2, batch, early), bf16),
            pltpu.SemaphoreType.DMA((len(sources),)),
        ],
        [hbm] * len(sources),
        "front",
        60,
    )(*sources)
    got1 = swap_cores(send1)

    sources = (
        dense_feat,
        pooled,
        cross_down,
        cross_up,
        cross_bias,
        delta_first,
        w_hidden1,
        crossed_t,
        small,
    )
    send2, keep2, *pooled_out = call(
        functools.partial(middle_kernel, n_z),
        [packed(rows_back)] * 2 + [wide(2, tab_grp, batch, width)] * n_z,
        held_like(sources)
        + [
            pltpu.VMEM((n_z, 2, tab_grp, batch, width), bf16),
            pltpu.VMEM((batch, feat), bf16),
            pltpu.VMEM((2, batch, rank // 2), bf16),
            pltpu.VMEM((2, batch, late), bf16),
            pltpu.VMEM((48, LANES), f32),
            pltpu.SemaphoreType.DMA((len(sources),)),
        ],
        [hbm] * len(sources),
        "middle",
        60,
    )(*sources)
    got2 = swap_cores(send2)

    low_first = tuple(range(row_bits))
    high_first = low_first[::-1]

    class Terms:
        def __init__(self, arrays, picks):
            self.items = []
            for array in arrays:
                self.add(array, picks)

        def add(self, array, picks=()):
            whole_axes = [slice(0, size) for size in array.shape[len(picks) :]]
            self.items.append((array, list(picks) + whole_axes))

        def narrowed(self, axis, what):
            items = []
            for array, picks in self.items:
                at = [number for number, pick in enumerate(picks) if isinstance(pick, slice)][axis]
                items.append((array, picks[:at] + [what] + picks[at + 1 :]))
            return items

        def far_near(self, axis, near, far):
            sent = self.narrowed(axis, far)
            self.items = self.narrowed(axis, near)
            return sent

    class Halving(Terms):
        def __init__(self, arrays, order, picks=()):
            dims = len(picks)
            arrays = [
                array.reshape(array.shape[:dims] + (2,) * row_bits + array.shape[dims + 1 :])
                for array in arrays
            ]
            super().__init__(arrays, picks)
            self.order, self.left = order, list(range(row_bits - 1, -1, -1))

        def part(self, at):
            axis = self.left.index(self.order[at])
            self.left.remove(self.order[at])
            return self.far_near(axis, 0, 1)

    def row_step(streams, at, deps):
        sent = take_sums([stream.part(at) for stream in streams], deps)
        for stream, value in zip(streams, sent):
            stream.add(swap_row(value, stream.order[at]))
        return list(sent)

    class Dense:
        def __init__(self, keep, got):
            self.low = Halving([keep, got], low_first, [0])
            self.high = Halving([keep, got], high_first, [1])

        def first_step(self, deps):
            halves = (self.low, self.high)
            sent = fetch_sums([half.part(0) for half in halves], deps)
            self.near = [half.items for half in halves]
            for half, value in zip(halves, sent):
                half.items = []
                half.add(swap_row(value, half.order[0]))
            return list(sent)

        def settle(self, deps):
            for half, value in zip((self.low, self.high), fetch_sums(self.near, deps)):
                half.add(value)
                half.items.reverse()

        def row_step(self, at, deps):
            deps = [*deps, self.low.items[-1][0], self.high.items[-1][0]]
            return row_step((self.low, self.high), at, deps)

        def z_step(self, stage, deps):
            middle = n_z >> (stage + 1)
            items, deps = self.high.items, [*deps, self.low.items[-1][0]]
            if stage > 0:
                items = self.low.far_near(0, slice(0, middle), slice(middle, 2 * middle))
            (sent,) = take_sums([items], deps)
            self.low.add(swap_z(sent, 1 << stage))
            return [sent]

        def z_own(self, deps):
            (self.own,) = take_sums([self.low.items], deps)
            self.back = swap_z(self.own, 1 << (z_bits - 1)) if z_bits > 1 else None
            return [self.own]

        def z_back(self, deps):
            for stage in range(z_bits - 1, 0, -1):
                if stage < z_bits - 1:
                    self.back = swap_z(self.own, 1 << stage)
                (back,) = after([self.back], deps)
                self.own = jnp.concatenate([self.own, back], axis=0)
            far = swap_z(self.own, 1)
            self.pieces = [self.own, far, swap_cores(self.own), swap_cores(far)]
            return [self.own]

    (got1,) = after([got1], [pooled_out[0]])
    one, two = Dense(keep1, got1), Dense(keep2, got2)
    one.first_step([])
    values, half = {0: pooled_out[0]}, n_z // 2
    for which in [half, *range(1, half)]:
        values[which] = swap_z(pooled_out[which], which)
    for which in range(half + 1, n_z):
        (moved,) = after([pooled_out[which]], [values[half], values[which - half]])
        values[which] = swap_z(moved, which)
    one.settle([values[1]])
    last = [values[which] for which in range(1, half + 1)]
    for at in range(1, row_bits):
        last = one.row_step(at, last)
    last = two.first_step(last)
    last = one.z_step(0, last)
    two.settle(last)
    values = [values[which] for which in range(n_z)]
    far_values = call(
        functools.partial(select_kernel, n_z),
        [wide(n_z // 2, tab_grp, batch, width)] * 2,
        [],
        [vmem] * n_z + [anywhere],
        "select",
        8,
    )(*values, last[0])
    values += [swap_cores(value) for value in far_values]
    slots = jnp.transpose(lookup_slots, (0, 2, 1))
    last, shares = [far_values[0]], []
    for table in range(tab_grp):
        sums = pl.pallas_call(
            functools.partial(count_kernel, n_row, table, hot, n_z),
            out_shape=wide(n_row, u_shard, width),
            grid=(n_row,),
            in_specs=[vmem] * (3 + n_z) + [anywhere],
            out_specs=pl.BlockSpec((1, u_shard, width), lambda at: (at, 0, 0)),
            compiler_params=pltpu.CompilerParams(vmem_limit_bytes=16 * MIB),
            cost_estimate=no_cost(),
            name="counts",
        )(slots, *values, last[0])
        shares.append(Halving([sums], high_first if table % 2 else low_first))
        last = [sums]
        if table == 0:
            for stage in range(1, z_bits):
                last = one.z_step(stage, last)
            for at in range(1, row_bits):
                last = two.row_step(at, last)
            last = two.z_step(0, last)
    last = row_step(shares, 0, last)
    last = one.z_own(last)
    for stage in range(1, z_bits):
        last = two.z_step(stage, last)
    for at in range(1, row_bits):
        last = row_step(shares, at, last)
    last = two.z_own(last)
    last = one.z_back(last)
    row_grads = sum_rows([share.items for share in shares], last)
    two.z_back([row_grads])

    g_down, g_up, g_first, g_second, g_cbias, g_bias1, g_bias2, g_logit = call(
        unpack_kernel,
        [
            jax.ShapeDtypeStruct((feat // n_row, rank), f32),
            jax.ShapeDtypeStruct((rank // n_row, feat), f32),
            jax.ShapeDtypeStruct((feat // n_row, hid), f32),
            jax.ShapeDtypeStruct((hid // n_row, hid), f32),
            jax.ShapeDtypeStruct((feat // n_row,), f32),
        ]
        + [jax.ShapeDtypeStruct((hid // n_row,), f32)] * 3,
        [pltpu.VMEM((2, rows, LANES), bf16) for rows in (rows_front, rows_back)]
        + [pltpu.VMEM((56, LANES), f32)],
        [vmem] * 8,
        "unpack",
        24,
    )(*one.pieces, *two.pieces)
    return (row_grads, g_down, g_up, g_cbias, g_first, g_bias1, g_second, g_bias2, g_logit)


def solution(mesh):
    in_specs = (
        P(("table", "row"), None),
        P(("table", "row"), None),
        P(("table", "row")),
        P(),
        P(),
        P(),
        P(),
        P(),
        P(),
        P(),
        P(),
        P("table", None, None),
    )
    out_specs = (
        P("table", "row", None),
        P("row", None),
        P("row", None),
        P("row"),
        P("row", None),
        P("row"),
        P("row", None),
        P("row"),
        P("row"),
    )
    return jax.shard_map(local, mesh=mesh, in_specs=in_specs, out_specs=out_specs, check_vma=False)
```

```python
import functools
import itertools

import jax
import jax.numpy as jnp
from jax import lax
from jax.experimental import pallas as pl
from jax.experimental.pallas import tpu as pltpu
from jax.sharding import PartitionSpec as P

loss_scale = 16.0
LANES = 128
SPAN = 9 * LANES
MIB = 1024 * 1024
bf16 = jnp.bfloat16
f32 = jnp.float32


def round_up(value, unit):
    return -(-value // unit) * unit


def matmul(left, right):
    return jnp.dot(left, right, preferred_element_type=f32)


def matmul_rt(left, right):
    return lax.dot_general(left, right, (((1,), (1,)), ((), ())), preferred_element_type=f32)


def reverse_bits(value, bits):
    out = 0
    for bit in range(bits):
        out = out | (((value >> bit) & 1) << (bits - 1 - bit))
    return out


def places_of(z_pos, n_z):
    bits = n_z.bit_length() - 1
    return [reverse_bits(z_pos ^ quarter, bits) for quarter in range(n_z)]


def put_blocks(ref, row_pos, places, offset, value):
    shards, n_half, rows_q = ref.shape[1], ref.shape[2], ref.shape[3]
    rows = value.shape[0] // shards
    step = round_up(rows, 16)
    blocks = value.shape[1] // LANES
    for shard in range(shards):
        slot = shard ^ row_pos
        for block in range(blocks):
            done = 0
            while done < rows:
                quarter, at = divmod(offset + block * step + done, rows_q)
                length = min(rows - done, rows_q - at)
                place = places[quarter]
                ref[lax.div(place, n_half), slot, lax.rem(place, n_half), at : at + length, :] = value[
                    shard * rows + done : shard * rows + done + length,
                    block * LANES : (block + 1) * LANES,
                ].astype(ref.dtype)
                done += length
    return offset + blocks * step


def put_rows(ref, offset, value):
    for block in range(value.shape[1] // LANES):
        ref[offset + block : offset + block + 1, :] = value[:, block * LANES : (block + 1) * LANES]


def position():
    table_pos = lax.axis_index("table")
    return lax.rem(table_pos, 2), lax.axis_index("row"), table_pos


class Loads:
    def __init__(self, sources, targets, sems):
        self.copies = [
            pltpu.make_async_copy(source, target, sems.at[at])
            for at, (source, target) in enumerate(zip(sources, targets))
        ]
        self.targets = targets
        self.ready = set()
        for copy in self.copies:
            copy.start()

    def __call__(self, at):
        if at not in self.ready:
            self.copies[at].wait()
            self.ready.add(at)
        return self.targets[at][...]


def as_row(value):
    return value.reshape(1, value.shape[-1])


def front_kernel(*refs):
    sources, outs, targets = refs[:11], refs[11:16], refs[16:27]
    halves, thirds, sems = refs[27:]
    send, keep, crossed_t_out, first_out, small = outs
    load = Loads(sources, targets, sems)
    core, row_pos, table_pos = position()
    places = places_of(lax.div(table_pos, 2), 2 * send.shape[2])
    stacked = jnp.concatenate([load(0), load(1)], axis=1)
    cross_down = load(2)
    reduced = matmul(stacked, cross_down).astype(bf16)
    widened = matmul(reduced, load(3)) + as_row(load(4))
    wide = stacked.astype(f32)
    crossed = (wide * widened + wide).astype(bf16)
    pre_first = matmul(crossed, load(5)) + as_row(load(6))
    sig_first = jax.nn.sigmoid(pre_first)
    act_first = (pre_first * sig_first).astype(bf16)
    slope_first = sig_first * (1.0 + pre_first * (1.0 - sig_first))
    w_hidden2 = load(7)
    pre_second = matmul(act_first, w_hidden2) + as_row(load(8))
    sig_second = jax.nn.sigmoid(pre_second)
    act_second = (pre_second * sig_second).astype(bf16).astype(f32)
    slope_second = sig_second * (1.0 + pre_second * (1.0 - sig_second))
    w_logit = as_row(load(9))
    logits = jnp.sum(act_second * w_logit, axis=1, keepdims=True)
    labels = as_row(load(10))
    count = labels.shape[1]
    same = lax.broadcasted_iota(jnp.int32, (count, count), 0) == lax.broadcasted_iota(
        jnp.int32, (count, count), 1
    )
    label_col = jnp.sum(jnp.where(same, labels.astype(f32), 0.0), axis=1, keepdims=True)
    delta_logit = loss_scale * (jax.nn.sigmoid(logits) - label_col)
    delta_second = (delta_logit * w_logit * slope_second).astype(bf16)
    put_rows(small, 16, jnp.sum(act_second * delta_logit, axis=0, keepdims=True))
    put_rows(small, 8, jnp.sum(delta_second.astype(f32), axis=0, keepdims=True))
    half = halves.shape[2]
    halves[0] = delta_second[:, :half]
    halves[1] = delta_second[:, half:]
    delta_first = (matmul_rt(delta_second, w_hidden2) * slope_first).astype(bf16)
    first_out[...] = delta_first
    put_rows(small, 0, jnp.sum(delta_first.astype(f32), axis=0, keepdims=True))
    part = thirds.shape[2]
    thirds[0] = delta_first[:, :part]
    thirds[1] = delta_first[:, half : half + part]
    act_t = act_first.T
    crossed_t = crossed.T
    crossed_t_out[...] = crossed_t
    for ref, who in ((send, 1 - core), (keep, core)):
        offset = put_blocks(ref, row_pos, places, 0, matmul(act_t, halves[who]))
        put_blocks(ref, row_pos, places, offset, matmul(crossed_t, thirds[who]))


def middle_kernel(n_z, *refs):
    sources, send, keep = refs[:9], refs[9], refs[10]
    pooled_outs = refs[11 : 11 + n_z]
    rest = refs[11 + n_z :]
    targets = rest[:9]
    by_group, wide_delta, half_delta, sixths, small, sems = rest[9:]
    load = Loads(sources, targets, sems)
    core, row_pos, table_pos = position()
    z_pos = lax.div(table_pos, 2)
    places = places_of(z_pos, 2 * send.shape[2])
    stacked = jnp.concatenate([load(0), load(1)], axis=1)
    cross_down = load(2)
    reduced = matmul(stacked, cross_down).astype(bf16)
    cross_up = load(3)
    widened = matmul(reduced, cross_up) + as_row(load(4))
    delta_first = load(5)
    delta_crossed = matmul_rt(delta_first, load(6))
    delta_widened = (delta_crossed * stacked.astype(f32)).astype(bf16)
    wide_delta[...] = delta_widened
    delta_reduced = matmul_rt(delta_widened, cross_up).astype(bf16)
    delta_stacked = delta_crossed * (widened + 1.0) + matmul_rt(delta_reduced, cross_down)
    width = targets[0].shape[1]
    per_group = by_group.shape[2]
    for table in range(2 * n_z * per_group):
        group = table // per_group
        by_group[group // 2, group % 2, table % per_group] = delta_stacked[
            :, width * (table + 1) : width * (table + 2)
        ].astype(bf16)
    for which in range(n_z):
        pooled_outs[which][0] = by_group[z_pos ^ which, core]
        pooled_outs[which][1] = by_group[z_pos ^ which, 1 - core]

    n_row, rank, feat = send.shape[1], delta_reduced.shape[1], delta_widened.shape[1]
    hid = delta_first.shape[1]
    part = hid // 2 - sixths.shape[2]
    half_delta[0] = delta_reduced[:, : rank // 2]
    half_delta[1] = delta_reduced[:, rank // 2 :]
    sixths[0] = delta_first[:, part : hid // 2]
    sixths[1] = delta_first[:, hid // 2 + part :]
    put_rows(small, 24, jnp.sum(delta_widened.astype(f32), axis=0, keepdims=True))
    small[0:24, :] = load(8)
    small[41:48, :] = jnp.zeros((7, LANES), f32)
    sums = jnp.concatenate([small[...]] * n_row, axis=0)
    crossed_t, reduced_t, stacked_t = load(7), reduced.T, stacked.T
    for ref, who in ((send, 1 - core), (keep, core)):
        offset = put_blocks(ref, row_pos, places, 0, matmul(crossed_t, sixths[who]))
        offset = put_blocks(ref, row_pos, places, offset, matmul(stacked_t, half_delta[who]))
        start = pl.multiple_of(who * (feat - SPAN), LANES)
        offset = put_blocks(
            ref, row_pos, places, offset, matmul(reduced_t, wide_delta[:, pl.ds(start, SPAN)])
        )
        offset = put_blocks(ref, row_pos, places, offset, sums)
        tail = 2 * ref.shape[2] * ref.shape[3] - offset
        if tail:
            put_blocks(ref, row_pos, places, offset, jnp.zeros((n_row * tail, LANES), f32))


def select_kernel(n_z, *refs):
    for which in range(n_z):
        out = refs[len(refs) - 2 + which // (n_z // 2)]
        out[which % (n_z // 2)] = refs[which][1]


def count_kernel(n_row, table, hot, n_z, slots, *rest):
    direct, crossed, out = rest[:n_z], rest[n_z : n_z + 2], rest[-1]
    near = n_z // 2
    block = out.shape[1]
    samples = crossed[0].shape[2]
    core, row_pos, table_pos = position()
    z_pos = lax.div(table_pos, 2)
    base = (pl.program_id(0) ^ row_pos) * block
    names = lax.broadcasted_iota(jnp.int16, (block, samples), 0)
    total = jnp.zeros((block, out.shape[2]), f32)
    one = jnp.ones((block, samples), bf16)
    zero = jnp.zeros((block, samples), bf16)
    for which in range(n_z):
        far = crossed[which // near]
        for held, who in ((direct[which][0, table], core), (far[which % near, table], 1 - core)):
            source = 2 * (z_pos ^ which) + who
            start = pl.multiple_of((source * n_row + row_pos) * samples, LANES)
            lines = slots[table, :, pl.ds(start, samples)] - base
            lines = jnp.where((lines >= 0) & (lines < block), lines, block).astype(jnp.int16)
            counts = zero
            for look in range(hot):
                line = jnp.broadcast_to(lines[look : look + 1, :], (block, samples))
                counts = counts + jnp.where(line == names, one, zero)
            total = total + matmul(counts, held)
    out[0] = total.astype(out.dtype)


def unpack_kernel(*refs):
    parts = refs[0:8]
    outs = refs[8:12]
    small_outs = refs[12:16]
    held, small = refs[16:18], refs[18]
    g_down, g_up, g_first, g_second = made = refs[19:23]
    sems = refs[23]
    copies = []

    def send(which, columns):
        span = (slice(None), pl.ds(columns.start * LANES, len(columns) * LANES))
        copy = pltpu.make_async_copy(
            made[which].at[span], outs[which].at[span], sems.at[len(copies)]
        )
        copy.start()
        copies.append(copy)

    core, row_pos, table_pos = position()
    z_pos = lax.div(table_pos, 2)
    for stream in range(2):
        lower, upper, lower_other, upper_other = parts[4 * stream : 4 * stream + 4]
        ref = held[stream]
        rows = lower.shape[1]
        n_z = 2 * lower.shape[0]
        z_bits = n_z.bit_length() - 1
        for who, pieces in ((core, (lower, upper)), (1 - core, (lower_other, upper_other))):
            for place in range(n_z):
                start = pl.multiple_of((reverse_bits(place, z_bits) ^ z_pos) * rows, 16)
                ref[who, pl.ds(start, rows), :] = pieces[place // (n_z // 2)][place % (n_z // 2)]
    front, back = held

    def take(ref, out, half, offset, columns):
        rows = out.shape[0]
        step = round_up(rows, 16)
        for column in columns:
            out[:, column * LANES : (column + 1) * LANES] = ref[
                half, offset : offset + rows, :
            ].astype(f32)
            offset += step
        return offset

    blocks = g_first.shape[1] // LANES // 2
    early = blocks - blocks // 4
    for half in range(2):
        count = g_second.shape[1] // LANES // 2
        columns = range(half * count, (half + 1) * count)
        offset = take(front, g_second, half, 0, columns)
        send(3, columns)
        columns = range(half * blocks, half * blocks + early)
        take(front, g_first, half, offset, columns)
        send(2, columns)
    for half in range(2):
        columns = range(half * blocks + early, (half + 1) * blocks)
        offset = take(back, g_first, half, 0, columns)
        send(2, columns)
        count = g_down.shape[1] // LANES // 2
        columns = range(half * count, (half + 1) * count)
        offset = take(back, g_down, half, offset, columns)
        send(0, columns)
        count = g_up.shape[1] // LANES
        columns = range(half * (count - 9), half * (count - 9) + 9)
        offset = take(back, g_up, half, offset, columns)
    send(1, range(g_up.shape[1] // LANES))
    small[0:48, :] = back[0, offset : offset + 48, :].astype(f32)
    small[48:, :] = jnp.zeros((small.shape[0] - 48, LANES), f32)
    for out, first in zip(small_outs, (24, 0, 8, 16)):
        share = out.shape[0]
        begin = row_pos * share
        row, lane = lax.div(begin, LANES), lax.rem(begin, LANES)
        lanes = lax.broadcasted_iota(jnp.int32, (1, LANES), 1)
        for start in range(0, share, LANES):
            length = min(LANES, share - start)
            this = small[pl.ds(first + row + start // LANES, 1), :]
            later = small[pl.ds(first + row + start // LANES + 1, 1), :]
            both = jnp.where(lanes < lane, later, this)
            turned = pltpu.roll(both, lax.rem(LANES - lane, LANES), 1)
            out[start : start + length] = turned.reshape(LANES)[:length]
    for copy in copies:
        copy.wait()


def whole(memory=pltpu.VMEM):
    return pl.BlockSpec(memory_space=memory)


def no_cost():
    return pl.CostEstimate(flops=0, transcendentals=0, bytes_accessed=0)


def call(body, outs, scratch, in_specs, name, mib):
    return pl.pallas_call(
        body,
        out_shape=outs,
        in_specs=in_specs,
        out_specs=[whole()] * len(outs),
        scratch_shapes=scratch,
        compiler_params=pltpu.CompilerParams(vmem_limit_bytes=mib * MIB),
        cost_estimate=no_cost(),
        name=name,
    )


def after(values, deps):
    return list(lax.optimization_barrier(tuple(values) + tuple(deps))[: len(values)])


def held_like(values):
    return [pltpu.VMEM(value.shape, value.dtype) for value in values]


def sum_rows_kernel(plan, *refs):
    out = refs[-1]
    for table, terms in enumerate(plan):
        total = None
        for which, picks in terms:
            part = refs[which][picks].astype(f32)
            total = part if total is None else total + part
        out[table] = total


def sum_rows(groups, deps):
    arrays = [array for items in groups for array, _ in items]
    plan, count = [], 0
    for items in groups:
        plan.append([(count + at, tuple(picks)) for at, (_, picks) in enumerate(items)])
        count += len(items)
    kept = [pick.stop - pick.start for pick in groups[0][0][1] if isinstance(pick, slice)]
    return call(
        functools.partial(sum_rows_kernel, plan),
        [jax.ShapeDtypeStruct((len(groups), *kept), f32)],
        [],
        [whole()] * len(arrays) + [whole(pl.ANY)] * len(deps),
        "rows",
        24,
    )(*arrays, *deps)[0]


def sum_kernel(plan, n_in, *refs):
    outs = refs[len(refs) - len(plan) :]
    for out, terms in zip(outs, plan):
        rows = out.shape[-2]
        chunk = next(size for size in (64, 48, 80, 32, 16, 8, rows) if rows % size == 0)

        def one_chunk(at, carry, out=out, terms=terms, chunk=chunk):
            window = pl.ds(pl.multiple_of(at * chunk, chunk), chunk)
            for lead in itertools.product(*[range(size) for size in out.shape[:-2]]):
                total = None
                for which, picks in terms:
                    axes, place = iter(lead), []
                    for pick in picks[:-2]:
                        place.append(pick.start + next(axes) if isinstance(pick, slice) else pick)
                    part = refs[which][(*place, window, slice(None))].astype(f32)
                    total = part if total is None else total + part
                out[(*lead, window, slice(None))] = total.astype(out.dtype)
            return carry

        lax.fori_loop(0, rows // chunk, one_chunk, 0)


def fetch_sum_kernel(plan, n_in, *refs):
    outs = refs[n_in : n_in + len(plan)]
    held, sems = refs[n_in + len(plan) : -1], refs[-1]
    copies, by_out = [], []
    for terms in plan:
        parts = []
        for which, picks in terms:
            at = len(copies)
            place = tuple(
                pl.ds(pick.start, pick.stop - pick.start) if isinstance(pick, slice) else pick
                for pick in picks
            )
            copies.append(pltpu.make_async_copy(refs[which].at[place], held[at], sems.at[at]))
            parts.append((at, tuple(slice(0, size) for size in held[at].shape)))
        by_out.append(parts)
    for copy in copies:
        copy.start()
    for out, parts in zip(outs, by_out):
        for at, _ in parts:
            copies[at].wait()
        sum_kernel([parts], 0, *held, out)


def fetch_sums(groups, deps):
    arrays, plan, shapes, scratch = [], [], [], []
    for items in groups:
        kept = tuple(pick.stop - pick.start for pick in items[0][1] if isinstance(pick, slice))
        shapes.append(jax.ShapeDtypeStruct(kept, bf16))
        terms = []
        for array, picks in items:
            found = [at for at, known in enumerate(arrays) if known is array]
            if not found:
                arrays.append(array)
            terms.append((found[0] if found else len(arrays) - 1, tuple(picks)))
            scratch.append(pltpu.VMEM(kept, array.dtype))
        plan.append(terms)
    n_in = len(arrays) + len(deps)
    return call(
        functools.partial(fetch_sum_kernel, plan, n_in),
        shapes,
        scratch + [pltpu.SemaphoreType.DMA((len(scratch),))],
        [whole(pltpu.HBM)] * len(arrays) + [whole(pl.ANY)] * len(deps),
        "first_sums",
        24,
    )(*arrays, *deps)


def take_sums(groups, deps, dtype=bf16):
    arrays, plan, shapes = [], [], []
    for items in groups:
        terms = []
        for array, picks in items:
            found = [at for at, known in enumerate(arrays) if known is array]
            if not found:
                arrays.append(array)
            terms.append((found[0] if found else len(arrays) - 1, tuple(picks)))
        plan.append(terms)
        kept = [pick.stop - pick.start for pick in items[0][1] if isinstance(pick, slice)]
        shapes.append(jax.ShapeDtypeStruct(tuple(kept), dtype))
    return call(
        functools.partial(sum_kernel, plan, len(arrays)),
        shapes,
        [],
        [whole()] * len(arrays) + [whole(pl.ANY)] * len(deps),
        "sums",
        24,
    )(*arrays, *deps)


def local(
    dense_feat,
    pooled,
    labels,
    cross_down,
    cross_up,
    cross_bias,
    w_hidden1,
    bias1,
    w_hidden2,
    bias2,
    w_logit,
    lookup_slots,
):
    n_table = lax.axis_size("table")
    n_row = lax.axis_size("row")
    n_z = n_table // 2
    row_bits = n_row.bit_length() - 1
    z_bits = n_z.bit_length() - 1
    batch, width = dense_feat.shape
    feat, rank = cross_down.shape
    hid = w_hidden1.shape[1]
    tab_grp, _, hot = lookup_slots.shape
    u_shard = batch * n_table * hot // 16

    def swap_cores(value):
        return lax.ppermute(value, "table", [(at, at ^ 1) for at in range(n_table)])

    def swap_z(value, which):
        return lax.ppermute(value, "table", [(at, at ^ (2 * which)) for at in range(n_table)])

    def swap_row(value, bit):
        return lax.ppermute(value, "row", [(at, at ^ (1 << bit)) for at in range(n_row)])

    late = hid // 8
    early = hid // 2 - late
    rows_front = (hid // 2 // LANES) * round_up(hid // n_row, 16)
    rows_front += (early // LANES) * round_up(feat // n_row, 16)
    rows_back = (late // LANES) * round_up(feat // n_row, 16)
    rows_back += (rank // 2 // LANES) * round_up(feat // n_row, 16)
    rows_back += 9 * round_up(rank // n_row, 16) + 48
    rows_front, rows_back = (round_up(rows, 16 * n_z) for rows in (rows_front, rows_back))

    def packed(rows):
        return jax.ShapeDtypeStruct((2, n_row, n_z // 2, rows // n_z, LANES), bf16)

    def wide(*shape):
        return jax.ShapeDtypeStruct(shape, bf16)

    hbm, vmem, anywhere = whole(pltpu.HBM), whole(), whole(pl.ANY)

    sources = (
        dense_feat,
        pooled,
        cross_down,
        cross_up,
        cross_bias,
        w_hidden1,
        bias1,
        w_hidden2,
        bias2,
        w_logit,
        labels,
    )
    send1, keep1, crossed_t, delta_first, small = call(
        front_kernel,
        [packed(rows_front)] * 2
        + [wide(feat, batch), wide(batch, hid), jax.ShapeDtypeStruct((24, LANES), f32)],
        held_like(sources)
        + [
            pltpu.VMEM((2, batch, hid // 2), bf16),
            pltpu.VMEM((2, batch, early), bf16),
            pltpu.SemaphoreType.DMA((len(sources),)),
        ],
        [hbm] * len(sources),
        "front",
        60,
    )(*sources)
    got1 = swap_cores(send1)

    sources = (
        dense_feat,
        pooled,
        cross_down,
        cross_up,
        cross_bias,
        delta_first,
        w_hidden1,
        crossed_t,
        small,
    )
    send2, keep2, *pooled_out = call(
        functools.partial(middle_kernel, n_z),
        [packed(rows_back)] * 2 + [wide(2, tab_grp, batch, width)] * n_z,
        held_like(sources)
        + [
            pltpu.VMEM((n_z, 2, tab_grp, batch, width), bf16),
            pltpu.VMEM((batch, feat), bf16),
            pltpu.VMEM((2, batch, rank // 2), bf16),
            pltpu.VMEM((2, batch, late), bf16),
            pltpu.VMEM((48, LANES), f32),
            pltpu.SemaphoreType.DMA((len(sources),)),
        ],
        [hbm] * len(sources),
        "middle",
        60,
    )(*sources)
    got2 = swap_cores(send2)

    low_first = tuple(range(row_bits))
    high_first = low_first[::-1]

    class Terms:
        def __init__(self, arrays, picks):
            self.items = []
            for array in arrays:
                self.add(array, picks)

        def add(self, array, picks=()):
            whole_axes = [slice(0, size) for size in array.shape[len(picks) :]]
            self.items.append((array, list(picks) + whole_axes))

        def narrowed(self, axis, what):
            items = []
            for array, picks in self.items:
                at = [number for number, pick in enumerate(picks) if isinstance(pick, slice)][axis]
                items.append((array, picks[:at] + [what] + picks[at + 1 :]))
            return items

        def far_near(self, axis, near, far):
            sent = self.narrowed(axis, far)
            self.items = self.narrowed(axis, near)
            return sent

    class Halving(Terms):
        def __init__(self, arrays, order, picks=()):
            dims = len(picks)
            arrays = [
                array.reshape(array.shape[:dims] + (2,) * row_bits + array.shape[dims + 1 :])
                for array in arrays
            ]
            super().__init__(arrays, picks)
            self.order, self.left = order, list(range(row_bits - 1, -1, -1))

        def part(self, at):
            axis = self.left.index(self.order[at])
            self.left.remove(self.order[at])
            return self.far_near(axis, 0, 1)

    def row_step(streams, at, deps):
        sent = take_sums([stream.part(at) for stream in streams], deps)
        for stream, value in zip(streams, sent):
            stream.add(swap_row(value, stream.order[at]))
        return list(sent)

    class Dense:
        def __init__(self, keep, got):
            self.low = Halving([keep, got], low_first, [0])
            self.high = Halving([keep, got], high_first, [1])

        def first_step(self, deps):
            halves = (self.low, self.high)
            sent = fetch_sums([half.part(0) for half in halves], deps)
            self.near = [half.items for half in halves]
            for half, value in zip(halves, sent):
                half.items = []
                half.add(swap_row(value, half.order[0]))
            return list(sent)

        def settle(self, deps):
            for half, value in zip((self.low, self.high), fetch_sums(self.near, deps)):
                half.add(value)
                half.items.reverse()

        def row_step(self, at, deps):
            deps = [*deps, self.low.items[-1][0], self.high.items[-1][0]]
            return row_step((self.low, self.high), at, deps)

        def z_step(self, stage, deps):
            middle = n_z >> (stage + 1)
            items, deps = self.high.items, [*deps, self.low.items[-1][0]]
            if stage > 0:
                items = self.low.far_near(0, slice(0, middle), slice(middle, 2 * middle))
            (sent,) = take_sums([items], deps)
            self.low.add(swap_z(sent, 1 << stage))
            return [sent]

        def z_own(self, deps):
            (self.own,) = take_sums([self.low.items], deps)
            self.back = swap_z(self.own, 1 << (z_bits - 1)) if z_bits > 1 else None
            return [self.own]

        def z_back(self, deps):
            for stage in range(z_bits - 1, 0, -1):
                if stage < z_bits - 1:
                    self.back = swap_z(self.own, 1 << stage)
                (back,) = after([self.back], deps)
                self.own = jnp.concatenate([self.own, back], axis=0)
            far = swap_z(self.own, 1)
            self.pieces = [self.own, far, swap_cores(self.own), swap_cores(far)]
            return [self.own]

    (got1,) = after([got1], [pooled_out[0]])
    one, two = Dense(keep1, got1), Dense(keep2, got2)
    one.first_step([])
    values, half = {0: pooled_out[0]}, n_z // 2
    for which in [half, *range(1, half)]:
        values[which] = swap_z(pooled_out[which], which)
    for which in range(half + 1, n_z):
        (moved,) = after([pooled_out[which]], [values[half], values[which - half]])
        values[which] = swap_z(moved, which)
    one.settle([values[1]])
    last = [values[which] for which in range(1, half + 1)]
    for at in range(1, row_bits):
        last = one.row_step(at, last)
    last = two.first_step(last)
    last = one.z_step(0, last)
    two.settle(last)
    values = [values[which] for which in range(n_z)]
    far_values = call(
        functools.partial(select_kernel, n_z),
        [wide(n_z // 2, tab_grp, batch, width)] * 2,
        [],
        [vmem] * n_z + [anywhere],
        "select",
        8,
    )(*values, last[0])
    values += [swap_cores(value) for value in far_values]
    slots = jnp.transpose(lookup_slots, (0, 2, 1))
    last, shares = [far_values[0]], []
    for table in range(tab_grp):
        sums = pl.pallas_call(
            functools.partial(count_kernel, n_row, table, hot, n_z),
            out_shape=wide(n_row, u_shard, width),
            grid=(n_row,),
            in_specs=[vmem] * (3 + n_z) + [anywhere],
            out_specs=pl.BlockSpec((1, u_shard, width), lambda at: (at, 0, 0)),
            compiler_params=pltpu.CompilerParams(vmem_limit_bytes=16 * MIB),
            cost_estimate=no_cost(),
            name="counts",
        )(slots, *values, last[0])
        shares.append(Halving([sums], high_first if table % 2 else low_first))
        last = [sums]
        if table == 0:
            for at in range(1, row_bits):
                last = two.row_step(at, last)
            for stage in range(1, z_bits):
                last = one.z_step(stage, last)
            last = two.z_step(0, last)
    last = row_step(shares, 0, last)
    last = one.z_own(last)
    for stage in range(1, z_bits):
        last = two.z_step(stage, last)
    for at in range(1, row_bits):
        last = row_step(shares, at, last)
    last = two.z_own(last)
    last = one.z_back(last)
    row_grads = sum_rows([share.items for share in shares], last)
    two.z_back([row_grads])

    shapes = [(feat // n_row, rank), (rank // n_row, feat), (feat // n_row, hid), (hid // n_row, hid)]
    shapes += [(feat // n_row,)] + [(hid // n_row,)] * 3
    g_down, g_up, g_first, g_second, g_cbias, g_bias1, g_bias2, g_logit = pl.pallas_call(
        unpack_kernel,
        out_shape=[jax.ShapeDtypeStruct(shape, f32) for shape in shapes],
        in_specs=[vmem] * 8,
        out_specs=[hbm] * 4 + [vmem] * 4,
        scratch_shapes=[pltpu.VMEM((2, rows, LANES), bf16) for rows in (rows_front, rows_back)]
        + [pltpu.VMEM((56, LANES), f32)]
        + [pltpu.VMEM(shape, f32) for shape in shapes[:4]]
        + [pltpu.SemaphoreType.DMA((9,))],
        compiler_params=pltpu.CompilerParams(vmem_limit_bytes=24 * MIB),
        cost_estimate=no_cost(),
        name="unpack",
    )(*one.pieces, *two.pieces)
    return (row_grads, g_down, g_up, g_cbias, g_first, g_bias1, g_second, g_bias2, g_logit)


def solution(mesh):
    in_specs = (
        P(("table", "row"), None),
        P(("table", "row"), None),
        P(("table", "row")),
        P(),
        P(),
        P(),
        P(),
        P(),
        P(),
        P(),
        P(),
        P("table", None, None),
    )
    out_specs = (
        P("table", "row", None),
        P("row", None),
        P("row", None),
        P("row"),
        P("row", None),
        P("row"),
        P("row", None),
        P("row"),
        P("row"),
    )
    return jax.shard_map(local, mesh=mesh, in_specs=in_specs, out_specs=out_specs, check_vma=False)
```

```python
import functools
import itertools

import jax
import jax.numpy as jnp
from jax import lax
from jax.experimental import pallas as pl
from jax.experimental.pallas import tpu as pltpu
from jax.sharding import PartitionSpec as P

loss_scale = 16.0
LANES = 128
SPAN = 9 * LANES
MIB = 1024 * 1024
bf16 = jnp.bfloat16
f32 = jnp.float32


def round_up(value, unit):
    return -(-value // unit) * unit


def matmul(left, right):
    return jnp.dot(left, right, preferred_element_type=f32)


def matmul_rt(left, right):
    return lax.dot_general(left, right, (((1,), (1,)), ((), ())), preferred_element_type=f32)


def reverse_bits(value, bits):
    out = 0
    for bit in range(bits):
        out = out | (((value >> bit) & 1) << (bits - 1 - bit))
    return out


def places_of(z_pos, n_z):
    bits = n_z.bit_length() - 1
    return [reverse_bits(z_pos ^ quarter, bits) for quarter in range(n_z)]


def put_blocks(ref, row_pos, places, offset, value):
    shards, n_half, rows_q = ref.shape[1], ref.shape[2], ref.shape[3]
    rows = value.shape[0] // shards
    step = round_up(rows, 16)
    blocks = value.shape[1] // LANES
    for shard in range(shards):
        slot = shard ^ row_pos
        for block in range(blocks):
            done = 0
            while done < rows:
                quarter, at = divmod(offset + block * step + done, rows_q)
                length = min(rows - done, rows_q - at)
                place = places[quarter]
                ref[lax.div(place, n_half), slot, lax.rem(place, n_half), at : at + length, :] = value[
                    shard * rows + done : shard * rows + done + length,
                    block * LANES : (block + 1) * LANES,
                ].astype(ref.dtype)
                done += length
    return offset + blocks * step


def put_rows(ref, offset, value):
    for block in range(value.shape[1] // LANES):
        ref[offset + block : offset + block + 1, :] = value[:, block * LANES : (block + 1) * LANES]


def position():
    table_pos = lax.axis_index("table")
    return lax.rem(table_pos, 2), lax.axis_index("row"), table_pos


class Loads:
    def __init__(self, sources, targets, sems):
        self.copies = [
            pltpu.make_async_copy(source, target, sems.at[at])
            for at, (source, target) in enumerate(zip(sources, targets))
        ]
        self.targets = targets
        self.ready = set()
        for copy in self.copies:
            copy.start()

    def __call__(self, at):
        if at not in self.ready:
            self.copies[at].wait()
            self.ready.add(at)
        return self.targets[at][...]


def as_row(value):
    return value.reshape(1, value.shape[-1])


def front_kernel(*refs):
    sources, outs, targets = refs[:11], refs[11:16], refs[16:27]
    halves, thirds, sems = refs[27:]
    send, keep, crossed_t_out, first_out, small = outs
    load = Loads(sources, targets, sems)
    core, row_pos, table_pos = position()
    places = places_of(lax.div(table_pos, 2), 2 * send.shape[2])
    stacked = jnp.concatenate([load(0), load(1)], axis=1)
    cross_down = load(2)
    reduced = matmul(stacked, cross_down).astype(bf16)
    widened = matmul(reduced, load(3)) + as_row(load(4))
    wide = stacked.astype(f32)
    crossed = (wide * widened + wide).astype(bf16)
    pre_first = matmul(crossed, load(5)) + as_row(load(6))
    sig_first = jax.nn.sigmoid(pre_first)
    act_first = (pre_first * sig_first).astype(bf16)
    slope_first = sig_first * (1.0 + pre_first * (1.0 - sig_first))
    w_hidden2 = load(7)
    pre_second = matmul(act_first, w_hidden2) + as_row(load(8))
    sig_second = jax.nn.sigmoid(pre_second)
    act_second = (pre_second * sig_second).astype(bf16).astype(f32)
    slope_second = sig_second * (1.0 + pre_second * (1.0 - sig_second))
    w_logit = as_row(load(9))
    logits = jnp.sum(act_second * w_logit, axis=1, keepdims=True)
    labels = as_row(load(10))
    count = labels.shape[1]
    same = lax.broadcasted_iota(jnp.int32, (count, count), 0) == lax.broadcasted_iota(
        jnp.int32, (count, count), 1
    )
    label_col = jnp.sum(jnp.where(same, labels.astype(f32), 0.0), axis=1, keepdims=True)
    delta_logit = loss_scale * (jax.nn.sigmoid(logits) - label_col)
    delta_second = (delta_logit * w_logit * slope_second).astype(bf16)
    put_rows(small, 16, jnp.sum(act_second * delta_logit, axis=0, keepdims=True))
    put_rows(small, 8, jnp.sum(delta_second.astype(f32), axis=0, keepdims=True))
    half = halves.shape[2]
    halves[0] = delta_second[:, :half]
    halves[1] = delta_second[:, half:]
    delta_first = (matmul_rt(delta_second, w_hidden2) * slope_first).astype(bf16)
    first_out[...] = delta_first
    put_rows(small, 0, jnp.sum(delta_first.astype(f32), axis=0, keepdims=True))
    part = thirds.shape[2]
    thirds[0] = delta_first[:, :part]
    thirds[1] = delta_first[:, half : half + part]
    act_t = act_first.T
    crossed_t = crossed.T
    crossed_t_out[...] = crossed_t
    for ref, who in ((send, 1 - core), (keep, core)):
        offset = put_blocks(ref, row_pos, places, 0, matmul(act_t, halves[who]))
        put_blocks(ref, row_pos, places, offset, matmul(crossed_t, thirds[who]))


def middle_kernel(n_z, *refs):
    sources, send, keep = refs[:9], refs[9], refs[10]
    pooled_outs = refs[11 : 11 + n_z]
    rest = refs[11 + n_z :]
    targets = rest[:9]
    by_group, wide_delta, half_delta, sixths, small, sems = rest[9:]
    load = Loads(sources, targets, sems)
    core, row_pos, table_pos = position()
    z_pos = lax.div(table_pos, 2)
    places = places_of(z_pos, 2 * send.shape[2])
    stacked = jnp.concatenate([load(0), load(1)], axis=1)
    cross_down = load(2)
    reduced = matmul(stacked, cross_down).astype(bf16)
    cross_up = load(3)
    widened = matmul(reduced, cross_up) + as_row(load(4))
    delta_first = load(5)
    delta_crossed = matmul_rt(delta_first, load(6))
    delta_widened = (delta_crossed * stacked.astype(f32)).astype(bf16)
    wide_delta[...] = delta_widened
    delta_reduced = matmul_rt(delta_widened, cross_up).astype(bf16)
    delta_stacked = delta_crossed * (widened + 1.0) + matmul_rt(delta_reduced, cross_down)
    width = targets[0].shape[1]
    per_group = by_group.shape[2]
    for table in range(2 * n_z * per_group):
        group = table // per_group
        by_group[group // 2, group % 2, table % per_group] = delta_stacked[
            :, width * (table + 1) : width * (table + 2)
        ].astype(bf16)
    for which in range(n_z):
        pooled_outs[which][0] = by_group[z_pos ^ which, core]
        pooled_outs[which][1] = by_group[z_pos ^ which, 1 - core]

    n_row, rank, feat = send.shape[1], delta_reduced.shape[1], delta_widened.shape[1]
    hid = delta_first.shape[1]
    part = hid // 2 - sixths.shape[2]
    half_delta[0] = delta_reduced[:, : rank // 2]
    half_delta[1] = delta_reduced[:, rank // 2 :]
    sixths[0] = delta_first[:, part : hid // 2]
    sixths[1] = delta_first[:, hid // 2 + part :]
    put_rows(small, 24, jnp.sum(delta_widened.astype(f32), axis=0, keepdims=True))
    small[0:24, :] = load(8)
    small[41:48, :] = jnp.zeros((7, LANES), f32)
    sums = jnp.concatenate([small[...]] * n_row, axis=0)
    crossed_t, reduced_t, stacked_t = load(7), reduced.T, stacked.T
    for ref, who in ((send, 1 - core), (keep, core)):
        offset = put_blocks(ref, row_pos, places, 0, matmul(crossed_t, sixths[who]))
        offset = put_blocks(ref, row_pos, places, offset, matmul(stacked_t, half_delta[who]))
        start = pl.multiple_of(who * (feat - SPAN), LANES)
        offset = put_blocks(
            ref, row_pos, places, offset, matmul(reduced_t, wide_delta[:, pl.ds(start, SPAN)])
        )
        offset = put_blocks(ref, row_pos, places, offset, sums)
        tail = 2 * ref.shape[2] * ref.shape[3] - offset
        if tail:
            put_blocks(ref, row_pos, places, offset, jnp.zeros((n_row * tail, LANES), f32))


def select_kernel(n_z, *refs):
    for which in range(n_z):
        out = refs[len(refs) - 2 + which // (n_z // 2)]
        out[which % (n_z // 2)] = refs[which][1]


def count_kernel(n_row, table, hot, n_z, slots, *rest):
    direct, crossed, out = rest[:n_z], rest[n_z : n_z + 2], rest[-1]
    near = n_z // 2
    block = out.shape[1]
    samples = crossed[0].shape[2]
    core, row_pos, table_pos = position()
    z_pos = lax.div(table_pos, 2)
    base = (pl.program_id(0) ^ row_pos) * block
    names = lax.broadcasted_iota(jnp.int16, (block, samples), 0)
    total = jnp.zeros((block, out.shape[2]), f32)
    one = jnp.ones((block, samples), bf16)
    zero = jnp.zeros((block, samples), bf16)
    for which in range(n_z):
        far = crossed[which // near]
        for held, who in ((direct[which][0, table], core), (far[which % near, table], 1 - core)):
            source = 2 * (z_pos ^ which) + who
            start = pl.multiple_of((source * n_row + row_pos) * samples, LANES)
            lines = slots[table, :, pl.ds(start, samples)] - base
            lines = jnp.where((lines >= 0) & (lines < block), lines, block).astype(jnp.int16)
            counts = zero
            for look in range(hot):
                line = jnp.broadcast_to(lines[look : look + 1, :], (block, samples))
                counts = counts + jnp.where(line == names, one, zero)
            total = total + matmul(counts, held)
    out[0] = total.astype(out.dtype)


def unpack_kernel(*refs):
    parts = refs[0:8]
    g_down, g_up, g_first, g_second = refs[8:12]
    small_outs = refs[12:16]
    held, small = refs[16:18], refs[18]
    core, row_pos, table_pos = position()
    z_pos = lax.div(table_pos, 2)
    for stream in range(2):
        lower, upper, lower_other, upper_other = parts[4 * stream : 4 * stream + 4]
        ref = held[stream]
        rows = lower.shape[1]
        n_z = 2 * lower.shape[0]
        z_bits = n_z.bit_length() - 1
        for who, pieces in ((core, (lower, upper)), (1 - core, (lower_other, upper_other))):
            for place in range(n_z):
                start = pl.multiple_of((reverse_bits(place, z_bits) ^ z_pos) * rows, 16)
                ref[who, pl.ds(start, rows), :] = pieces[place // (n_z // 2)][place % (n_z // 2)]
    front, back = held

    def take(ref, out, half, offset, columns):
        rows = out.shape[0]
        step = round_up(rows, 16)
        for column in columns:
            out[:, column * LANES : (column + 1) * LANES] = ref[
                half, offset : offset + rows, :
            ].astype(f32)
            offset += step
        return offset

    for half in range(2):
        blocks = g_second.shape[1] // LANES // 2
        offset = take(front, g_second, half, 0, range(half * blocks, (half + 1) * blocks))
        blocks = g_first.shape[1] // LANES // 2
        early = blocks - blocks // 4
        take(front, g_first, half, offset, range(half * blocks, half * blocks + early))
        offset = take(back, g_first, half, 0, range(half * blocks + early, (half + 1) * blocks))
        blocks = g_down.shape[1] // LANES // 2
        offset = take(back, g_down, half, offset, range(half * blocks, (half + 1) * blocks))
        blocks = g_up.shape[1] // LANES
        offset = take(back, g_up, half, offset, range(half * (blocks - 9), half * (blocks - 9) + 9))
    small[0:48, :] = back[0, offset : offset + 48, :].astype(f32)
    small[48:, :] = jnp.zeros((small.shape[0] - 48, LANES), f32)
    for out, first in zip(small_outs, (24, 0, 8, 16)):
        share = out.shape[0]
        begin = row_pos * share
        row, lane = lax.div(begin, LANES), lax.rem(begin, LANES)
        lanes = lax.broadcasted_iota(jnp.int32, (1, LANES), 1)
        for start in range(0, share, LANES):
            length = min(LANES, share - start)
            this = small[pl.ds(first + row + start // LANES, 1), :]
            later = small[pl.ds(first + row + start // LANES + 1, 1), :]
            both = jnp.where(lanes < lane, later, this)
            turned = pltpu.roll(both, lax.rem(LANES - lane, LANES), 1)
            out[start : start + length] = turned.reshape(LANES)[:length]


def whole(memory=pltpu.VMEM):
    return pl.BlockSpec(memory_space=memory)


def no_cost():
    return pl.CostEstimate(flops=0, transcendentals=0, bytes_accessed=0)


def call(body, outs, scratch, in_specs, name, mib):
    return pl.pallas_call(
        body,
        out_shape=outs,
        in_specs=in_specs,
        out_specs=[whole()] * len(outs),
        scratch_shapes=scratch,
        compiler_params=pltpu.CompilerParams(vmem_limit_bytes=mib * MIB),
        cost_estimate=no_cost(),
        name=name,
    )


def after(values, deps):
    return list(lax.optimization_barrier(tuple(values) + tuple(deps))[: len(values)])


def held_like(values):
    return [pltpu.VMEM(value.shape, value.dtype) for value in values]


def sum_rows_kernel(plan, *refs):
    out = refs[-1]
    for table, terms in enumerate(plan):
        total = None
        for which, picks in terms:
            part = refs[which][picks].astype(f32)
            total = part if total is None else total + part
        out[table] = total


def sum_rows(groups, deps):
    arrays = [array for items in groups for array, _ in items]
    plan, count = [], 0
    for items in groups:
        plan.append([(count + at, tuple(picks)) for at, (_, picks) in enumerate(items)])
        count += len(items)
    kept = [pick.stop - pick.start for pick in groups[0][0][1] if isinstance(pick, slice)]
    return call(
        functools.partial(sum_rows_kernel, plan),
        [jax.ShapeDtypeStruct((len(groups), *kept), f32)],
        [],
        [whole()] * len(arrays) + [whole(pl.ANY)] * len(deps),
        "rows",
        24,
    )(*arrays, *deps)[0]


def sum_kernel(plan, n_in, *refs):
    outs = refs[len(refs) - len(plan) :]
    for out, terms in zip(outs, plan):
        rows = out.shape[-2]
        chunk = next(size for size in (64, 48, 80, 32, 16, 8, rows) if rows % size == 0)

        def one_chunk(at, carry, out=out, terms=terms, chunk=chunk):
            window = pl.ds(pl.multiple_of(at * chunk, chunk), chunk)
            for lead in itertools.product(*[range(size) for size in out.shape[:-2]]):
                total = None
                for which, picks in terms:
                    axes, place = iter(lead), []
                    for pick in picks[:-2]:
                        place.append(pick.start + next(axes) if isinstance(pick, slice) else pick)
                    part = refs[which][(*place, window, slice(None))].astype(f32)
                    total = part if total is None else total + part
                out[(*lead, window, slice(None))] = total.astype(out.dtype)
            return carry

        lax.fori_loop(0, rows // chunk, one_chunk, 0)


def fetch_sum_kernel(plan, n_in, *refs):
    outs = refs[n_in : n_in + len(plan)]
    held, sems = refs[n_in + len(plan) : -1], refs[-1]
    copies, by_out = [], []
    for terms in plan:
        parts = []
        for which, picks in terms:
            at = len(copies)
            place = tuple(
                pl.ds(pick.start, pick.stop - pick.start) if isinstance(pick, slice) else pick
                for pick in picks
            )
            copies.append(pltpu.make_async_copy(refs[which].at[place], held[at], sems.at[at]))
            parts.append((at, tuple(slice(0, size) for size in held[at].shape)))
        by_out.append(parts)
    for copy in copies:
        copy.start()
    for out, parts in zip(outs, by_out):
        for at, _ in parts:
            copies[at].wait()
        sum_kernel([parts], 0, *held, out)


def fetch_sums(groups, deps):
    arrays, plan, shapes, scratch = [], [], [], []
    for items in groups:
        kept = tuple(pick.stop - pick.start for pick in items[0][1] if isinstance(pick, slice))
        shapes.append(jax.ShapeDtypeStruct(kept, bf16))
        terms = []
        for array, picks in items:
            found = [at for at, known in enumerate(arrays) if known is array]
            if not found:
                arrays.append(array)
            terms.append((found[0] if found else len(arrays) - 1, tuple(picks)))
            scratch.append(pltpu.VMEM(kept, array.dtype))
        plan.append(terms)
    n_in = len(arrays) + len(deps)
    return call(
        functools.partial(fetch_sum_kernel, plan, n_in),
        shapes,
        scratch + [pltpu.SemaphoreType.DMA((len(scratch),))],
        [whole(pltpu.HBM)] * len(arrays) + [whole(pl.ANY)] * len(deps),
        "first_sums",
        24,
    )(*arrays, *deps)


def take_sums(groups, deps, dtype=bf16):
    arrays, plan, shapes = [], [], []
    for items in groups:
        terms = []
        for array, picks in items:
            found = [at for at, known in enumerate(arrays) if known is array]
            if not found:
                arrays.append(array)
            terms.append((found[0] if found else len(arrays) - 1, tuple(picks)))
        plan.append(terms)
        kept = [pick.stop - pick.start for pick in items[0][1] if isinstance(pick, slice)]
        shapes.append(jax.ShapeDtypeStruct(tuple(kept), dtype))
    return call(
        functools.partial(sum_kernel, plan, len(arrays)),
        shapes,
        [],
        [whole()] * len(arrays) + [whole(pl.ANY)] * len(deps),
        "sums",
        24,
    )(*arrays, *deps)


def local(
    dense_feat,
    pooled,
    labels,
    cross_down,
    cross_up,
    cross_bias,
    w_hidden1,
    bias1,
    w_hidden2,
    bias2,
    w_logit,
    lookup_slots,
):
    n_table = lax.axis_size("table")
    n_row = lax.axis_size("row")
    n_z = n_table // 2
    row_bits = n_row.bit_length() - 1
    z_bits = n_z.bit_length() - 1
    batch, width = dense_feat.shape
    feat, rank = cross_down.shape
    hid = w_hidden1.shape[1]
    tab_grp, _, hot = lookup_slots.shape
    u_shard = batch * n_table * hot // 16

    def swap_cores(value):
        return lax.ppermute(value, "table", [(at, at ^ 1) for at in range(n_table)])

    def swap_z(value, which):
        return lax.ppermute(value, "table", [(at, at ^ (2 * which)) for at in range(n_table)])

    def swap_row(value, bit):
        return lax.ppermute(value, "row", [(at, at ^ (1 << bit)) for at in range(n_row)])

    late = hid // 8
    early = hid // 2 - late
    rows_front = (hid // 2 // LANES) * round_up(hid // n_row, 16)
    rows_front += (early // LANES) * round_up(feat // n_row, 16)
    rows_back = (late // LANES) * round_up(feat // n_row, 16)
    rows_back += (rank // 2 // LANES) * round_up(feat // n_row, 16)
    rows_back += 9 * round_up(rank // n_row, 16) + 48
    rows_front, rows_back = (round_up(rows, 16 * n_z) for rows in (rows_front, rows_back))

    def packed(rows):
        return jax.ShapeDtypeStruct((2, n_row, n_z // 2, rows // n_z, LANES), bf16)

    def wide(*shape):
        return jax.ShapeDtypeStruct(shape, bf16)

    hbm, vmem, anywhere = whole(pltpu.HBM), whole(), whole(pl.ANY)

    sources = (
        dense_feat,
        pooled,
        cross_down,
        cross_up,
        cross_bias,
        w_hidden1,
        bias1,
        w_hidden2,
        bias2,
        w_logit,
        labels,
    )
    send1, keep1, crossed_t, delta_first, small = call(
        front_kernel,
        [packed(rows_front)] * 2
        + [wide(feat, batch), wide(batch, hid), jax.ShapeDtypeStruct((24, LANES), f32)],
        held_like(sources)
        + [
            pltpu.VMEM((2, batch, hid // 2), bf16),
            pltpu.VMEM((2, batch, early), bf16),
            pltpu.SemaphoreType.DMA((len(sources),)),
        ],
        [hbm] * len(sources),
        "front",
        60,
    )(*sources)
    got1 = swap_cores(send1)

    sources = (
        dense_feat,
        pooled,
        cross_down,
        cross_up,
        cross_bias,
        delta_first,
        w_hidden1,
        crossed_t,
        small,
    )
    send2, keep2, *pooled_out = call(
        functools.partial(middle_kernel, n_z),
        [packed(rows_back)] * 2 + [wide(2, tab_grp, batch, width)] * n_z,
        held_like(sources)
        + [
            pltpu.VMEM((n_z, 2, tab_grp, batch, width), bf16),
            pltpu.VMEM((batch, feat), bf16),
            pltpu.VMEM((2, batch, rank // 2), bf16),
            pltpu.VMEM((2, batch, late), bf16),
            pltpu.VMEM((48, LANES), f32),
            pltpu.SemaphoreType.DMA((len(sources),)),
        ],
        [hbm] * len(sources),
        "middle",
        60,
    )(*sources)
    got2 = swap_cores(send2)

    low_first = tuple(range(row_bits))
    high_first = low_first[::-1]

    class Terms:
        def __init__(self, arrays, picks):
            self.items = []
            for array in arrays:
                self.add(array, picks)

        def add(self, array, picks=()):
            whole_axes = [slice(0, size) for size in array.shape[len(picks) :]]
            self.items.append((array, list(picks) + whole_axes))

        def narrowed(self, axis, what):
            items = []
            for array, picks in self.items:
                at = [number for number, pick in enumerate(picks) if isinstance(pick, slice)][axis]
                items.append((array, picks[:at] + [what] + picks[at + 1 :]))
            return items

        def far_near(self, axis, near, far):
            sent = self.narrowed(axis, far)
            self.items = self.narrowed(axis, near)
            return sent

    class Halving(Terms):
        def __init__(self, arrays, order, picks=()):
            dims = len(picks)
            arrays = [
                array.reshape(array.shape[:dims] + (2,) * row_bits + array.shape[dims + 1 :])
                for array in arrays
            ]
            super().__init__(arrays, picks)
            self.order, self.left = order, list(range(row_bits - 1, -1, -1))

        def part(self, at):
            axis = self.left.index(self.order[at])
            self.left.remove(self.order[at])
            return self.far_near(axis, 0, 1)

    def row_step(streams, at, deps):
        sent = take_sums([stream.part(at) for stream in streams], deps)
        for stream, value in zip(streams, sent):
            stream.add(swap_row(value, stream.order[at]))
        return list(sent)

    class Dense:
        def __init__(self, keep, got):
            self.low = Halving([keep, got], low_first, [0])
            self.high = Halving([keep, got], high_first, [1])

        def first_step(self, deps):
            halves = (self.low, self.high)
            sent = fetch_sums([half.part(0) for half in halves], deps)
            self.near = [half.items for half in halves]
            for half, value in zip(halves, sent):
                half.items = []
                half.add(swap_row(value, half.order[0]))
            return list(sent)

        def settle(self, deps):
            for half, value in zip((self.low, self.high), fetch_sums(self.near, deps)):
                half.add(value)
                half.items.reverse()

        def row_step(self, at, deps):
            deps = [*deps, self.low.items[-1][0], self.high.items[-1][0]]
            return row_step((self.low, self.high), at, deps)

        def z_step(self, stage, deps):
            middle = n_z >> (stage + 1)
            items, deps = self.high.items, [*deps, self.low.items[-1][0]]
            if stage > 0:
                items = self.low.far_near(0, slice(0, middle), slice(middle, 2 * middle))
            (sent,) = take_sums([items], deps)
            self.low.add(swap_z(sent, 1 << stage))
            return [sent]

        def z_own(self, deps):
            (self.own,) = take_sums([self.low.items], deps)
            self.back = swap_z(self.own, 1 << (z_bits - 1)) if z_bits > 1 else None
            return [self.own]

        def z_back(self, deps):
            for stage in range(z_bits - 1, 0, -1):
                if stage < z_bits - 1:
                    self.back = swap_z(self.own, 1 << stage)
                (back,) = after([self.back], deps)
                self.own = jnp.concatenate([self.own, back], axis=0)
            far = swap_z(self.own, 1)
            self.pieces = [self.own, far, swap_cores(self.own), swap_cores(far)]
            return [self.own]

    (got1,) = after([got1], [pooled_out[0]])
    one, two = Dense(keep1, got1), Dense(keep2, got2)
    one.first_step([])
    values, half = {0: pooled_out[0]}, n_z // 2
    for which in [half, *range(1, half)]:
        values[which] = swap_z(pooled_out[which], which)
    for which in range(half + 1, n_z):
        values[which] = swap_z(pooled_out[which], which)
    one.settle([values[1]])
    last = [values[1]]
    for at in range(1, row_bits):
        last = one.row_step(at, last)
    last = two.first_step([*last, *[values[which] for which in range(1, n_z)]])
    last = one.z_step(0, last)
    two.settle(last)
    values = [values[which] for which in range(n_z)]
    far_values = call(
        functools.partial(select_kernel, n_z),
        [wide(n_z // 2, tab_grp, batch, width)] * 2,
        [],
        [vmem] * n_z + [anywhere],
        "select",
        8,
    )(*values, last[0])
    values += [swap_cores(value) for value in far_values]
    slots = jnp.transpose(lookup_slots, (0, 2, 1))
    last, shares = [far_values[0]], []
    for table in range(tab_grp):
        sums = pl.pallas_call(
            functools.partial(count_kernel, n_row, table, hot, n_z),
            out_shape=wide(n_row, u_shard, width),
            grid=(n_row,),
            in_specs=[vmem] * (3 + n_z) + [anywhere],
            out_specs=pl.BlockSpec((1, u_shard, width), lambda at: (at, 0, 0)),
            compiler_params=pltpu.CompilerParams(vmem_limit_bytes=16 * MIB),
            cost_estimate=no_cost(),
            name="counts",
        )(slots, *values, last[0])
        shares.append(Halving([sums], high_first if table % 2 else low_first))
        last = [sums]
        if table == 0:
            for at in range(1, row_bits):
                last = two.row_step(at, last)
            for stage in range(1, z_bits):
                last = one.z_step(stage, last)
            last = two.z_step(0, last)
    last = row_step(shares, 0, last)
    last = one.z_own(last)
    for stage in range(1, z_bits):
        last = two.z_step(stage, last)
    for at in range(1, row_bits):
        last = row_step(shares, at, last)
    last = two.z_own(last)
    last = one.z_back(last)
    row_grads = sum_rows([share.items for share in shares], last)
    two.z_back([row_grads])

    g_down, g_up, g_first, g_second, g_cbias, g_bias1, g_bias2, g_logit = call(
        unpack_kernel,
        [
            jax.ShapeDtypeStruct((feat // n_row, rank), f32),
            jax.ShapeDtypeStruct((rank // n_row, feat), f32),
            jax.ShapeDtypeStruct((feat // n_row, hid), f32),
            jax.ShapeDtypeStruct((hid // n_row, hid), f32),
            jax.ShapeDtypeStruct((feat // n_row,), f32),
        ]
        + [jax.ShapeDtypeStruct((hid // n_row,), f32)] * 3,
        [pltpu.VMEM((2, rows, LANES), bf16) for rows in (rows_front, rows_back)]
        + [pltpu.VMEM((56, LANES), f32)],
        [vmem] * 8,
        "unpack",
        24,
    )(*one.pieces, *two.pieces)
    return (row_grads, g_down, g_up, g_cbias, g_first, g_bias1, g_second, g_bias2, g_logit)


def solution(mesh):
    in_specs = (
        P(("table", "row"), None),
        P(("table", "row"), None),
        P(("table", "row")),
        P(),
        P(),
        P(),
        P(),
        P(),
        P(),
        P(),
        P(),
        P("table", None, None),
    )
    out_specs = (
        P("table", "row", None),
        P("row", None),
        P("row", None),
        P("row"),
        P("row", None),
        P("row"),
        P("row", None),
        P("row"),
        P("row"),
    )
    return jax.shard_map(local, mesh=mesh, in_specs=in_specs, out_specs=out_specs, check_vma=False)
```
